128 devices in a mesh: dp: 16 (over y_hi, z, core), tensor: 8 (over y_lo, x).
Axes of the slice: x: 4, y: 4 (y_hi: 2, y_lo: 2; y = y_hi * 2 + y_lo), z: 4, core: 2. Of those that a mesh axis runs over, the one named last changes fastest.
Arguments:
- tokens: bfloat16 [2048, 8192], P('dp'), may hold values from -6 to 6
- target: bfloat16 [2048, 8192], P('dp'), may hold values from -6 to 6
- norm_gain: float32 [8192], replicated, may hold values from 0.1 to 1.9
- w_query: bfloat16 [8192, 4096], P(None, 'tensor'), may hold values from -0.0625 to 0.0625
- w_key: bfloat16 [8192, 1024], P(None, 'tensor'), may hold values from -0.0625 to 0.0625
- w_value: bfloat16 [8192, 1024], P(None, 'tensor'), may hold values from -0.0625 to 0.0625
- w_out: bfloat16 [4096, 8192], P('tensor'), may hold values from -0.09375 to 0.09375
- t_query: float32 [4096], P('tensor'), may hold values from -4 to 4
- t_key: float32 [1024], P('tensor'), may hold values from -4 to 4
- t_value: float32 [1024], P('tensor'), may hold values from -4 to 4
- t_out: float32 [8192], replicated, may hold values from -4 to 4
Outputs:
- hvp_query: float32 [8192, 4096], P('dp', 'tensor')
- hvp_key: float32 [8192, 1024], P('dp', 'tensor')
- hvp_value: float32 [8192, 1024], P('dp', 'tensor')
- hvp_out: float32 [8192, 4096], P('dp', 'tensor')
The draws below stay inside these ranges and needn't reach their ends.
All inputs are finite; a program needn't handle non-finite values.
Results may differ from the reference program's by a relative error of at most 0.02.
Values may be sent and summed in bfloat16 or wider, within the bound.
A program may use at most 128 MiB of HBM per device.

```python
import math
import jax
import jax.numpy as jnp
from jax import lax

D = 8192
HD = 128
QH_DEV = 4
SEQ = 128
Q_HEADS = 32
KV_HEADS = 8
TOKENS = 2048
N_DP = 16
N_TENSOR = 8


def spiked(entries, stream_key, source, target, shards_of, factor):
    def block_of(dim):
        return (jnp.arange(entries.shape[dim]) // (entries.shape[dim] // shards_of)).reshape((-1,) + (1,) * (entries.ndim - 1 - dim))

    near = jax.random.permutation(stream_key, shards_of)[block_of(target)]
    far = (block_of(target) + shards_of // 2) % shards_of
    return jnp.where((block_of(source) == near) | (block_of(source) == far), factor * entries, entries)


def block_levels(own_key, dims, cuts, least, top_value):
    gain = 1.0
    for dim, blocks in cuts:
        draws = jax.random.uniform(jax.random.fold_in(jax.random.fold_in(own_key, 6), dim), (blocks,), jnp.float32, least / len(cuts), top_value / len(cuts))
        gain = gain * jnp.repeat(jnp.exp(draws), dims[dim] // blocks).reshape((-1,) + (1,) * (len(dims) - 1 - dim))
    return gain


def gaussian(stream_key, dims, scale, bound, cuts=(), dtype=jnp.bfloat16):
    gain = block_levels(stream_key, dims, cuts, -0.22, 0.18) if cuts else 1.0
    values = jax.random.normal(stream_key, dims, jnp.float32) * scale * gain
    return jnp.minimum(jnp.maximum(values, -bound), bound).astype(dtype)


def gaussian_with(stream_key, extent, width, bound, split, heavy, dtype=jnp.bfloat16):
    array = width * jax.random.normal(stream_key, extent, jnp.float32)
    if split:
        array = array * block_levels(stream_key, extent, split, -0.22, 0.18)
    return jnp.clip(spiked(array, jax.random.fold_in(stream_key, 3), *heavy), -bound, bound).astype(dtype)


def setup_inputs(seed: int = 0) -> dict:
    key_of = jax.random.split(jax.random.key(seed), 12)
    return {
        "tokens": gaussian_with(key_of[0], (TOKENS, D), 1.0, 6.0, ((0, 16),), (0, 1, 16, 2.0)),
        "target": gaussian_with(key_of[1], (TOKENS, D), 1.0, 6.0, ((0, 16),), (0, 1, 16, 2.0)),
        "norm_gain": jnp.clip(1.0 + 0.18 * jax.random.normal(key_of[2], (D,), jnp.float32), 0.1, 1.9),
        "w_query": gaussian(key_of[3], (D, Q_HEADS * HD), D ** -0.5, 0.0625, ((1, 8),)),
        "w_key": gaussian(key_of[4], (D, KV_HEADS * HD), D ** -0.5, 0.0625, ((1, 8),)),
        "w_value": gaussian(key_of[5], (D, KV_HEADS * HD), D ** -0.5, 0.0625, ((1, 8),)),
        "w_out": gaussian(key_of[6], (Q_HEADS * HD, D), (Q_HEADS * HD) ** -0.5, 0.09375, ((0, 8),)),
        "t_query": gaussian(key_of[7], (Q_HEADS * HD,), 1.0, 4.0, ((0, 8),), jnp.float32),
        "t_key": gaussian(key_of[8], (KV_HEADS * HD,), 1.0, 4.0, ((0, 8),), jnp.float32),
        "t_value": gaussian(key_of[9], (KV_HEADS * HD,), 1.0, 4.0, ((0, 8),), jnp.float32),
        "t_out": gaussian(key_of[10], (D,), 1.0, 4.0, (), jnp.float32),
    }


EPS = 1e-05

def rms_norm(row_block, norm_gain):
    widened = row_block.astype(jnp.float32)
    inv_rms = lax.rsqrt(lax.optimization_barrier(jnp.mean(widened * widened, axis=1, keepdims=True)) + EPS)
    return (widened * inv_rms * norm_gain.astype(jnp.float32)).astype(jnp.bfloat16)

def rotary(vectors, head_size):
    length = vectors.shape[0]
    half_width = head_size // 2
    position = jnp.arange(length).astype(jnp.float32)
    frequency = jnp.exp(-math.log(10000.0) * jnp.arange(half_width).astype(jnp.float32) * 2.0 / head_size)
    angles = position[:, None] * frequency[None, :]
    bcast_shape = (length,) + (1,) * (vectors.ndim - 2) + (half_width,)
    cosine_table = jnp.cos(angles).reshape(bcast_shape)
    sine_table = jnp.sin(angles).reshape(bcast_shape)
    front_half = vectors[..., :half_width]
    back_half = vectors[..., half_width:]
    return jnp.concatenate([front_half * cosine_table - back_half * sine_table, back_half * cosine_table + front_half * sine_table], -1)

def attend(proj_query, proj_key, proj_value):
    length = proj_query.shape[0]
    kv_count = proj_key.shape[1] // HD
    group_size = proj_query.shape[1] // proj_key.shape[1]
    rot_query = rotary(proj_query.reshape(length, kv_count, group_size, HD), HD)
    rot_key = rotary(proj_key.reshape(length, kv_count, HD), HD)
    head_values = proj_value.reshape(length, kv_count, HD)
    scores = jnp.einsum('skgd,tkd->kgst', rot_query, rot_key, precision=lax.Precision.HIGHEST) / math.sqrt(HD)
    causal = jnp.arange(length)[:, None] >= jnp.arange(length)[None, :]
    scores = jnp.where(causal, scores, -1e+30)
    attn_probs = jax.nn.softmax(scores, axis=-1)
    mixed_heads = jnp.einsum('kgst,tkd->skgd', attn_probs, head_values, precision=lax.Precision.HIGHEST)
    return mixed_heads.reshape(length, kv_count * group_size * HD)

def pullback(proj_query, proj_key, proj_value, cotangent):
    return jax.vjp(attend, proj_query, proj_key, proj_value)[1](cotangent)

def local_forward(normed, slice_query, slice_key, slice_value, slice_out, scale_query, scale_key, scale_value, t_out):
    proj_query = jnp.dot(normed, slice_query, preferred_element_type=jnp.float32)
    proj_key = jnp.dot(normed, slice_key, preferred_element_type=jnp.float32)
    proj_value = jnp.dot(normed, slice_value, preferred_element_type=jnp.float32)
    tan_query = proj_query * scale_query
    tan_key = proj_key * scale_key
    tan_value = proj_value * scale_value
    attn, tan_attn = jax.jvp(attend, (proj_query, proj_key, proj_value), (tan_query, tan_key, tan_value))
    attn_low = attn.astype(jnp.bfloat16)
    tan_attn_low = tan_attn.astype(jnp.bfloat16)
    length = normed.shape[0]
    products = jnp.dot(jnp.concatenate([attn_low, tan_attn_low], 0), slice_out, preferred_element_type=jnp.float32)
    part_rows = products[:length]
    tan_part = products[length:] + part_rows * t_out
    return (proj_query, proj_key, proj_value, tan_query, tan_key, tan_value, attn_low, tan_attn_low, part_rows, tan_part)

def local_grad(residual, tan_residual, slice_out, t_out, forward_vals):
    length = residual.shape[0]
    back_tan = (tan_residual.astype(jnp.float32) + residual.astype(jnp.float32) * t_out).astype(jnp.bfloat16)
    back_lhs = jnp.concatenate([residual, back_tan], 0)
    back_rows = lax.dot_general(back_lhs, slice_out, (((1,), (1,)), ((), ())), preferred_element_type=jnp.float32)
    primals = (forward_vals[0], forward_vals[1], forward_vals[2], back_rows[:length])
    tangents = (forward_vals[3], forward_vals[4], forward_vals[5], back_rows[length:])
    unused, grad_tans = jax.jvp(pullback, primals, tangents)
    return jnp.concatenate(list(grad_tans), 1).astype(jnp.bfloat16)

def reference(tokens, target, norm_gain, w_query, w_key, w_value, w_out, t_query, t_key, t_value, t_out):
    q_width = QH_DEV * HD
    k_width = HD
    in_width = q_width + 2 * k_width

    def shard(index):
        return (lax.dynamic_slice_in_dim(w_query, index * q_width, q_width, 1), lax.dynamic_slice_in_dim(w_key, index * k_width, k_width, 1), lax.dynamic_slice_in_dim(w_value, index * k_width, k_width, 1), lax.dynamic_slice_in_dim(w_out, index * q_width, q_width, 0), lax.dynamic_slice_in_dim(t_query, index * q_width, q_width, 0), lax.dynamic_slice_in_dim(t_key, index * k_width, k_width, 0), lax.dynamic_slice_in_dim(t_value, index * k_width, k_width, 0))
    shards = jnp.arange(N_TENSOR).astype(jnp.int32)

    def per_group(running, group_rows):
        acc_in, acc_out = running
        x_rows, target_rows = group_rows
        normed = rms_norm(x_rows, norm_gain)

        def first(index):
            pieces = shard(index)
            forward_vals = local_forward(normed, *pieces, t_out)
            return (forward_vals[8].astype(jnp.bfloat16), forward_vals[9].astype(jnp.bfloat16))
        part_all, tan_all = lax.map(first, shards)
        part_all = lax.optimization_barrier(part_all)
        tan_all = lax.optimization_barrier(tan_all)
        sum_total = lax.optimization_barrier(jnp.sum(part_all.astype(jnp.float32), 0))
        tan_total = lax.optimization_barrier(jnp.sum(tan_all.astype(jnp.float32), 0))
        residual = (x_rows.astype(jnp.float32) + sum_total - target_rows.astype(jnp.float32)).astype(jnp.bfloat16)
        tan_residual = tan_total.astype(jnp.bfloat16)

        def second(index):
            pieces = shard(index)
            forward_vals = local_forward(normed, *pieces, t_out)
            grad_tangent = local_grad(residual, tan_residual, pieces[3], t_out, forward_vals)
            in_term = lax.dot_general(normed, grad_tangent, (((0,), (0,)), ((), ())), preferred_element_type=jnp.float32)
            resid_pair = jnp.concatenate([tan_residual, residual], 0)
            attn_pair = jnp.concatenate([forward_vals[6], forward_vals[7]], 0)
            out_term = lax.dot_general(resid_pair, attn_pair, (((0,), (0,)), ((), ())), preferred_element_type=jnp.float32)
            return (in_term.astype(jnp.bfloat16), out_term.astype(jnp.bfloat16))
        in_terms, out_terms = lax.map(second, shards)
        in_terms = lax.optimization_barrier(in_terms)
        out_terms = lax.optimization_barrier(out_terms)
        return ((acc_in + in_terms.astype(jnp.float32), acc_out + out_terms.astype(jnp.float32)), None)
    token_groups = tokens.reshape(N_DP, SEQ, D)
    target_groups = target.reshape(N_DP, SEQ, D)
    start = (jnp.zeros((N_TENSOR, D, in_width), jnp.float32), jnp.zeros((N_TENSOR, D, q_width), jnp.float32))
    (acc_in, acc_out), unused = lax.scan(per_group, start, (token_groups, target_groups))
    hvp_query = jnp.transpose(acc_in[:, :, :q_width], (1, 0, 2)).reshape(D, N_TENSOR * q_width)
    hvp_key = jnp.transpose(acc_in[:, :, q_width:q_width + k_width], (1, 0, 2)).reshape(D, N_TENSOR * k_width)
    hvp_value = jnp.transpose(acc_in[:, :, q_width + k_width:], (1, 0, 2)).reshape(D, N_TENSOR * k_width)
    hvp_out = jnp.transpose(acc_out, (1, 0, 2)).reshape(D, N_TENSOR * q_width)
    return (hvp_query, hvp_key, hvp_value, hvp_out)
```

```python
import functools
import math

import jax
import jax.numpy as jnp
import numpy as np
from jax import lax
from jax.experimental import pallas as pl
from jax.experimental.pallas import tpu as pltpu
from jax.sharding import PartitionSpec as P

HD = 128
HEADS = 4
SEQ = 128
D = 8192
QW = HEADS * HD
N_DP = 16
N_T = 8
C = 512
EPS = 1e-05
F32 = jnp.float32
BF16 = jnp.bfloat16
MESH = pl.DeviceIdType.MESH


def mm(a, b):
    return lax.dot_general(
        a.astype(BF16), b.astype(BF16), (((1,), (0,)), ((), ())), preferred_element_type=F32
    )


def mm_nt(a, b):
    return lax.dot_general(
        a.astype(BF16), b.astype(BF16), (((1,), (1,)), ((), ())), preferred_element_type=F32
    )


def mm_tn(a, b):
    return lax.dot_general(
        a.astype(BF16), b.astype(BF16), (((0,), (0,)), ((), ())), preferred_element_type=F32
    )


def mm_nt_wide(a, b):
    a_hi = a.astype(BF16)
    b_hi = b.astype(BF16)
    a_lo = (a - a_hi.astype(F32)).astype(BF16)
    b_lo = (b - b_hi.astype(F32)).astype(BF16)
    return mm_nt(a_hi, b_hi) + (mm_nt(a_hi, b_lo) + mm_nt(a_lo, b_hi))


def swap_halves(x):
    return jnp.concatenate([x[:, HD // 2 :], x[:, : HD // 2]], axis=1)


def stack_heads(x):
    return jnp.concatenate([x[:, h * HD : (h + 1) * HD] for h in range(HEADS)], axis=0)


def kernel(
    tok_hbm, tgt_hbm, gain, wq_hbm, wk_hbm, wv_hbm, wo_hbm, tq, tk, tv, t_out, cos_t, sin_t,
    hq, hk, hv, ho,
    tok, tgt, wq, wk, wv, wo, nrm, nrm_g, att_g, res_g, grd_g,
    pa, pb, ra1, rb1, ra2, rb2, r_a, r_b, g_acc, proj,
    prob, tprob, rot_q, kv, gbuf,
    in_sem, wqkv_sem, wo_sem,
    nrm_s, nrm_r, att_s, att_r, res_s, res_r, grd_s, grd_r,
    a1_s, a1_r, b1_s, b1_r, a2_s, a2_r, b2_s, b2_r,
    ax_s, ax_r, ay_s, ay_r, bx_s, bx_r, bf_s, bf_r, by_s, by_r,
):
    d = lax.axis_index("dp")
    t = lax.axis_index("tensor")
    x = lax.rem(t, 4)
    y = t // 4

    def at(dy, dx):
        return lax.rem(y + dy, 2) * 4 + lax.rem(x + dx, 4)

    def remote(src, dst, s_sem, r_sem, **where):
        return pltpu.make_async_remote_copy(
            src_ref=src, dst_ref=dst, send_sem=s_sem, recv_sem=r_sem,
            device_id=where, device_id_type=MESH,
        )

    tok_copy = pltpu.make_async_copy(tok_hbm, tok, in_sem.at[0])
    tok_copy.start()
    tgt_copy = pltpu.make_async_copy(
        tgt_hbm.at[:, pl.ds(pl.multiple_of(t * 2 * C, 2 * C), 2 * C)], tgt, in_sem.at[1]
    )

    def w_copies(c):
        rows = pl.ds(c * C, C)
        return (
            pltpu.make_async_copy(wq_hbm.at[rows, :], wq.at[c], wqkv_sem.at[0, c]),
            pltpu.make_async_copy(wk_hbm.at[rows, :], wk.at[c], wqkv_sem.at[1, c]),
            pltpu.make_async_copy(wv_hbm.at[rows, :], wv.at[c], wqkv_sem.at[2, c]),
        )

    def wo_copy(c):
        return pltpu.make_async_copy(
            wo_hbm.at[:, pl.ds(pl.multiple_of(c * C, C), C)], wo.at[c], wo_sem.at[c]
        )

    @pl.loop(0, N_DP)
    def _(c):
        for cp in w_copies(c):
            cp.start()

    tgt_copy.start()

    @pl.loop(0, N_DP)
    def _(c):
        wo_copy(c).start()

    bar = pltpu.get_barrier_semaphore()

    @pl.loop(1, N_DP)
    def _(r):
        pl.semaphore_signal(
            bar, inc=1, device_id={"dp": lax.rem(d + r, N_DP)}, device_id_type=MESH
        )

    for dy, dx in ((1, 0), (0, 1), (0, 2), (0, 3)):
        pl.semaphore_signal(bar, inc=1, device_id={"tensor": at(dy, dx)}, device_id_type=MESH)

    tok_copy.wait()

    def square_step(c, acc):
        v = tok[:, pl.ds(pl.multiple_of(c * C, C), C)].astype(F32)
        return acc + v * v

    squares = lax.fori_loop(0, N_DP, square_step, jnp.zeros((SEQ, C), F32))
    inv = lax.rsqrt(jnp.sum(squares, axis=1, keepdims=True) * (1.0 / D) + EPS)

    @pl.loop(0, N_DP)
    def _(c):
        cols = pl.ds(pl.multiple_of(c * C, C), C)
        nrm[c] = (tok[:, cols].astype(F32) * inv * gain[:, cols]).astype(BF16)

    nrm_g[d] = nrm[d]

    pl.semaphore_wait(bar, N_DP - 1 + 4)

    def nrm_copy(r):
        dest = lax.rem(d + r, N_DP)
        return remote(nrm.at[dest], nrm_g.at[d], nrm_s.at[r], nrm_r.at[d], dp=dest)

    @pl.loop(1, N_DP)
    def _(r):
        nrm_copy(r).start()

    proj[...] = jnp.zeros_like(proj)

    @pl.loop(0, N_DP)
    def _(c):
        for cp in w_copies(c):
            cp.wait()
        lhs = nrm[c]
        proj[:, :QW] += mm(lhs, wq[c])
        proj[:, QW : QW + HD] += mm(lhs, wk[c])
        proj[:, QW + HD :] += mm(lhs, wv[c])

    cos1 = cos_t[...]
    sin1 = sin_t[...]
    cos4 = jnp.concatenate([cos1] * HEADS, axis=0)
    sin4 = jnp.concatenate([sin1] * HEADS, axis=0)
    scale = 1.0 / math.sqrt(HD)

    q2 = proj[:, :QW]
    key = proj[:, QW : QW + HD]
    val = proj[:, QW + HD :]
    tval = val * tv[...]
    qs = stack_heads(q2)
    tqs = stack_heads(q2 * tq[...])
    rq = qs * cos4 + swap_halves(qs) * sin4
    trq = tqs * cos4 + swap_halves(tqs) * sin4
    tkey = key * tk[...]
    rk = key * cos1 + swap_halves(key) * sin1
    trk = tkey * cos1 + swap_halves(tkey) * sin1
    rot_q[...] = jnp.concatenate([rq.astype(BF16), trq.astype(BF16)], axis=0)
    kv[0] = rk.astype(BF16)
    kv[1] = trk.astype(BF16)
    kv[2] = val.astype(BF16)
    kv[3] = tval.astype(BF16)
    scores = mm_nt_wide(rq, rk) * scale
    tscores = (mm_nt_wide(trq, rk) + mm_nt_wide(rq, trk)) * scale
    row = lax.rem(lax.broadcasted_iota(jnp.int32, (HEADS * SEQ, SEQ), 0), SEQ)
    col = lax.broadcasted_iota(jnp.int32, (HEADS * SEQ, SEQ), 1)
    scores = jnp.where(row >= col, scores, -1e30)
    e = jnp.exp(scores - jnp.max(scores, axis=1, keepdims=True))
    p = e / jnp.sum(e, axis=1, keepdims=True)
    tp = p * (tscores - jnp.sum(p * tscores, axis=1, keepdims=True))
    prob[...] = p
    tprob[...] = tp
    o = mm(p, val)
    to = mm(tp, val) + mm(p, tval)
    for h in range(HEADS):
        att_g[d, :SEQ, h * HD : (h + 1) * HD] = to[h * SEQ : (h + 1) * SEQ].astype(BF16)
        att_g[d, SEQ:, h * HD : (h + 1) * HD] = o[h * SEQ : (h + 1) * SEQ].astype(BF16)

    def att_copy(r):
        return remote(
            att_g.at[d], att_g.at[d], att_s.at[r], att_r.at[d], dp=lax.rem(d + r, N_DP)
        )

    @pl.loop(1, N_DP)
    def _(r):
        att_copy(r).start()

    @pl.loop(0, N_DP)
    def _(c):
        wo_copy(c).wait()

    def t_cols(c):
        return t_out[:, pl.ds(pl.multiple_of(c * C, C), C)]

    def part(dy, dx, half, dst):
        c = at(dy, dx) * 2 + half
        rows = mm(att_g[d], wo[c])
        dst[dy, dx, :SEQ, :] = rows[SEQ:].astype(BF16)
        dst[dy, dx, SEQ:, :] = (rows[:SEQ] + rows[SEQ:] * t_cols(c)).astype(BF16)

    def a1_copy(dx):
        return remote(pa.at[1, dx], ra1.at[dx], a1_s.at[dx], a1_r.at[dx], tensor=at(1, 0))

    def b1_copy(dy, dx):
        return remote(
            pb.at[dy, dx], rb1.at[dy, dx], b1_s.at[dy, dx], b1_r.at[dy, dx], tensor=at(0, dx)
        )

    def a2_copy(dx):
        return remote(pa.at[0, dx], ra2.at[dx], a2_s.at[dx], a2_r.at[dx], tensor=at(0, dx))

    def b2_copy():
        return remote(pb.at[1, 0], rb2, b2_s, b2_r, tensor=at(1, 0))

    for dx in (1, 3, 2):
        part(1, dx, 0, pa)
        a1_copy(dx).start()
        part(1, dx, 1, pb)
        b1_copy(1, dx).start()
    part(1, 0, 0, pa)
    a1_copy(0).start()
    for dx in (1, 3, 2):
        part(0, dx, 1, pb)
        b1_copy(0, dx).start()
    part(1, 0, 1, pb)
    for dx in (1, 3, 2, 0):
        part(0, dx, 0, pa)
    part(0, 0, 1, pb)
    for dx in (1, 3, 2):
        a1_copy(dx).wait_recv()
        pa[0, dx] = (pa[0, dx].astype(F32) + ra1[dx].astype(F32)).astype(BF16)
        a2_copy(dx).start()
    total = pb[1, 0].astype(F32)
    for dx in (1, 3, 2):
        b1_copy(1, dx).wait_recv()
        total += rb1[1, dx].astype(F32)
    pb[1, 0] = total.astype(BF16)
    b2_copy().start()

    tgt_copy.wait()

    def residual(total, half, dst):
        c = t * 2 + half
        base = tok[:, pl.ds(pl.multiple_of(c * C, C), C)].astype(F32)
        aim = tgt[:, half * C : (half + 1) * C].astype(F32)
        dst[t, :SEQ, :] = (base + total[:SEQ] - aim).astype(BF16)
        dst[t, SEQ:, :] = total[SEQ:].astype(BF16)

    def ax_copy(dx, j):
        return remote(r_a.at[j], r_a.at[j], ax_s.at[dx], ax_r.at[dx], tensor=at(0, dx))

    def ay_copy(dx, j):
        return remote(r_a.at[j], r_a.at[j], ay_s.at[dx], ay_r.at[dx], tensor=at(1, 0))

    def bx_copy(dx, j):
        return remote(r_b.at[j], r_b.at[j], bx_s.at[dx], bx_r.at[dx], tensor=at(0, dx))

    def bf_copy(dx, j):
        return remote(r_b.at[j], r_b.at[j], bf_s.at[dx], bf_r.at[dx], tensor=at(0, dx))

    def by_copy(j):
        return remote(r_b.at[j], r_b.at[j], by_s, by_r, tensor=at(1, 0))

    def res_copy(j, half):
        src = (r_a, r_b)[half]
        c = 2 * j + half
        return remote(src.at[j], res_g.at[d], res_s.at[c], res_r.at[d], dp=c)

    def use(j, half):
        src = (r_a, r_b)[half]
        c = 2 * j + half

        @pl.when(c != d)
        def _():
            res_copy(j, half).start()

        @pl.when(c == d)
        def _():
            res_g[d] = src[j]

        rows = src[j]
        first = rows[:SEQ]
        second = (rows[SEQ:].astype(F32) + first.astype(F32) * t_cols(c)).astype(BF16)
        g_acc[...] += mm_nt(jnp.concatenate([first, second], axis=0), wo[c])

    a1_copy(0).wait_recv()
    total = pa[0, 0].astype(F32) + ra1[0].astype(F32)
    for dx in (1, 3, 2):
        a2_copy(dx).wait_recv()
        total += ra2[dx].astype(F32)
    residual(total, 0, r_a)
    for dx in (1, 3, 2):
        ax_copy(dx, t).start()
    ay_copy(0, t).start()

    total = pb[0, 0].astype(F32)
    for dx in (1, 3, 2):
        b1_copy(0, dx).wait_recv()
        total += rb1[0, dx].astype(F32)
    b2_copy().wait_recv()
    total += rb2[...].astype(F32)
    residual(total, 1, r_b)
    by_copy(t).start()
    for dx in (1, 3, 2):
        bx_copy(dx, t).start()

    g_acc[...] = jnp.zeros_like(g_acc)
    use(t, 0)
    use(t, 1)
    j = at(1, 0)
    by_copy(j).wait_recv()
    for dx in (1, 3, 2):
        bf_copy(dx, j).start()
    use(j, 1)
    for dx in (1, 3, 2):
        j = at(0, 4 - dx)
        ax_copy(dx, j).wait_recv()
        ay_copy(dx, j).start()
        use(j, 0)
    use_order = (1, 3, 2)
    j = at(1, 0)
    ay_copy(0, j).wait_recv()
    use(j, 0)
    for dx in use_order:
        j = at(0, 4 - dx)
        bx_copy(dx, j).wait_recv()
        use(j, 1)
    for dx in use_order:
        j = at(1, 4 - dx)
        ay_copy(dx, j).wait_recv()
        use(j, 0)
        bf_copy(dx, j).wait_recv()
        use(j, 1)

    key = kv[0]
    tkey = kv[1]
    val = kv[2]
    tval = kv[3]
    g1 = stack_heads(g_acc[:SEQ]).astype(BF16)
    g2 = stack_heads(g_acc[SEQ:]).astype(BF16)
    p = prob[...]
    tp = tprob[...]
    dpr = mm_nt(g1, val)
    tdpr = mm_nt(g2, val) + mm_nt(g1, tval)
    tval_grad = mm_tn(jnp.concatenate([tp, p], axis=0), jnp.concatenate([g1, g2], axis=0))
    grd_g[d, :, QW + HD :] = tval_grad.astype(BF16)
    dpr = dpr - jnp.sum(p * dpr, axis=1, keepdims=True)
    tdpr = tdpr - jnp.sum(tp * dpr + p * tdpr, axis=1, keepdims=True)
    ds = (p * dpr).astype(BF16)
    tds = (tp * dpr + p * tdpr).astype(BF16)
    both = jnp.concatenate([tds, ds], axis=0)
    trk_grad = mm_tn(both, rot_q[...]) * scale
    trk_grad = trk_grad * cos1 - swap_halves(trk_grad) * sin1
    grd_g[d, :, QW : QW + HD] = trk_grad.astype(BF16)
    trq_grad = (mm(tds, key) + mm(ds, tkey)) * scale
    trq_grad = trq_grad * cos4 - swap_halves(trq_grad) * sin4
    for h in range(HEADS):
        grd_g[d, :, h * HD : (h + 1) * HD] = trq_grad[h * SEQ : (h + 1) * SEQ].astype(BF16)

    def grd_copy(r):
        return remote(
            grd_g.at[d], grd_g.at[d], grd_s.at[r], grd_r.at[d], dp=lax.rem(d + r, N_DP)
        )

    @pl.loop(1, N_DP)
    def _(r):
        grd_copy(r).start()

    @pl.loop(1, N_DP)
    def _(r):
        src = lax.rem(d + N_DP - r, N_DP)
        remote(att_g.at[src], att_g.at[src], att_s.at[r], att_r.at[src], dp=src).wait_recv()

    @pl.loop(1, N_DP)
    def _(r):
        src = lax.rem(d + N_DP - r, N_DP)
        remote(res_g.at[src], res_g.at[src], res_s.at[r], res_r.at[src], dp=src).wait_recv()

    STEP = 4
    ho[...] = jnp.zeros_like(ho)

    @pl.loop(0, N_DP // STEP)
    def _(s):
        rows = pl.ds(s * STEP, STEP)
        lhs = res_g[rows].reshape(STEP * 2 * SEQ, C)
        rhs = att_g[rows].reshape(STEP * 2 * SEQ, QW)
        ho[...] += mm_tn(lhs, rhs)

    @pl.loop(1, N_DP)
    def _(r):
        src = lax.rem(d + N_DP - r, N_DP)
        remote(nrm_g.at[src], nrm_g.at[src], nrm_s.at[r], nrm_r.at[src], dp=src).wait_recv()

    @pl.loop(1, N_DP)
    def _(r):
        src = lax.rem(d + N_DP - r, N_DP)
        remote(grd_g.at[src], grd_g.at[src], grd_s.at[r], grd_r.at[src], dp=src).wait_recv()

    gbuf[...] = jnp.zeros_like(gbuf)

    @pl.loop(0, N_DP // STEP)
    def _(s):
        rows = pl.ds(s * STEP, STEP)
        lhs = nrm_g[rows].reshape(STEP * SEQ, C)
        rhs = grd_g[rows].reshape(STEP * SEQ, QW + 2 * HD)
        gbuf[...] += mm_tn(lhs, rhs)

    hq[...] = gbuf[:, :QW]
    hk[...] = gbuf[:, QW : QW + HD]
    hv[...] = gbuf[:, QW + HD :]

    @pl.loop(1, N_DP)
    def _(r):
        nrm_copy(r).wait_send()
        att_copy(r).wait_send()
        grd_copy(r).wait_send()

    @pl.loop(0, N_T)
    def _(j):
        for half in range(2):

            @pl.when(2 * j + half != d)
            def _():
                res_copy(j, half).wait_send()

    for dx in range(4):
        a1_copy(dx).wait_send()
        ay_copy(dx, t).wait_send()
    for dx in (1, 2, 3):
        b1_copy(0, dx).wait_send()
        b1_copy(1, dx).wait_send()
        a2_copy(dx).wait_send()
        ax_copy(dx, t).wait_send()
        bx_copy(dx, t).wait_send()
        bf_copy(dx, t).wait_send()
    b2_copy().wait_send()
    by_copy(t).wait_send()


def tables():
    frequency = np.exp(
        np.float32(-math.log(10000.0)) * np.arange(HD // 2, dtype=np.float32) * np.float32(2.0)
        / np.float32(HD)
    ).astype(np.float32)
    angles = np.arange(SEQ, dtype=np.float32)[:, None] * frequency[None, :]
    cosine = np.cos(angles).astype(np.float32)
    sine = np.sin(angles).astype(np.float32)
    return np.concatenate([cosine, cosine], 1), np.concatenate([-sine, sine], 1)


def local(
    tokens, target, norm_gain, w_query, w_key, w_value, w_out, t_query, t_key, t_value, t_out
):
    cos_t, sin_t = tables()
    any_spec = pl.BlockSpec(memory_space=pl.ANY)
    vmem = pl.BlockSpec(memory_space=pltpu.VMEM)
    dma = pltpu.SemaphoreType.DMA
    block = (2 * SEQ, C)
    scratch = [
        pltpu.VMEM((SEQ, D), BF16),
        pltpu.VMEM((SEQ, 2 * C), BF16),
        pltpu.VMEM((N_DP, C, QW), BF16),
        pltpu.VMEM((N_DP, C, HD), BF16),
        pltpu.VMEM((N_DP, C, HD), BF16),
        pltpu.VMEM((N_DP, QW, C), BF16),
        pltpu.VMEM((N_DP, SEQ, C), BF16),
        pltpu.VMEM((N_DP, SEQ, C), BF16),
        pltpu.VMEM((N_DP, 2 * SEQ, QW), BF16),
        pltpu.VMEM((N_DP,) + block, BF16),
        pltpu.VMEM((N_DP, SEQ, QW + 2 * HD), BF16),
        pltpu.VMEM((2, 4) + block, BF16),
        pltpu.VMEM((2, 4) + block, BF16),
        pltpu.VMEM((4,) + block, BF16),
        pltpu.VMEM((2, 4) + block, BF16),
        pltpu.VMEM((4,) + block, BF16),
        pltpu.VMEM(block, BF16),
        pltpu.VMEM((N_T,) + block, BF16),
        pltpu.VMEM((N_T,) + block, BF16),
        pltpu.VMEM((2 * SEQ, QW), F32),
        pltpu.VMEM((SEQ, QW + 2 * HD), F32),
        pltpu.VMEM((HEADS * SEQ, SEQ), F32),
        pltpu.VMEM((HEADS * SEQ, SEQ), F32),
        pltpu.VMEM((2 * HEADS * SEQ, HD), BF16),
        pltpu.VMEM((4, SEQ, HD), BF16),
        pltpu.VMEM((C, QW + 2 * HD), F32),
        dma((2,)), dma((3, N_DP)), dma((N_DP,)),
        dma((N_DP,)), dma((N_DP,)), dma((N_DP,)), dma((N_DP,)),
        dma((N_DP,)), dma((N_DP,)), dma((N_DP,)), dma((N_DP,)),
        dma((4,)), dma((4,)), dma((2, 4)), dma((2, 4)), dma((4,)), dma((4,)), dma, dma,
        dma((4,)), dma((4,)), dma((4,)), dma((4,)),
        dma((4,)), dma((4,)), dma((4,)), dma((4,)), dma, dma,
    ]
    return pl.pallas_call(
        kernel,
        out_shape=(
            jax.ShapeDtypeStruct((C, QW), F32),
            jax.ShapeDtypeStruct((C, HD), F32),
            jax.ShapeDtypeStruct((C, HD), F32),
            jax.ShapeDtypeStruct((C, QW), F32),
        ),
        in_specs=[
            any_spec, any_spec, vmem, any_spec, any_spec, any_spec, any_spec,
            vmem, vmem, vmem, vmem, vmem, vmem,
        ],
        out_specs=(vmem, vmem, vmem, vmem),
        scratch_shapes=scratch,
        compiler_params=pltpu.CompilerParams(
            collective_id=0, has_side_effects=True, vmem_limit_bytes=62 * 1024 * 1024
        ),
        cost_estimate=pl.CostEstimate(
            flops=10_000_000_000, bytes_accessed=26_000_000, transcendentals=65536
        ),
        name="hvp",
    )(
        tokens, target, norm_gain.reshape(1, D), w_query, w_key, w_value, w_out,
        t_query.reshape(1, QW), t_key.reshape(1, HD), t_value.reshape(1, HD),
        t_out.reshape(1, D), jnp.asarray(cos_t), jnp.asarray(sin_t),
    )


def solution(mesh):
    return jax.shard_map(
        local,
        mesh=mesh,
        in_specs=(
            P("dp", None),
            P("dp", None),
            P(),
            P(None, "tensor"),
            P(None, "tensor"),
            P(None, "tensor"),
            P("tensor", None),
            P("tensor"),
            P("tensor"),
            P("tensor"),
            P(),
        ),
        out_specs=(P("dp", "tensor"), P("dp", "tensor"), P("dp", "tensor"), P("dp", "tensor")),
        check_vma=False,
    )
```

```python
import functools
import math

import jax
import jax.numpy as jnp
import numpy as np
from jax import lax
from jax.experimental import pallas as pl
from jax.experimental.pallas import tpu as pltpu
from jax.sharding import PartitionSpec as P

HD = 128
HEADS = 4
SEQ = 128
D = 8192
QW = HEADS * HD
N_DP = 16
N_T = 8
C = 512
EPS = 1e-05
F32 = jnp.float32
BF16 = jnp.bfloat16
MESH = pl.DeviceIdType.MESH


def mm(a, b):
    return lax.dot_general(
        a.astype(BF16), b.astype(BF16), (((1,), (0,)), ((), ())), preferred_element_type=F32
    )


def mm_nt(a, b):
    return lax.dot_general(
        a.astype(BF16), b.astype(BF16), (((1,), (1,)), ((), ())), preferred_element_type=F32
    )


def mm_tn(a, b):
    return lax.dot_general(
        a.astype(BF16), b.astype(BF16), (((0,), (0,)), ((), ())), preferred_element_type=F32
    )


def mm_nt_wide(a, b):
    a_hi = a.astype(BF16)
    b_hi = b.astype(BF16)
    a_lo = (a - a_hi.astype(F32)).astype(BF16)
    b_lo = (b - b_hi.astype(F32)).astype(BF16)
    return mm_nt(a_hi, b_hi) + (mm_nt(a_hi, b_lo) + mm_nt(a_lo, b_hi))


def swap_halves(x):
    return jnp.concatenate([x[:, HD // 2 :], x[:, : HD // 2]], axis=1)


def stack_heads(x):
    return jnp.concatenate([x[:, h * HD : (h + 1) * HD] for h in range(HEADS)], axis=0)


def kernel(
    tok_hbm, tgt_hbm, gain, wq_hbm, wk_hbm, wv_hbm, wo_hbm, tq, tk, tv, t_out, cos_t, sin_t,
    hq, hk, hv, ho,
    tok, tgt, wq, wk, wv, wo, nrm, nrm_g, att, sib, zr, yr, grd_g,
    pa, pb, ra1, rb1, ra2, rb2, r_a, r_b, g_acc, proj,
    prob, tprob, rot_q, kv,
    in_sem, wqkv_sem, wo_sem,
    nrm_s, nrm_r, sib_s, sib_r, z_s, z_r, y_s, y_r,
    gz_s, gz_r, gy_s, gy_r, gf_s, gf_r, gs_s, gs_r,
    a1_s, a1_r, b1_s, b1_r, a2_s, a2_r, b2_s, b2_r,
    ax_s, ax_r, ay_s, ay_r, bx_s, bx_r, bf_s, bf_r, by_s, by_r,
):
    d = lax.axis_index("dp")
    t = lax.axis_index("tensor")
    x = lax.rem(t, 4)
    y = t // 4
    core = lax.rem(d, 2)
    z = lax.rem(d // 2, 4)
    y_hi = d // 8

    def dev(ry, rz, rc):
        return (lax.rem(y_hi + ry, 2) * 4 + lax.rem(z + rz, 4)) * 2 + lax.rem(core + rc, 2)

    def at(dy, dx):
        return lax.rem(y + dy, 2) * 4 + lax.rem(x + dx, 4)

    def remote(src, dst, s_sem, r_sem, **where):
        return pltpu.make_async_remote_copy(
            src_ref=src, dst_ref=dst, send_sem=s_sem, recv_sem=r_sem,
            device_id=where, device_id_type=MESH,
        )

    tok_copy = pltpu.make_async_copy(tok_hbm, tok, in_sem.at[0])
    tok_copy.start()
    tgt_copy = pltpu.make_async_copy(
        tgt_hbm.at[:, pl.ds(pl.multiple_of(t * 2 * C, 2 * C), 2 * C)], tgt, in_sem.at[1]
    )

    def w_copies(c):
        rows = pl.ds(c * C, C)
        return (
            pltpu.make_async_copy(wq_hbm.at[rows, :], wq.at[c], wqkv_sem.at[0, c]),
            pltpu.make_async_copy(wk_hbm.at[rows, :], wk.at[c], wqkv_sem.at[1, c]),
            pltpu.make_async_copy(wv_hbm.at[rows, :], wv.at[c], wqkv_sem.at[2, c]),
        )

    def wo_copy(c):
        return pltpu.make_async_copy(
            wo_hbm.at[:, pl.ds(pl.multiple_of(c * C, C), C)], wo.at[c], wo_sem.at[c]
        )

    @pl.loop(0, N_DP)
    def _(c):
        for cp in w_copies(c):
            cp.start()

    tgt_copy.start()

    @pl.loop(0, N_DP)
    def _(c):
        wo_copy(c).start()

    bar = pltpu.get_barrier_semaphore()

    @pl.loop(1, N_DP)
    def _(r):
        pl.semaphore_signal(
            bar, inc=1, device_id={"dp": lax.rem(d + r, N_DP)}, device_id_type=MESH
        )

    for dy, dx in ((1, 0), (0, 1), (0, 2), (0, 3)):
        pl.semaphore_signal(bar, inc=1, device_id={"tensor": at(dy, dx)}, device_id_type=MESH)

    tok_copy.wait()

    def square_step(c, acc):
        v = tok[:, pl.ds(pl.multiple_of(c * C, C), C)].astype(F32)
        return acc + v * v

    squares = lax.fori_loop(0, N_DP, square_step, jnp.zeros((SEQ, C), F32))
    inv = lax.rsqrt(jnp.sum(squares, axis=1, keepdims=True) * (1.0 / D) + EPS)

    @pl.loop(0, N_DP)
    def _(c):
        cols = pl.ds(pl.multiple_of(c * C, C), C)
        nrm[c] = (tok[:, cols].astype(F32) * inv * gain[:, cols]).astype(BF16)

    nrm_g[d] = nrm[d]

    pl.semaphore_wait(bar, N_DP - 1 + 4)

    def nrm_copy(ry, rz, rc):
        dest = dev(ry, rz, rc)
        r = (ry * 4 + rz) * 2 + rc
        return remote(nrm.at[dest], nrm_g.at[d], nrm_s.at[r], nrm_r.at[r], dp=dest)

    early = [(0, rz, rc) for rz in (1, 3, 2) for rc in (0, 1)] + [(0, 0, 1)]
    early += [(1, rz, rc) for rz in (0, 2) for rc in (0, 1)]
    late = [(1, rz, rc) for rz in (1, 3) for rc in (0, 1)]
    for rel in early:
        nrm_copy(*rel).start()

    proj[...] = jnp.zeros_like(proj)

    @pl.loop(0, N_DP)
    def _(c):
        for cp in w_copies(c):
            cp.wait()
        lhs = nrm[c]
        proj[:, :QW] += mm(lhs, wq[c])
        proj[:, QW : QW + HD] += mm(lhs, wk[c])
        proj[:, QW + HD :] += mm(lhs, wv[c])

    cos1 = cos_t[...]
    sin1 = sin_t[...]
    cos4 = jnp.concatenate([cos1] * HEADS, axis=0)
    sin4 = jnp.concatenate([sin1] * HEADS, axis=0)
    scale = 1.0 / math.sqrt(HD)

    q2 = proj[:, :QW]
    key = proj[:, QW : QW + HD]
    val = proj[:, QW + HD :]
    tval = val * tv[...]
    qs = stack_heads(q2)
    tqs = stack_heads(q2 * tq[...])
    rq = qs * cos4 + swap_halves(qs) * sin4
    trq = tqs * cos4 + swap_halves(tqs) * sin4
    tkey = key * tk[...]
    rk = key * cos1 + swap_halves(key) * sin1
    trk = tkey * cos1 + swap_halves(tkey) * sin1
    rot_q[...] = jnp.concatenate([rq.astype(BF16), trq.astype(BF16)], axis=0)
    kv[0] = rk.astype(BF16)
    kv[1] = trk.astype(BF16)
    kv[2] = val.astype(BF16)
    kv[3] = tval.astype(BF16)
    scores = mm_nt_wide(rq, rk) * scale
    tscores = (mm_nt_wide(trq, rk) + mm_nt_wide(rq, trk)) * scale
    row = lax.rem(lax.broadcasted_iota(jnp.int32, (HEADS * SEQ, SEQ), 0), SEQ)
    col = lax.broadcasted_iota(jnp.int32, (HEADS * SEQ, SEQ), 1)
    scores = jnp.where(row >= col, scores, -1e30)
    e = jnp.exp(scores - jnp.max(scores, axis=1, keepdims=True))
    p = e / jnp.sum(e, axis=1, keepdims=True)
    tp = p * (tscores - jnp.sum(p * tscores, axis=1, keepdims=True))
    prob[...] = p
    tprob[...] = tp
    o = mm(p, val)
    to = mm(tp, val) + mm(p, tval)
    for h in range(HEADS):
        att[:SEQ, h * HD : (h + 1) * HD] = to[h * SEQ : (h + 1) * SEQ].astype(BF16)
        att[SEQ:, h * HD : (h + 1) * HD] = o[h * SEQ : (h + 1) * SEQ].astype(BF16)

    @pl.loop(0, N_DP)
    def _(c):
        wo_copy(c).wait()

    def t_cols(c):
        return t_out[:, pl.ds(pl.multiple_of(c * C, C), C)]

    def part(dy, dx, half, dst):
        c = at(dy, dx) * 2 + half
        rows = mm(att[...], wo[c])
        dst[dy, dx, :SEQ, :] = rows[SEQ:].astype(BF16)
        dst[dy, dx, SEQ:, :] = (rows[:SEQ] + rows[SEQ:] * t_cols(c)).astype(BF16)

    def a1_copy(dx):
        return remote(pa.at[1, dx], ra1.at[dx], a1_s.at[dx], a1_r.at[dx], tensor=at(1, 0))

    def b1_copy(dy, dx):
        return remote(
            pb.at[dy, dx], rb1.at[dy, dx], b1_s.at[dy, dx], b1_r.at[dy, dx], tensor=at(0, dx)
        )

    def a2_copy(dx):
        return remote(pa.at[0, dx], ra2.at[dx], a2_s.at[dx], a2_r.at[dx], tensor=at(0, dx))

    def b2_copy():
        return remote(pb.at[1, 0], rb2, b2_s, b2_r, tensor=at(1, 0))

    for dx in (1, 3, 2):
        part(1, dx, 0, pa)
        a1_copy(dx).start()
        part(1, dx, 1, pb)
        b1_copy(1, dx).start()
    part(1, 0, 0, pa)
    a1_copy(0).start()
    for dx in (1, 3, 2):
        part(0, dx, 1, pb)
        b1_copy(0, dx).start()
    part(1, 0, 1, pb)
    for dx in (1, 3, 2, 0):
        part(0, dx, 0, pa)
    part(0, 0, 1, pb)
    for dx in (1, 3, 2):
        a1_copy(dx).wait_recv()
        pa[0, dx] = (pa[0, dx].astype(F32) + ra1[dx].astype(F32)).astype(BF16)
        a2_copy(dx).start()
    total = pb[1, 0].astype(F32)
    for dx in (1, 3, 2):
        b1_copy(1, dx).wait_recv()
        total += rb1[1, dx].astype(F32)
    pb[1, 0] = total.astype(BF16)
    b2_copy().start()

    tgt_copy.wait()

    def residual(total, half, dst):
        c = t * 2 + half
        base = tok[:, pl.ds(pl.multiple_of(c * C, C), C)].astype(F32)
        aim = tgt[:, half * C : (half + 1) * C].astype(F32)
        dst[t, :SEQ, :] = (base + total[:SEQ] - aim).astype(BF16)
        dst[t, SEQ:, :] = total[SEQ:].astype(BF16)

    def ax_copy(dx, j):
        return remote(r_a.at[j], r_a.at[j], ax_s.at[dx], ax_r.at[dx], tensor=at(0, dx))

    def ay_copy(dx, j):
        return remote(r_a.at[j], r_a.at[j], ay_s.at[dx], ay_r.at[dx], tensor=at(1, 0))

    def bx_copy(dx, j):
        return remote(r_b.at[j], r_b.at[j], bx_s.at[dx], bx_r.at[dx], tensor=at(0, dx))

    def bf_copy(dx, j):
        return remote(r_b.at[j], r_b.at[j], bf_s.at[dx], bf_r.at[dx], tensor=at(0, dx))

    def by_copy(j):
        return remote(r_b.at[j], r_b.at[j], by_s, by_r, tensor=at(1, 0))

    def sib_copy(j, half):
        return remote(wq.at[half * N_T + j], sib.at[j], sib_s.at[j], sib_r.at[j], dp=dev(0, 0, 1))

    def use(j, half):
        src = (r_a, r_b)[half]
        rows = src[j]
        wq[half * N_T + j] = mm_tn(rows, att[...]).astype(BF16)

        @pl.when(core != half)
        def _():
            sib_copy(j, half).start()

        c = 2 * j + half
        first = rows[:SEQ]
        second = (rows[SEQ:].astype(F32) + first.astype(F32) * t_cols(c)).astype(BF16)
        g_acc[...] += mm_nt(jnp.concatenate([first, second], axis=0), wo[c])

    def z_copy(j):
        slot = core * N_T + j
        return remote(
            wq.at[slot], zr.at[j // 4, z], z_s.at[j], z_r.at[j // 4, z],
            dp=(y_hi * 4 + lax.rem(j, 4)) * 2 + core,
        )

    def combine(j):
        slot = core * N_T + j
        sib_copy(j, 0).wait_recv()
        wq[slot] = (wq[slot].astype(F32) + sib[j].astype(F32)).astype(BF16)

        @pl.when(lax.rem(j, 4) != z)
        def _():
            z_copy(j).start()

    a1_copy(0).wait_recv()
    total = pa[0, 0].astype(F32) + ra1[0].astype(F32)
    for dx in (1, 3, 2):
        a2_copy(dx).wait_recv()
        total += ra2[dx].astype(F32)
    residual(total, 0, r_a)
    for dx in (1, 3, 2):
        ax_copy(dx, t).start()
    ay_copy(0, t).start()

    total = pb[0, 0].astype(F32)
    for dx in (1, 3, 2):
        b1_copy(0, dx).wait_recv()
        total += rb1[0, dx].astype(F32)
    b2_copy().wait_recv()
    total += rb2[...].astype(F32)
    residual(total, 1, r_b)
    by_copy(t).start()
    for dx in (1, 3, 2):
        bx_copy(dx, t).start()

    g_acc[...] = jnp.zeros_like(g_acc)
    use(t, 0)
    use(t, 1)
    j = at(1, 0)
    by_copy(j).wait_recv()
    for dx in (1, 3, 2):
        bf_copy(dx, j).start()
    use(j, 1)
    combine(t)
    for dx in (1, 3, 2):
        j = at(0, 4 - dx)
        ax_copy(dx, j).wait_recv()
        ay_copy(dx, j).start()
        use(j, 0)
    j = at(1, 0)
    ay_copy(0, j).wait_recv()
    use(j, 0)
    pending = [j]
    for dx in (1, 3, 2):
        j = at(0, 4 - dx)
        bx_copy(dx, j).wait_recv()
        use(j, 1)
        combine(pending.pop())
        pending.append(j)
    for dx in (1, 3, 2):
        j = at(1, 4 - dx)
        ay_copy(dx, j).wait_recv()
        use(j, 0)
        combine(pending.pop())
        bf_copy(dx, j).wait_recv()
        use(j, 1)
        pending.append(j)

    key = kv[0]
    tkey = kv[1]
    val = kv[2]
    tval = kv[3]
    g1 = stack_heads(g_acc[:SEQ]).astype(BF16)
    g2 = stack_heads(g_acc[SEQ:]).astype(BF16)
    p = prob[...]
    tp = tprob[...]
    dpr = mm_nt(g1, val)
    tdpr = mm_nt(g2, val) + mm_nt(g1, tval)
    tval_grad = mm_tn(jnp.concatenate([tp, p], axis=0), jnp.concatenate([g1, g2], axis=0))
    grd_g[d, :, QW + HD :] = tval_grad.astype(BF16)
    dpr = dpr - jnp.sum(p * dpr, axis=1, keepdims=True)
    tdpr = tdpr - jnp.sum(tp * dpr + p * tdpr, axis=1, keepdims=True)
    ds = (p * dpr).astype(BF16)
    tds = (tp * dpr + p * tdpr).astype(BF16)
    both = jnp.concatenate([tds, ds], axis=0)
    trk_grad = mm_tn(both, rot_q[...]) * scale
    trk_grad = trk_grad * cos1 - swap_halves(trk_grad) * sin1
    grd_g[d, :, QW : QW + HD] = trk_grad.astype(BF16)
    trq_grad = (mm(tds, key) + mm(ds, tkey)) * scale
    trq_grad = trq_grad * cos4 - swap_halves(trq_grad) * sin4
    for h in range(HEADS):
        grd_g[d, :, h * HD : (h + 1) * HD] = trq_grad[h * SEQ : (h + 1) * SEQ].astype(BF16)

    def gs_copy(ry, rz):
        b = dev(ry, 4 - rz, 0)
        return remote(
            grd_g.at[b], grd_g.at[b], gs_s.at[ry, rz], gs_r.at[ry, rz], dp=dev(0, 0, 1)
        )

    def gz_copy(rz, b):
        return remote(grd_g.at[b], grd_g.at[b], gz_s.at[rz], gz_r.at[rz], dp=dev(0, rz, 0))

    def gf_copy(rz, b):
        return remote(grd_g.at[b], grd_g.at[b], gf_s.at[rz], gf_r.at[rz], dp=dev(0, rz, 0))

    def gy_copy(b):
        return remote(grd_g.at[b], grd_g.at[b], gy_s, gy_r, dp=dev(1, 0, 0))

    gy_copy(d).start()
    for rz in (1, 3, 2):
        gz_copy(rz, d).start()
    gs_copy(0, 0).start()
    combine(pending.pop())
    for rel in late:
        nrm_copy(*rel).start()
    b = dev(1, 0, 0)
    gy_copy(b).wait_recv()
    for rz in (1, 3, 2):
        gf_copy(rz, b).start()
    gs_copy(1, 0).start()

    def z_sum(yd):
        total = wq[core * N_T + yd * 4 + z].astype(F32)
        for rz in (1, 3, 2):
            src = lax.rem(z + 4 - rz, 4)
            remote(
                zr.at[yd, src], zr.at[yd, src], z_s.at[0], z_r.at[yd, src], dp=dev(0, rz, 0)
            ).wait_recv()
            total += zr[yd, src].astype(F32)
        return total

    other = lax.rem(y_hi + 1, 2)
    slot = core * N_T + other * 4 + z
    wq[slot] = z_sum(other).astype(BF16)
    y_copy = remote(wq.at[slot], yr, y_s, y_r, dp=dev(1, 0, 0))
    y_copy.start()
    ho[...] = z_sum(y_hi)

    for rz in (1, 3, 2):
        gz_copy(rz, dev(0, 4 - rz, 0)).wait_recv()
        gs_copy(0, rz).start()
    for rz in (1, 3, 2):
        gf_copy(rz, dev(1, 4 - rz, 0)).wait_recv()
        gs_copy(1, rz).start()
    y_copy.wait_recv()
    ho[...] += yr[...].astype(F32)

    for ry, rz, rc in early + late:
        src = dev(ry, 4 - rz, rc)
        r = (ry * 4 + rz) * 2 + rc
        remote(nrm_g.at[src], nrm_g.at[src], nrm_s.at[r], nrm_r.at[r], dp=src).wait_recv()
    for ry in range(2):
        for rz in range(4):
            b = dev(ry, 4 - rz, 1)
            remote(
                grd_g.at[b], grd_g.at[b], gs_s.at[ry, rz], gs_r.at[ry, rz], dp=dev(0, 0, 1)
            ).wait_recv()

    STEP = 4
    hq[...] = jnp.zeros_like(hq)
    hk[...] = jnp.zeros_like(hk)
    hv[...] = jnp.zeros_like(hv)

    @pl.loop(0, N_DP // STEP)
    def _(s):
        rows = pl.ds(s * STEP, STEP)
        lhs = nrm_g[rows].reshape(STEP * SEQ, C)
        rhs = grd_g[rows].reshape(STEP * SEQ, QW + 2 * HD)
        out = mm_tn(lhs, rhs)
        hq[...] += out[:, :QW]
        hk[...] += out[:, QW : QW + HD]
        hv[...] += out[:, QW + HD :]

    for rel in early + late:
        nrm_copy(*rel).wait_send()

    @pl.loop(0, N_T)
    def _(j):
        sib_copy(j, 0).wait_send()

        @pl.when(lax.rem(j, 4) != z)
        def _():
            z_copy(j).wait_send()

    for ry in range(2):
        for rz in range(4):
            gs_copy(ry, rz).wait_send()
    for dx in range(4):
        a1_copy(dx).wait_send()
        ay_copy(dx, t).wait_send()
    for dx in (1, 2, 3):
        b1_copy(0, dx).wait_send()
        b1_copy(1, dx).wait_send()
        a2_copy(dx).wait_send()
        ax_copy(dx, t).wait_send()
        bx_copy(dx, t).wait_send()
        bf_copy(dx, t).wait_send()
        gz_copy(dx, d).wait_send()
        gf_copy(dx, d).wait_send()
    gy_copy(d).wait_send()
    y_copy.wait_send()
    b2_copy().wait_send()
    by_copy(t).wait_send()


def tables():
    frequency = np.exp(
        np.float32(-math.log(10000.0)) * np.arange(HD // 2, dtype=np.float32) * np.float32(2.0)
        / np.float32(HD)
    ).astype(np.float32)
    angles = np.arange(SEQ, dtype=np.float32)[:, None] * frequency[None, :]
    cosine = np.cos(angles).astype(np.float32)
    sine = np.sin(angles).astype(np.float32)
    return np.concatenate([cosine, cosine], 1), np.concatenate([-sine, sine], 1)


def local(
    tokens, target, norm_gain, w_query, w_key, w_value, w_out, t_query, t_key, t_value, t_out
):
    cos_t, sin_t = tables()
    any_spec = pl.BlockSpec(memory_space=pl.ANY)
    vmem = pl.BlockSpec(memory_space=pltpu.VMEM)
    dma = pltpu.SemaphoreType.DMA
    block = (2 * SEQ, C)
    scratch = [
        pltpu.VMEM((SEQ, D), BF16),
        pltpu.VMEM((SEQ, 2 * C), BF16),
        pltpu.VMEM((N_DP, C, QW), BF16),
        pltpu.VMEM((N_DP, C, HD), BF16),
        pltpu.VMEM((N_DP, C, HD), BF16),
        pltpu.VMEM((N_DP, QW, C), BF16),
        pltpu.VMEM((N_DP, SEQ, C), BF16),
        pltpu.VMEM((N_DP, SEQ, C), BF16),
        pltpu.VMEM((2 * SEQ, QW), BF16),
        pltpu.VMEM((N_T, C, QW), BF16),
        pltpu.VMEM((2, 4, C, QW), BF16),
        pltpu.VMEM((C, QW), BF16),
        pltpu.VMEM((N_DP, SEQ, QW + 2 * HD), BF16),
        pltpu.VMEM((2, 4) + block, BF16),
        pltpu.VMEM((2, 4) + block, BF16),
        pltpu.VMEM((4,) + block, BF16),
        pltpu.VMEM((2, 4) + block, BF16),
        pltpu.VMEM((4,) + block, BF16),
        pltpu.VMEM(block, BF16),
        pltpu.VMEM((N_T,) + block, BF16),
        pltpu.VMEM((N_T,) + block, BF16),
        pltpu.VMEM((2 * SEQ, QW), F32),
        pltpu.VMEM((SEQ, QW + 2 * HD), F32),
        pltpu.VMEM((HEADS * SEQ, SEQ), F32),
        pltpu.VMEM((HEADS * SEQ, SEQ), F32),
        pltpu.VMEM((2 * HEADS * SEQ, HD), BF16),
        pltpu.VMEM((4, SEQ, HD), BF16),
        dma((2,)), dma((3, N_DP)), dma((N_DP,)),
        dma((N_DP,)), dma((N_DP,)), dma((N_T,)), dma((N_T,)), dma((N_T,)), dma((2, 4)), dma, dma,
        dma((4,)), dma((4,)), dma, dma, dma((4,)), dma((4,)), dma((2, 4)), dma((2, 4)),
        dma((4,)), dma((4,)), dma((2, 4)), dma((2, 4)), dma((4,)), dma((4,)), dma, dma,
        dma((4,)), dma((4,)), dma((4,)), dma((4,)),
        dma((4,)), dma((4,)), dma((4,)), dma((4,)), dma, dma,
    ]
    return pl.pallas_call(
        kernel,
        out_shape=(
            jax.ShapeDtypeStruct((C, QW), F32),
            jax.ShapeDtypeStruct((C, HD), F32),
            jax.ShapeDtypeStruct((C, HD), F32),
            jax.ShapeDtypeStruct((C, QW), F32),
        ),
        in_specs=[
            any_spec, any_spec, vmem, any_spec, any_spec, any_spec, any_spec,
            vmem, vmem, vmem, vmem, vmem, vmem,
        ],
        out_specs=(vmem, vmem, vmem, vmem),
        scratch_shapes=scratch,
        compiler_params=pltpu.CompilerParams(
            collective_id=0, has_side_effects=True, vmem_limit_bytes=62 * 1024 * 1024
        ),
        cost_estimate=pl.CostEstimate(
            flops=10_000_000_000, bytes_accessed=26_000_000, transcendentals=65536
        ),
        name="hvp",
    )(
        tokens, target, norm_gain.reshape(1, D), w_query, w_key, w_value, w_out,
        t_query.reshape(1, QW), t_key.reshape(1, HD), t_value.reshape(1, HD),
        t_out.reshape(1, D), jnp.asarray(cos_t), jnp.asarray(sin_t),
    )


def solution(mesh):
    return jax.shard_map(
        local,
        mesh=mesh,
        in_specs=(
            P("dp", None),
            P("dp", None),
            P(),
            P(None, "tensor"),
            P(None, "tensor"),
            P(None, "tensor"),
            P("tensor", None),
            P("tensor"),
            P("tensor"),
            P("tensor"),
            P(),
        ),
        out_specs=(P("dp", "tensor"), P("dp", "tensor"), P("dp", "tensor"), P("dp", "tensor")),
        check_vma=False,
    )
```

```python
import functools
import math

import jax
import jax.numpy as jnp
import numpy as np
from jax import lax
from jax.experimental import pallas as pl
from jax.experimental.pallas import tpu as pltpu
from jax.sharding import PartitionSpec as P

HD = 128
HEADS = 4
SEQ = 128
D = 8192
QW = HEADS * HD
N_DP = 16
N_T = 8
C = 512
EPS = 1e-05
F32 = jnp.float32
BF16 = jnp.bfloat16
MESH = pl.DeviceIdType.MESH


def mm(a, b):
    return lax.dot_general(
        a.astype(BF16), b.astype(BF16), (((1,), (0,)), ((), ())), preferred_element_type=F32
    )


def mm_nt(a, b):
    return lax.dot_general(
        a.astype(BF16), b.astype(BF16), (((1,), (1,)), ((), ())), preferred_element_type=F32
    )


def mm_tn(a, b):
    return lax.dot_general(
        a.astype(BF16), b.astype(BF16), (((0,), (0,)), ((), ())), preferred_element_type=F32
    )


def mm_nt_wide(a, b):
    a_hi = a.astype(BF16)
    b_hi = b.astype(BF16)
    a_lo = (a - a_hi.astype(F32)).astype(BF16)
    b_lo = (b - b_hi.astype(F32)).astype(BF16)
    return mm_nt(a_hi, b_hi) + (mm_nt(a_hi, b_lo) + mm_nt(a_lo, b_hi))


def swap_halves(x):
    return jnp.concatenate([x[:, HD // 2 :], x[:, : HD // 2]], axis=1)


def stack_heads(x):
    return jnp.concatenate([x[:, h * HD : (h + 1) * HD] for h in range(HEADS)], axis=0)


def kernel(
    tok_hbm, tgt_hbm, gain, wq_hbm, wk_hbm, wv_hbm, wo_hbm, tq, tk, tv, t_out, cos_t, sin_t,
    hq, hk, hv, ho,
    tok, tgt, wq, wk, wv, wo, nrm, nrm_g, att, sib, zf, zr, yr, grd_g,
    pa, pb, f0, v0, c0, f1, v1, c1, f2, v2, c2, r_a, r_b, g_acc, proj,
    prob, tprob, rot_q, kv,
    in_sem, wqkv_sem, wo_sem,
    nrm_s, nrm_r, sib_s, sib_r, z_s, z_r, y_s, y_r,
    gz_s, gz_r, gy_s, gy_r, gs_s, gs_r,
    s0_s, s0_r, s1_s, s1_r, s2_s, s2_r, g0_s, g0_r, g1_s, g1_r, g2_s, g2_r,
):
    d = lax.axis_index("dp")
    t = lax.axis_index("tensor")
    x = lax.rem(t, 4)
    y = t // 4
    core = lax.rem(d, 2)
    z = lax.rem(d // 2, 4)
    y_hi = d // 8

    def dev(ry, rz, rc):
        return (lax.rem(y_hi + ry, 2) * 4 + lax.rem(z + rz, 4)) * 2 + lax.rem(core + rc, 2)

    def at(dy, dx):
        return lax.rem(y + dy, 2) * 4 + lax.rem(x + dx, 4)

    def remote(src, dst, s_sem, r_sem, **where):
        return pltpu.make_async_remote_copy(
            src_ref=src, dst_ref=dst, send_sem=s_sem, recv_sem=r_sem,
            device_id=where, device_id_type=MESH,
        )

    tok_copy = pltpu.make_async_copy(tok_hbm, tok, in_sem.at[0])
    tok_copy.start()
    tgt_copy = pltpu.make_async_copy(
        tgt_hbm.at[:, pl.ds(pl.multiple_of(t * 2 * C, 2 * C), 2 * C)], tgt, in_sem.at[1]
    )

    def w_copies(c):
        rows = pl.ds(c * C, C)
        return (
            pltpu.make_async_copy(wq_hbm.at[rows, :], wq.at[c], wqkv_sem.at[0, c]),
            pltpu.make_async_copy(wk_hbm.at[rows, :], wk.at[c], wqkv_sem.at[1, c]),
            pltpu.make_async_copy(wv_hbm.at[rows, :], wv.at[c], wqkv_sem.at[2, c]),
        )

    def wo_copy(c):
        return pltpu.make_async_copy(
            wo_hbm.at[:, pl.ds(pl.multiple_of(c * C, C), C)], wo.at[c], wo_sem.at[c]
        )

    @pl.loop(0, N_DP)
    def _(c):
        for cp in w_copies(c):
            cp.start()

    tgt_copy.start()

    @pl.loop(0, N_DP)
    def _(c):
        wo_copy(c).start()

    bar = pltpu.get_barrier_semaphore()

    @pl.loop(1, N_DP)
    def _(r):
        pl.semaphore_signal(
            bar, inc=1, device_id={"dp": lax.rem(d + r, N_DP)}, device_id_type=MESH
        )

    for dy, dx in ((1, 0), (0, 1), (0, 2), (0, 3)):
        pl.semaphore_signal(bar, inc=1, device_id={"tensor": at(dy, dx)}, device_id_type=MESH)

    tok_copy.wait()

    def square_step(c, acc):
        v = tok[:, pl.ds(pl.multiple_of(c * C, C), C)].astype(F32)
        return acc + v * v

    squares = lax.fori_loop(0, N_DP, square_step, jnp.zeros((SEQ, C), F32))
    inv = lax.rsqrt(jnp.sum(squares, axis=1, keepdims=True) * (1.0 / D) + EPS)

    @pl.loop(0, N_DP)
    def _(c):
        cols = pl.ds(pl.multiple_of(c * C, C), C)
        nrm[c] = (tok[:, cols].astype(F32) * inv * gain[:, cols]).astype(BF16)

    nrm_g[d] = nrm[d]

    pl.semaphore_wait(bar, N_DP - 1 + 4)

    def nrm_copy(ry, rz, rc):
        dest = dev(ry, rz, rc)
        r = (ry * 4 + rz) * 2 + rc
        return remote(nrm.at[dest], nrm_g.at[d], nrm_s.at[r], nrm_r.at[r], dp=dest)

    early = [(0, rz, rc) for rz in (1, 3, 2) for rc in (0, 1)] + [(0, 0, 1)]
    crossing = [[(1, rz, rc) for rc in (0, 1)] for rz in (2, 1, 3, 0)]
    everyone = early + sum(crossing, [])

    def nrm_cross(i):
        for rel in crossing[i]:
            nrm_copy(*rel).start()

    for rel in early:
        nrm_copy(*rel).start()
    nrm_cross(0)

    proj[...] = jnp.zeros_like(proj)

    @pl.loop(0, N_DP)
    def _(c):
        for cp in w_copies(c):
            cp.wait()
        lhs = nrm[c]
        proj[:, :QW] += mm(lhs, wq[c])
        proj[:, QW : QW + HD] += mm(lhs, wk[c])
        proj[:, QW + HD :] += mm(lhs, wv[c])

    cos1 = cos_t[...]
    sin1 = sin_t[...]
    cos4 = jnp.concatenate([cos1] * HEADS, axis=0)
    sin4 = jnp.concatenate([sin1] * HEADS, axis=0)
    scale = 1.0 / math.sqrt(HD)

    q2 = proj[:, :QW]
    key = proj[:, QW : QW + HD]
    val = proj[:, QW + HD :]
    tval = val * tv[...]
    qs = stack_heads(q2)
    tqs = stack_heads(q2 * tq[...])
    rq = qs * cos4 + swap_halves(qs) * sin4
    trq = tqs * cos4 + swap_halves(tqs) * sin4
    tkey = key * tk[...]
    rk = key * cos1 + swap_halves(key) * sin1
    trk = tkey * cos1 + swap_halves(tkey) * sin1
    rot_q[...] = jnp.concatenate([rq.astype(BF16), trq.astype(BF16)], axis=0)
    kv[0] = rk.astype(BF16)
    kv[1] = trk.astype(BF16)
    kv[2] = val.astype(BF16)
    kv[3] = tval.astype(BF16)
    scores = mm_nt_wide(rq, rk) * scale
    tscores = (mm_nt_wide(trq, rk) + mm_nt_wide(rq, trk)) * scale
    row = lax.rem(lax.broadcasted_iota(jnp.int32, (HEADS * SEQ, SEQ), 0), SEQ)
    col = lax.broadcasted_iota(jnp.int32, (HEADS * SEQ, SEQ), 1)
    scores = jnp.where(row >= col, scores, -1e30)
    e = jnp.exp(scores - jnp.max(scores, axis=1, keepdims=True))
    p = e / jnp.sum(e, axis=1, keepdims=True)
    tp = p * (tscores - jnp.sum(p * tscores, axis=1, keepdims=True))
    prob[...] = p
    tprob[...] = tp
    o = mm(p, val)
    to = mm(tp, val) + mm(p, tval)
    for h in range(HEADS):
        att[:SEQ, h * HD : (h + 1) * HD] = to[h * SEQ : (h + 1) * SEQ].astype(BF16)
        att[SEQ:, h * HD : (h + 1) * HD] = o[h * SEQ : (h + 1) * SEQ].astype(BF16)

    @pl.loop(0, N_DP)
    def _(c):
        wo_copy(c).wait()

    def t_cols(c):
        return t_out[:, pl.ds(pl.multiple_of(c * C, C), C)]

    def part(dy, dx, half, dst):
        c = at(dy, dx) * 2 + half
        rows = mm(att[...], wo[c])
        dst[dy, dx, :SEQ, :] = rows[SEQ:].astype(BF16)
        dst[dy, dx, SEQ:, :] = (rows[:SEQ] + rows[SEQ:] * t_cols(c)).astype(BF16)

    class Stream:
        def __init__(self, buf, r0, n, half_in, full_in, across, s, r, out, g_s, g_r):
            self.buf, self.r0, self.n, self.h = buf, r0, n, n // 2
            self.half_in, self.full_in, self.across = half_in, full_in, across
            self.s, self.r, self.out, self.g_s, self.g_r = s, r, out, g_s, g_r

        def ring(self, dy, k):
            h = self.h
            dx, upper, step = ((2, 0, 1), (2, 1, 3), (1, 1, 1), (3, 0, 3), (1, 0, 1), (3, 1, 3))[k]
            src = self.buf.at[dy, dx, pl.ds(self.r0 + upper * h, h)]
            side = 0 if step == 1 else 1
            dst = self.half_in.at[dy, side] if k < 2 else self.full_in.at[dy, side, pl.ds(upper * h, h)]
            return remote(src, dst, self.s.at[dy, k], self.r.at[dy, k], tensor=at(0, step))

        def cross(self, dx):
            rows = pl.ds(self.r0, self.n)
            return remote(
                self.buf.at[1, dx, rows], self.across.at[dx], self.s.at[2, dx], self.r.at[2, dx],
                tensor=at(1, 0),
            )

        def add(self, dy, dx, upper, value):
            lo = self.r0 + upper * self.h
            rows = slice(lo, lo + value.shape[0])
            self.buf[dy, dx, rows] = (self.buf[dy, dx, rows].astype(F32) + value.astype(F32)).astype(BF16)

        def relay(self, dy):
            self.ring(dy, 0).wait_recv()
            self.add(dy, 1, 0, self.half_in[dy, 0])
            self.ring(dy, 4).start()
            self.ring(dy, 1).wait_recv()
            self.add(dy, 3, 1, self.half_in[dy, 1])
            self.ring(dy, 5).start()

        def row_sum(self, dy):
            for k in (2, 3, 4, 5):
                self.ring(dy, k).wait_recv()
            own = self.buf[dy, 0, self.r0 : self.r0 + self.n].astype(F32)
            return own + self.full_in[dy, 0].astype(F32) + self.full_in[dy, 1].astype(F32)

        def gather(self, k, sender=True):
            sent = (t, t, t, at(0, 3), at(0, 1)) + (
                (at(0, 3), at(0, 1), at(0, 2)) if self.r0 == 0 and self.n == SEQ
                else (at(1, 0), at(1, 0), at(1, 3), at(1, 1))
            )
            came = (at(1, 0), at(0, 3), at(0, 1), at(0, 2), at(0, 2)) + (
                (at(1, 3), at(1, 1), at(1, 2)) if self.r0 == 0 and self.n == SEQ
                else (at(1, 3), at(1, 1), at(1, 2), at(1, 2))
            )
            first_y = not (self.r0 == 0 and self.n == SEQ)
            to = (at(1, 0), at(0, 1), at(0, 3), at(0, 1), at(0, 3)) + (
                (at(0, 1), at(0, 3), at(0, 1), at(0, 3)) if first_y else (at(1, 0),) * 3
            )
            j = sent[k] if sender else came[k]
            lo, n = self.r0, self.n
            if k == 3 or (k == 7 and first_y):
                n = self.h
            if k == 4 or (k == 8 and first_y):
                lo, n = lo + self.h, self.h
            ref = self.out.at[j, pl.ds(lo, n)]
            return remote(ref, ref, self.g_s.at[k], self.g_r.at[k], tensor=to[k])

        def came(self, *ks):
            for k in ks:
                self.gather(k, False).wait_recv()

    s0 = Stream(pa, 0, SEQ, f0, v0, c0, s0_s, s0_r, r_a, g0_s, g0_r)
    s1 = Stream(pa, SEQ, SEQ, f1, v1, c1, s1_s, s1_r, r_a, g1_s, g1_r)
    s2 = Stream(pb, 0, 2 * SEQ, f2, v2, c2, s2_s, s2_r, r_b, g2_s, g2_r)
    x_first = (s2, s1)

    for dx, ks in ((2, (0, 1)), (1, (2,)), (3, (3,))):
        part(1, dx, 1, pb)
        for k in ks:
            s2.ring(1, k).start()
        part(1, dx, 0, pa)
        for k in ks:
            s1.ring(1, k).start()
        s0.cross(dx).start()
    part(0, 2, 1, pb)
    part(0, 2, 0, pa)
    for st in x_first:
        st.ring(0, 0).start()
        st.ring(0, 1).start()
    part(1, 0, 0, pa)
    s0.cross(0).start()
    for dx in (1, 3):
        part(0, dx, 1, pb)
        part(0, dx, 0, pa)
    part(1, 0, 1, pb)
    part(0, 0, 1, pb)
    part(0, 0, 0, pa)
    for st in x_first:
        st.relay(1)
    for st in x_first:
        st.ring(0, 2).start()
        st.ring(0, 3).start()
    for dx, ks in ((2, (0, 1)), (1, (2,)), (3, (3,))):
        s0.cross(dx).wait_recv()
        s0.add(0, dx, 0, s0.across[dx])
        for k in ks:
            s0.ring(0, k).start()
    nrm_cross(1)
    for st in x_first:
        st.relay(0)
    for st in x_first:
        st.buf[1, 0, st.r0 : st.r0 + st.n] = st.row_sum(1).astype(BF16)
        st.cross(0).start()
    s0.relay(0)

    tgt_copy.wait()

    def residual(total, half, dst):
        c = t * 2 + half
        base = tok[:, pl.ds(pl.multiple_of(c * C, C), C)].astype(F32)
        aim = tgt[:, half * C : (half + 1) * C].astype(F32)
        dst[t, :SEQ, :] = (base + total - aim).astype(BF16)

    def block_sum(st):
        total = st.row_sum(0)
        st.cross(0).wait_recv()
        return total + st.across[0].astype(F32)

    total = block_sum(s2)
    residual(total[:SEQ], 1, r_b)
    r_b[t, SEQ:, :] = total[SEQ:].astype(BF16)
    for k in (0, 1, 2):
        s2.gather(k).start()
    r_a[t, SEQ:, :] = block_sum(s1).astype(BF16)
    for k in (0, 1, 2):
        s1.gather(k).start()
    residual(block_sum(s0), 0, r_a)
    for k in (1, 2, 0):
        s0.gather(k).start()

    def sib_copy(j, half):
        return remote(wq.at[half * N_T + j], sib.at[j], sib_s.at[j], sib_r.at[j], dp=dev(0, 0, 1))

    def use(j, half):
        src = (r_a, r_b)[half]
        rows = src[j]
        wq[half * N_T + j] = mm_tn(rows, att[...]).astype(BF16)

        @pl.when(core != half)
        def _():
            sib_copy(j, half).start()

        c = 2 * j + half
        first = rows[:SEQ]
        second = (rows[SEQ:].astype(F32) + first.astype(F32) * t_cols(c)).astype(BF16)
        g_acc[...] += mm_nt(jnp.concatenate([first, second], axis=0), wo[c])

    def z_copy(j, k):
        rel, upper, step = ((2, 0, 1), (2, 1, 3), (1, 1, 1), (3, 0, 3), (1, 0, 1), (3, 1, 3))[k]
        yd = j // 4
        rows = pl.ds(upper * (C // 2), C // 2)
        side = 0 if step == 1 else 1
        dst = zf.at[yd, side] if k < 2 else zr.at[yd, side, rows]
        return remote(
            wq.at[core * N_T + j, rows], dst, z_s.at[yd, k], z_r.at[yd, k], dp=dev(0, step, 0)
        )

    def z_rel(j):
        return lax.rem(lax.rem(j, 4) + 4 - z, 4)

    def combine(j):
        slot = core * N_T + j
        sib_copy(j, 0).wait_recv()
        wq[slot] = (wq[slot].astype(F32) + sib[j].astype(F32)).astype(BF16)

        @pl.when(z_rel(j) == 2)
        def _():
            z_copy(j, 0).start()
            z_copy(j, 1).start()

        @pl.when(z_rel(j) == 1)
        def _():
            z_copy(j, 2).start()

        @pl.when(z_rel(j) == 3)
        def _():
            z_copy(j, 3).start()

    def z_relay(j):
        slot = core * N_T + j
        half = C // 2

        @pl.when(z_rel(j) == 1)
        def _():
            z_copy(j, 0).wait_recv()
            wq[slot, :half] = (wq[slot, :half].astype(F32) + zf[j // 4, 0].astype(F32)).astype(BF16)
            z_copy(j, 4).start()

        @pl.when(z_rel(j) == 3)
        def _():
            z_copy(j, 1).wait_recv()
            wq[slot, half:] = (wq[slot, half:].astype(F32) + zf[j // 4, 1].astype(F32)).astype(BF16)
            z_copy(j, 5).start()

    g_acc[...] = jnp.zeros_like(g_acc)
    use(t, 1)
    use(t, 0)
    combine(t)
    for k in (1, 2):
        for st in x_first:
            st.came(k)
            st.gather(k + 2).start()
        s0.came(k)
        s0.gather(k + 2).start()
        s0.gather(k + 4).start()
    use(at(0, 3), 1)
    z_relay(t)
    use(at(0, 3), 0)
    use(at(0, 1), 1)
    use(at(0, 1), 0)
    for st in x_first:
        st.came(0)
    use(at(1, 0), 1)
    s0.came(0)
    use(at(1, 0), 0)
    for st in x_first:
        st.gather(5).start()
        st.gather(6).start()
    nrm_cross(2)
    combine(at(0, 3))
    combine(at(0, 1))
    combine(at(1, 0))
    for st in x_first:
        st.came(3, 4)
    s0.came(3, 4)
    s0.gather(7).start()
    use(at(0, 2), 1)
    use(at(0, 2), 0)
    z_relay(at(0, 3))
    z_relay(at(0, 1))
    combine(at(0, 2))
    for k in (5, 6):
        for st in x_first:
            st.came(k)
            st.gather(k + 2).start()
    for k, j in ((5, at(1, 3)), (6, at(1, 1))):
        use(j, 1)
        s0.came(k)
        use(j, 0)
    z_relay(at(1, 0))
    combine(at(1, 3))
    combine(at(1, 1))
    nrm_cross(3)
    for st in x_first:
        st.came(7, 8)
    s0.came(7)
    use(at(1, 2), 1)
    use(at(1, 2), 0)

    key = kv[0]
    tkey = kv[1]
    val = kv[2]
    tval = kv[3]
    g1 = stack_heads(g_acc[:SEQ]).astype(BF16)
    g2 = stack_heads(g_acc[SEQ:]).astype(BF16)
    p = prob[...]
    tp = tprob[...]
    dpr = mm_nt(g1, val)
    tdpr = mm_nt(g2, val) + mm_nt(g1, tval)
    tval_grad = mm_tn(jnp.concatenate([tp, p], axis=0), jnp.concatenate([g1, g2], axis=0))
    grd_g[d, :, QW + HD :] = tval_grad.astype(BF16)
    dpr = dpr - jnp.sum(p * dpr, axis=1, keepdims=True)
    tdpr = tdpr - jnp.sum(tp * dpr + p * tdpr, axis=1, keepdims=True)
    ds = (p * dpr).astype(BF16)
    tds = (tp * dpr + p * tdpr).astype(BF16)
    both = jnp.concatenate([tds, ds], axis=0)
    trk_grad = mm_tn(both, rot_q[...]) * scale
    trk_grad = trk_grad * cos1 - swap_halves(trk_grad) * sin1
    grd_g[d, :, QW : QW + HD] = trk_grad.astype(BF16)
    trq_grad = (mm(tds, key) + mm(ds, tkey)) * scale
    trq_grad = trq_grad * cos4 - swap_halves(trq_grad) * sin4
    for h in range(HEADS):
        grd_g[d, :, h * HD : (h + 1) * HD] = trq_grad[h * SEQ : (h + 1) * SEQ].astype(BF16)

    def gs_copy(ry, rz):
        b = dev(ry, 4 - rz, 0)
        return remote(
            grd_g.at[b], grd_g.at[b], gs_s.at[ry, rz], gs_r.at[ry, rz], dp=dev(0, 0, 1)
        )

    def gz_copy(ry, k, sender=True):
        step = (1, 3, 1, 3)[k]
        back = (0, 0, 1, 1)[k] if sender else (1, 1, 2, 2)[k]
        b = dev(ry, 4 - back if step == 1 else back, 0)
        h = SEQ // 2
        rows = (pl.ds(0, SEQ), pl.ds(0, SEQ), pl.ds(0, h), pl.ds(h, h))[k]
        ref = grd_g.at[b, rows]
        return remote(ref, ref, gz_s.at[ry, k], gz_r.at[ry, k], dp=dev(0, step, 0))

    def gy_copy(b):
        return remote(grd_g.at[b], grd_g.at[b], gy_s, gy_r, dp=dev(1, 0, 0))

    gy_copy(d).start()
    gz_copy(0, 0).start()
    gz_copy(0, 1).start()
    gs_copy(0, 0).start()
    combine(at(1, 2))
    z_relay(at(0, 2))
    gy_copy(dev(1, 0, 0)).wait_recv()
    gz_copy(1, 0).start()
    gz_copy(1, 1).start()
    gs_copy(1, 0).start()
    for ry in range(2):
        for k, rz in ((0, 1), (1, 3)):
            gz_copy(ry, k, False).wait_recv()
            gz_copy(ry, k + 2).start()
            gs_copy(ry, rz).start()
        if ry == 0:
            z_relay(at(1, 3))
            z_relay(at(1, 1))
            z_relay(at(1, 2))

    def z_sum(yd, upper):
        rows = slice(upper * (C // 2), (upper + 1) * (C // 2))
        for k in ((3, 4), (2, 5))[upper]:
            z_copy(yd * 4, k).wait_recv()
        total = wq[core * N_T + yd * 4 + z, rows].astype(F32)
        return total + zr[yd, 0, rows].astype(F32) + zr[yd, 1, rows].astype(F32)

    def y_copy(upper):
        rows = pl.ds(upper * (C // 2), C // 2)
        return remote(
            wq.at[core * N_T + other * 4 + z, rows], yr.at[rows], y_s.at[upper], y_r.at[upper],
            dp=dev(1, 0, 0),
        )

    other = lax.rem(y_hi + 1, 2)
    for upper in range(2):
        rows = slice(upper * (C // 2), (upper + 1) * (C // 2))
        wq[core * N_T + other * 4 + z, rows] = z_sum(other, upper).astype(BF16)
        y_copy(upper).start()
    for upper in range(2):
        ho[upper * (C // 2) : (upper + 1) * (C // 2), :] = z_sum(y_hi, upper)

    for ry in range(2):
        gz_copy(ry, 2, False).wait_recv()
        gz_copy(ry, 3, False).wait_recv()
        gs_copy(ry, 2).start()
    for upper in range(2):
        y_copy(upper).wait_recv()
    ho[...] += yr[...].astype(F32)

    for ry, rz, rc in everyone:
        src = dev(ry, 4 - rz, rc)
        r = (ry * 4 + rz) * 2 + rc
        remote(nrm_g.at[src], nrm_g.at[src], nrm_s.at[r], nrm_r.at[r], dp=src).wait_recv()
    for ry in range(2):
        for rz in range(4):
            b = dev(ry, 4 - rz, 1)
            remote(
                grd_g.at[b], grd_g.at[b], gs_s.at[ry, rz], gs_r.at[ry, rz], dp=dev(0, 0, 1)
            ).wait_recv()

    def product(first):
        rows = pl.ds(first * N_T, N_T)
        lhs = nrm_g[rows].reshape(N_T * SEQ, C)
        rhs = grd_g[rows].reshape(N_T * SEQ, QW + 2 * HD)
        return mm_tn(lhs, rhs)

    out = product(0) + product(1)
    hq[...] = out[:, :QW]
    hk[...] = out[:, QW : QW + HD]
    hv[...] = out[:, QW + HD :]

    for rel in everyone:
        nrm_copy(*rel).wait_send()

    @pl.loop(0, N_T)
    def _(j):
        sib_copy(j, 0).wait_send()

    for yd in range(2):
        for k in range(6):
            z_copy(yd * 4, k).wait_send()
        for k in range(4):
            gz_copy(yd, k).wait_send()
        for rz in range(4):
            gs_copy(yd, rz).wait_send()
        y_copy(yd).wait_send()
    gy_copy(d).wait_send()
    for st in x_first:
        for k in range(6):
            st.ring(0, k).wait_send()
            st.ring(1, k).wait_send()
        st.cross(0).wait_send()
        for k in range(9):
            st.gather(k).wait_send()
    for k in range(6):
        s0.ring(0, k).wait_send()
    for dx in range(4):
        s0.cross(dx).wait_send()
    for k in range(8):
        s0.gather(k).wait_send()


def tables():
    frequency = np.exp(
        np.float32(-math.log(10000.0)) * np.arange(HD // 2, dtype=np.float32) * np.float32(2.0)
        / np.float32(HD)
    ).astype(np.float32)
    angles = np.arange(SEQ, dtype=np.float32)[:, None] * frequency[None, :]
    cosine = np.cos(angles).astype(np.float32)
    sine = np.sin(angles).astype(np.float32)
    return np.concatenate([cosine, cosine], 1), np.concatenate([-sine, sine], 1)


def local(
    tokens, target, norm_gain, w_query, w_key, w_value, w_out, t_query, t_key, t_value, t_out
):
    cos_t, sin_t = tables()
    any_spec = pl.BlockSpec(memory_space=pl.ANY)
    vmem = pl.BlockSpec(memory_space=pltpu.VMEM)
    dma = pltpu.SemaphoreType.DMA
    block = (2 * SEQ, C)
    scratch = [
        pltpu.VMEM((SEQ, D), BF16),
        pltpu.VMEM((SEQ, 2 * C), BF16),
        pltpu.VMEM((N_DP, C, QW), BF16),
        pltpu.VMEM((N_DP, C, HD), BF16),
        pltpu.VMEM((N_DP, C, HD), BF16),
        pltpu.VMEM((N_DP, QW, C), BF16),
        pltpu.VMEM((N_DP, SEQ, C), BF16),
        pltpu.VMEM((N_DP, SEQ, C), BF16),
        pltpu.VMEM((2 * SEQ, QW), BF16),
        pltpu.VMEM((N_T, C, QW), BF16),
        pltpu.VMEM((2, 2, C // 2, QW), BF16),
        pltpu.VMEM((2, 2, C, QW), BF16),
        pltpu.VMEM((C, QW), BF16),
        pltpu.VMEM((N_DP, SEQ, QW + 2 * HD), BF16),
        pltpu.VMEM((2, 4) + block, BF16),
        pltpu.VMEM((2, 4) + block, BF16),
        pltpu.VMEM((1, 2, SEQ // 2, C), BF16),
        pltpu.VMEM((1, 2, SEQ, C), BF16),
        pltpu.VMEM((4, SEQ, C), BF16),
        pltpu.VMEM((2, 2, SEQ // 2, C), BF16),
        pltpu.VMEM((2, 2, SEQ, C), BF16),
        pltpu.VMEM((1, SEQ, C), BF16),
        pltpu.VMEM((2, 2, SEQ, C), BF16),
        pltpu.VMEM((2, 2, 2 * SEQ, C), BF16),
        pltpu.VMEM((1, 2 * SEQ, C), BF16),
        pltpu.VMEM((N_T,) + block, BF16),
        pltpu.VMEM((N_T,) + block, BF16),
        pltpu.VMEM((2 * SEQ, QW), F32),
        pltpu.VMEM((SEQ, QW + 2 * HD), F32),
        pltpu.VMEM((HEADS * SEQ, SEQ), F32),
        pltpu.VMEM((HEADS * SEQ, SEQ), F32),
        pltpu.VMEM((2 * HEADS * SEQ, HD), BF16),
        pltpu.VMEM((4, SEQ, HD), BF16),
        dma((2,)), dma((3, N_DP)), dma((N_DP,)),
        dma((N_DP,)), dma((N_DP,)), dma((N_T,)), dma((N_T,)), dma((2, 6)), dma((2, 6)),
        dma((2,)), dma((2,)), dma((2, 4)), dma((2, 4)), dma, dma, dma((2, 4)), dma((2, 4)),
        dma((3, 6)), dma((3, 6)), dma((3, 6)), dma((3, 6)), dma((3, 6)), dma((3, 6)),
        dma((9,)), dma((9,)), dma((9,)), dma((9,)), dma((9,)), dma((9,)),
    ]
    return pl.pallas_call(
        kernel,
        out_shape=(
            jax.ShapeDtypeStruct((C, QW), F32),
            jax.ShapeDtypeStruct((C, HD), F32),
            jax.ShapeDtypeStruct((C, HD), F32),
            jax.ShapeDtypeStruct((C, QW), F32),
        ),
        in_specs=[
            any_spec, any_spec, vmem, any_spec, any_spec, any_spec, any_spec,
            vmem, vmem, vmem, vmem, vmem, vmem,
        ],
        out_specs=(vmem, vmem, vmem, vmem),
        scratch_shapes=scratch,
        compiler_params=pltpu.CompilerParams(
            collective_id=0, has_side_effects=True, vmem_limit_bytes=62 * 1024 * 1024
        ),
        cost_estimate=pl.CostEstimate(
            flops=10_000_000_000, bytes_accessed=26_000_000, transcendentals=65536
        ),
        name="hvp",
    )(
        tokens, target, norm_gain.reshape(1, D), w_query, w_key, w_value, w_out,
        t_query.reshape(1, QW), t_key.reshape(1, HD), t_value.reshape(1, HD),
        t_out.reshape(1, D), jnp.asarray(cos_t), jnp.asarray(sin_t),
    )


def solution(mesh):
    return jax.shard_map(
        local,
        mesh=mesh,
        in_specs=(
            P("dp", None),
            P("dp", None),
            P(),
            P(None, "tensor"),
            P(None, "tensor"),
            P(None, "tensor"),
            P("tensor", None),
            P("tensor"),
            P("tensor"),
            P("tensor"),
            P(),
        ),
        out_specs=(P("dp", "tensor"), P("dp", "tensor"), P("dp", "tensor"), P("dp", "tensor")),
        check_vma=False,
    )
```

```python
import functools
import math

import jax
import jax.numpy as jnp
import numpy as np
from jax import lax
from jax.experimental import pallas as pl
from jax.experimental.pallas import tpu as pltpu
from jax.sharding import PartitionSpec as P

HD = 128
HEADS = 4
SEQ = 128
D = 8192
QW = HEADS * HD
N_DP = 16
N_T = 8
C = 512
EPS = 1e-05
F32 = jnp.float32
BF16 = jnp.bfloat16
MESH = pl.DeviceIdType.MESH


def mm(a, b):
    return lax.dot_general(
        a.astype(BF16), b.astype(BF16), (((1,), (0,)), ((), ())), preferred_element_type=F32
    )


def mm_nt(a, b):
    return lax.dot_general(
        a.astype(BF16), b.astype(BF16), (((1,), (1,)), ((), ())), preferred_element_type=F32
    )


def mm_tn(a, b):
    return lax.dot_general(
        a.astype(BF16), b.astype(BF16), (((0,), (0,)), ((), ())), preferred_element_type=F32
    )


def mm_nt_wide(a, b):
    a_hi = a.astype(BF16)
    b_hi = b.astype(BF16)
    a_lo = (a - a_hi.astype(F32)).astype(BF16)
    b_lo = (b - b_hi.astype(F32)).astype(BF16)
    return mm_nt(a_hi, b_hi) + (mm_nt(a_hi, b_lo) + mm_nt(a_lo, b_hi))


def swap_halves(x):
    return jnp.concatenate([x[:, HD // 2 :], x[:, : HD // 2]], axis=1)


def stack_heads(x):
    return jnp.concatenate([x[:, h * HD : (h + 1) * HD] for h in range(HEADS)], axis=0)


def kernel(
    tok_hbm, tgt_hbm, gain, wq_hbm, wk_hbm, wv_hbm, wo_hbm, tq, tk, tv, t_out, cos_t, sin_t,
    hq, hk, hv, ho,
    tok, tgt, wq, wk, wv, wo, nrm, nrm_g, att, sib, zf, zr, yr, grd_g,
    pq, pf, pv, pc, r_all, g_acc, proj,
    prob, tprob, rot_q, kv,
    in_sem, wqkv_sem, wo_sem,
    nrm_s, nrm_r, sib_s, sib_r, z_s, z_r, y_s, y_r,
    gz_s, gz_r, gy_s, gy_r, gs_s, gs_r,
    rs_s, rs_r, cr_s, cr_r, ga_s, ga_r,
):
    d = lax.axis_index("dp")
    t = lax.axis_index("tensor")
    x = lax.rem(t, 4)
    y = t // 4
    core = lax.rem(d, 2)
    z = lax.rem(d // 2, 4)
    y_hi = d // 8

    def dev(ry, rz, rc):
        return (lax.rem(y_hi + ry, 2) * 4 + lax.rem(z + rz, 4)) * 2 + lax.rem(core + rc, 2)

    def at(dy, dx):
        return lax.rem(y + dy, 2) * 4 + lax.rem(x + dx, 4)

    def remote(src, dst, s_sem, r_sem, **where):
        return pltpu.make_async_remote_copy(
            src_ref=src, dst_ref=dst, send_sem=s_sem, recv_sem=r_sem,
            device_id=where, device_id_type=MESH,
        )

    tok_copy = pltpu.make_async_copy(tok_hbm, tok, in_sem.at[0])
    tok_copy.start()
    tgt_copy = pltpu.make_async_copy(
        tgt_hbm.at[:, pl.ds(pl.multiple_of(t * 2 * C, 2 * C), 2 * C)], tgt, in_sem.at[1]
    )

    def w_copies(c):
        rows = pl.ds(c * C, C)
        return (
            pltpu.make_async_copy(wq_hbm.at[rows, :], wq.at[c], wqkv_sem.at[0, c]),
            pltpu.make_async_copy(wk_hbm.at[rows, :], wk.at[c], wqkv_sem.at[1, c]),
            pltpu.make_async_copy(wv_hbm.at[rows, :], wv.at[c], wqkv_sem.at[2, c]),
        )

    def wo_copy(c):
        return pltpu.make_async_copy(
            wo_hbm.at[:, pl.ds(pl.multiple_of(c * C, C), C)], wo.at[c], wo_sem.at[c]
        )

    @pl.loop(0, N_DP)
    def _(c):
        for cp in w_copies(c):
            cp.start()

    tgt_copy.start()

    @pl.loop(0, N_DP)
    def _(c):
        wo_copy(c).start()

    bar = pltpu.get_barrier_semaphore()

    @pl.loop(1, N_DP)
    def _(r):
        pl.semaphore_signal(
            bar, inc=1, device_id={"dp": lax.rem(d + r, N_DP)}, device_id_type=MESH
        )

    for dy, dx in ((1, 0), (0, 1), (0, 2), (0, 3)):
        pl.semaphore_signal(bar, inc=1, device_id={"tensor": at(dy, dx)}, device_id_type=MESH)

    tok_copy.wait()

    def square_step(c, acc):
        v = tok[:, pl.ds(pl.multiple_of(c * C, C), C)].astype(F32)
        return acc + v * v

    squares = lax.fori_loop(0, N_DP, square_step, jnp.zeros((SEQ, C), F32))
    inv = lax.rsqrt(jnp.sum(squares, axis=1, keepdims=True) * (1.0 / D) + EPS)

    @pl.loop(0, N_DP)
    def _(c):
        cols = pl.ds(pl.multiple_of(c * C, C), C)
        nrm[c] = (tok[:, cols].astype(F32) * inv * gain[:, cols]).astype(BF16)

    nrm_g[d] = nrm[d]

    pl.semaphore_wait(bar, N_DP - 1 + 4)

    def nrm_copy(ry, rz, rc):
        dest = dev(ry, rz, rc)
        r = (ry * 4 + rz) * 2 + rc
        return remote(nrm.at[dest], nrm_g.at[d], nrm_s.at[r], nrm_r.at[r], dp=dest)

    early = [(0, rz, rc) for rz in (1, 3, 2) for rc in (0, 1)] + [(0, 0, 1)]
    crossing = [[(1, rz, rc) for rc in (0, 1)] for rz in (2, 1, 3, 0)]
    everyone = early + sum(crossing, [])

    def nrm_cross(i):
        for rel in crossing[i]:
            nrm_copy(*rel).start()

    for rel in early:
        nrm_copy(*rel).start()
    nrm_cross(0)

    proj[...] = jnp.zeros_like(proj)

    @pl.loop(0, N_DP)
    def _(c):
        for cp in w_copies(c):
            cp.wait()
        lhs = nrm[c]
        proj[:, :QW] += mm(lhs, wq[c])
        proj[:, QW : QW + HD] += mm(lhs, wk[c])
        proj[:, QW + HD :] += mm(lhs, wv[c])

    cos1 = cos_t[...]
    sin1 = sin_t[...]
    cos4 = jnp.concatenate([cos1] * HEADS, axis=0)
    sin4 = jnp.concatenate([sin1] * HEADS, axis=0)
    scale = 1.0 / math.sqrt(HD)

    q2 = proj[:, :QW]
    key = proj[:, QW : QW + HD]
    val = proj[:, QW + HD :]
    tval = val * tv[...]
    qs = stack_heads(q2)
    tqs = stack_heads(q2 * tq[...])
    rq = qs * cos4 + swap_halves(qs) * sin4
    trq = tqs * cos4 + swap_halves(tqs) * sin4
    tkey = key * tk[...]
    rk = key * cos1 + swap_halves(key) * sin1
    trk = tkey * cos1 + swap_halves(tkey) * sin1
    rot_q[...] = jnp.concatenate([rq.astype(BF16), trq.astype(BF16)], axis=0)
    kv[0] = rk.astype(BF16)
    kv[1] = trk.astype(BF16)
    kv[2] = val.astype(BF16)
    kv[3] = tval.astype(BF16)
    scores = mm_nt_wide(rq, rk) * scale
    tscores = (mm_nt_wide(trq, rk) + mm_nt_wide(rq, trk)) * scale
    row = lax.rem(lax.broadcasted_iota(jnp.int32, (HEADS * SEQ, SEQ), 0), SEQ)
    col = lax.broadcasted_iota(jnp.int32, (HEADS * SEQ, SEQ), 1)
    scores = jnp.where(row >= col, scores, -1e30)
    e = jnp.exp(scores - jnp.max(scores, axis=1, keepdims=True))
    p = e / jnp.sum(e, axis=1, keepdims=True)
    tp = p * (tscores - jnp.sum(p * tscores, axis=1, keepdims=True))
    prob[...] = p
    tprob[...] = tp
    o = mm(p, val)
    to = mm(tp, val) + mm(p, tval)
    for h in range(HEADS):
        att[:SEQ, h * HD : (h + 1) * HD] = to[h * SEQ : (h + 1) * SEQ].astype(BF16)
        att[SEQ:, h * HD : (h + 1) * HD] = o[h * SEQ : (h + 1) * SEQ].astype(BF16)

    @pl.loop(0, N_DP)
    def _(c):
        wo_copy(c).wait()

    W = C // 2

    def t_cols(c, sub):
        return t_out[:, pl.ds(pl.multiple_of(c * C + sub * W, W), W)]

    class Quarter:
        def __init__(self, q, y_first, base):
            self.q, self.half, self.sub, self.y_first, self.base = q, q // 2, q % 2, y_first, base
            self.cols = slice(self.sub * W, (self.sub + 1) * W)

        def part(self, dy, dx):
            c = at(dy, dx) * 2 + self.half
            rows = mm(att[...], wo[c, :, self.cols])
            pq[self.q, dy, dx, :SEQ, :] = rows[SEQ:].astype(BF16)
            pq[self.q, dy, dx, SEQ:, :] = (rows[:SEQ] + rows[SEQ:] * t_cols(c, self.sub)).astype(BF16)

        def ring(self, dy, k):
            dx, upper, step = ((2, 0, 1), (2, 1, 3), (1, 1, 1), (3, 0, 3), (1, 0, 1), (3, 1, 3))[k]
            rows = pl.ds(upper * SEQ, SEQ)
            side = 0 if step == 1 else 1
            dst = pf.at[self.q, dy, side] if k < 2 else pv.at[self.q, dy, side, rows]
            return remote(
                pq.at[self.q, dy, dx, rows], dst, rs_s.at[self.q, dy, k], rs_r.at[self.q, dy, k],
                tensor=at(0, step),
            )

        def cross(self, dx):
            slot = self.base + dx
            return remote(
                pq.at[self.q, 1, dx], pc.at[slot], cr_s.at[slot], cr_r.at[slot], tensor=at(1, 0)
            )

        def add(self, dx, rows, dy, value):
            old = pq[self.q, dy, dx, rows].astype(F32)
            pq[self.q, dy, dx, rows] = (old + value.astype(F32)).astype(BF16)

        def relay(self, dy):
            self.ring(dy, 0).wait_recv()
            self.add(1, slice(0, SEQ), dy, pf[self.q, dy, 0])
            self.ring(dy, 4).start()
            self.ring(dy, 1).wait_recv()
            self.add(3, slice(SEQ, 2 * SEQ), dy, pf[self.q, dy, 1])
            self.ring(dy, 5).start()

        def row_sum(self, dy):
            for k in (2, 3, 4, 5):
                self.ring(dy, k).wait_recv()
            own = pq[self.q, dy, 0].astype(F32)
            return own + pv[self.q, dy, 0].astype(F32) + pv[self.q, dy, 1].astype(F32)

        def gather(self, k, sender=True):
            if self.y_first:
                sent = (t, t, t, at(0, 3), at(0, 1), at(0, 3), at(0, 1), at(0, 2))
                came = (at(1, 0), at(0, 3), at(0, 1), at(0, 2), at(0, 2), at(1, 3), at(1, 1), at(1, 2))
                to = (at(1, 0), at(0, 1), at(0, 3), at(0, 1), at(0, 3)) + (at(1, 0),) * 3
                lower, upper = (3,), (4,)
            else:
                sent = (t, t, t, at(0, 3), at(0, 1), at(1, 0), at(1, 0), at(1, 3), at(1, 1))
                came = (at(1, 0), at(0, 3), at(0, 1), at(0, 2), at(0, 2)) + (
                    at(1, 3), at(1, 1), at(1, 2), at(1, 2),
                )
                to = (at(1, 0),) + (at(0, 1), at(0, 3)) * 4
                lower, upper = (3, 7), (4, 8)
            j = (sent if sender else came)[k]
            ref = r_all.at[self.q, j]
            if k in lower:
                ref = r_all.at[self.q, j, pl.ds(0, SEQ)]
            if k in upper:
                ref = r_all.at[self.q, j, pl.ds(SEQ, SEQ)]
            return remote(ref, ref, ga_s.at[self.q, k], ga_r.at[self.q, k], tensor=to[k])

        def came(self, *ks):
            for k in ks:
                self.gather(k, False).wait_recv()

        def pass_on(self, *ks):
            for k in ks:
                self.gather(k).start()

        def first(self):
            if self.y_first:
                for dx in (2, 1, 3, 0):
                    self.part(1, dx)
                    self.cross(dx).start()
                for dx in (2, 1, 3, 0):
                    self.part(0, dx)
                return
            for dy in (1, 0):
                for dx, ks in ((2, (0, 1)), (1, (2,)), (3, (3,))):
                    self.part(dy, dx)
                    for k in ks:
                        self.ring(dy, k).start()
            self.part(1, 0)
            self.part(0, 0)

        def second(self):
            if self.y_first:
                for dx, ks in ((2, (0, 1)), (1, (2,)), (3, (3,))):
                    self.cross(dx).wait_recv()
                    self.add(dx, slice(None), 0, pc[self.base + dx])
                    for k in ks:
                        self.ring(0, k).start()
                return
            self.relay(1)
            self.relay(0)

        def third(self):
            if self.y_first:
                self.relay(0)
                return
            pq[self.q, 1, 0] = self.row_sum(1).astype(BF16)
            self.cross(0).start()

        def finish(self):
            total = self.row_sum(0)
            self.cross(0).wait_recv()
            total = total + pc[self.base].astype(F32)
            c = t * 2 + self.half
            base = tok[:, pl.ds(pl.multiple_of(c * C + self.sub * W, W), W)].astype(F32)
            aim = tgt[:, self.q * W : (self.q + 1) * W].astype(F32)
            r_all[self.q, t, :SEQ, :] = (base + total[:SEQ] - aim).astype(BF16)
            r_all[self.q, t, SEQ:, :] = total[SEQ:].astype(BF16)
            self.pass_on(*((1, 2, 0) if self.y_first else (0, 1, 2)))

        def sib_copy(self, j):
            rows = pl.ds(self.sub * W, W)
            return remote(
                wq.at[self.half * N_T + j, rows], sib.at[j, rows], sib_s.at[j, self.sub],
                sib_r.at[j, self.sub], dp=dev(0, 0, 1),
            )

        def use(self, *blocks):
            for j in blocks:
                rows = r_all[self.q, j]
                wq[self.half * N_T + j, self.cols] = mm_tn(rows, att[...]).astype(BF16)

                @pl.when(core != self.half)
                def _():
                    self.sib_copy(j).start()

                c = 2 * j + self.half
                res = rows[:SEQ]
                back = (rows[SEQ:].astype(F32) + res.astype(F32) * t_cols(c, self.sub)).astype(BF16)
                g_acc[...] += mm_nt(jnp.concatenate([res, back], axis=0), wo[c, :, self.cols])

        def z_copy(self, j, k):
            dx, upper, step = ((2, 0, 1), (2, 1, 3), (1, 1, 1), (3, 0, 3), (1, 0, 1), (3, 1, 3))[k]
            yd = j // 4
            rows = pl.ds(self.sub * W + upper * SEQ, SEQ)
            side = 0 if step == 1 else 1
            dst = zf.at[self.sub, yd, side] if k < 2 else zr.at[yd, side, rows]
            return remote(
                wq.at[self.half * N_T + j, rows], dst, z_s.at[self.sub, yd, k],
                z_r.at[self.sub, yd, k], dp=dev(0, step, 0),
            )

        def combine(self, *blocks):
            @pl.when(core == self.half)
            def _():
                for j in blocks:
                    slot = self.half * N_T + j
                    self.sib_copy(j).wait_recv()
                    both = wq[slot, self.cols].astype(F32) + sib[j, self.cols].astype(F32)
                    wq[slot, self.cols] = both.astype(BF16)
                    rel = lax.rem(lax.rem(j, 4) + 4 - z, 4)
                    for want, ks in ((2, (0, 1)), (1, (2,)), (3, (3,))):

                        @pl.when(rel == want)
                        def _():
                            for k in ks:
                                self.z_copy(j, k).start()

        def z_relay(self, *blocks):
            @pl.when(core == self.half)
            def _():
                for j in blocks:
                    slot = self.half * N_T + j
                    rel = lax.rem(lax.rem(j, 4) + 4 - z, 4)
                    for want, side in ((1, 0), (3, 1)):

                        @pl.when(rel == want)
                        def _():
                            self.z_copy(j, side).wait_recv()
                            lo = self.sub * W + side * SEQ
                            old = wq[slot, lo : lo + SEQ].astype(F32)
                            new = old + zf[self.sub, j // 4, side].astype(F32)
                            wq[slot, lo : lo + SEQ] = new.astype(BF16)
                            self.z_copy(j, 4 + side).start()

        def near(self):
            self.came(1)
            self.pass_on(*((3, 5) if self.y_first else (3,)))
            self.came(2)
            self.pass_on(*((4, 6) if self.y_first else (4,)))
            if not self.y_first:
                self.came(0)
                self.pass_on(5, 6)

        def far(self):
            if self.y_first:
                self.came(3, 4)
                self.pass_on(7)
            else:
                self.came(5)
                self.pass_on(7)
                self.came(6)
                self.pass_on(8)

        def own(self):
            self.use(t)

        def near_use(self):
            self.use(at(0, 3), at(0, 1))
            self.combine(t)
            if self.y_first:
                self.came(0)
            self.use(at(1, 0))

        def next_use(self):
            if not self.y_first:
                self.came(3, 4)
            self.combine(at(0, 3), at(0, 1))
            self.use(at(0, 2))

        def far_use(self):
            if self.y_first:
                self.came(5, 6)
            self.combine(at(1, 0), at(0, 2))
            self.use(at(1, 3), at(1, 1))

        def last_use(self):
            self.came(*((7,) if self.y_first else (7, 8)))
            self.use(at(1, 2))
            self.combine(at(1, 3), at(1, 1))

        def relay_near(self):
            self.z_relay(t, at(0, 3), at(0, 1))

        def last(self):
            self.combine(at(1, 2))
            self.z_relay(at(1, 0), at(0, 2))

        def relay_far(self):
            self.z_relay(at(1, 3), at(1, 1), at(1, 2))

        def wait_sends(self):
            for dy in (0,) if self.y_first else (0, 1):
                for k in range(6):
                    self.ring(dy, k).wait_send()
            for dx in range(4) if self.y_first else (0,):
                self.cross(dx).wait_send()
            for k in range(8 if self.y_first else 9):
                self.gather(k).wait_send()

            @pl.when(core != self.half)
            def _():
                for j in range(N_T):
                    self.sib_copy(j).wait_send()

            @pl.when(core == self.half)
            def _():
                for yd in range(2):
                    for k in range(6):
                        self.z_copy(yd * 4, k).wait_send()

    q0 = Quarter(0, False, 0)
    q1 = Quarter(2, False, 1)
    q2 = Quarter(1, True, 2)
    q3 = Quarter(3, False, 6)
    g_acc[...] = jnp.zeros_like(g_acc)
    tgt_copy.wait()
    q0.first()
    q2.first()
    q0.second()
    q1.first()
    q0.third()
    q1.second()
    q0.finish()
    q2.second()
    q3.first()
    q1.third()
    nrm_cross(1)
    q0.own()
    q0.near()
    q1.finish()
    q2.third()
    q0.near_use()
    q3.second()
    nrm_cross(2)
    q1.own()
    q0.next_use()
    q0.far()
    q0.far_use()
    q1.near()
    q1.near_use()
    q2.finish()
    q0.relay_near()
    q3.third()
    q0.last_use()
    q1.far()
    q1.next_use()
    q0.last()
    q2.own()
    q2.near()
    q1.far_use()
    q3.finish()
    q2.near_use()
    q2.far()
    q1.relay_near()
    q1.last_use()
    q0.relay_far()
    q3.own()
    q3.near()
    q2.next_use()
    q2.far_use()
    q1.last()
    q3.near_use()
    q3.far()
    nrm_cross(3)
    q2.relay_near()
    q2.last_use()
    q3.next_use()
    q3.far_use()
    q3.last_use()

    key = kv[0]
    tkey = kv[1]
    val = kv[2]
    tval = kv[3]
    g1 = stack_heads(g_acc[:SEQ]).astype(BF16)
    g2 = stack_heads(g_acc[SEQ:]).astype(BF16)
    p = prob[...]
    tp = tprob[...]
    dpr = mm_nt(g1, val)
    tdpr = mm_nt(g2, val) + mm_nt(g1, tval)
    tval_grad = mm_tn(jnp.concatenate([tp, p], axis=0), jnp.concatenate([g1, g2], axis=0))
    grd_g[d, :, QW + HD :] = tval_grad.astype(BF16)
    dpr = dpr - jnp.sum(p * dpr, axis=1, keepdims=True)
    tdpr = tdpr - jnp.sum(tp * dpr + p * tdpr, axis=1, keepdims=True)
    ds = (p * dpr).astype(BF16)
    tds = (tp * dpr + p * tdpr).astype(BF16)
    both = jnp.concatenate([tds, ds], axis=0)
    trk_grad = mm_tn(both, rot_q[...]) * scale
    trk_grad = trk_grad * cos1 - swap_halves(trk_grad) * sin1
    grd_g[d, :, QW : QW + HD] = trk_grad.astype(BF16)
    trq_grad = (mm(tds, key) + mm(ds, tkey)) * scale
    trq_grad = trq_grad * cos4 - swap_halves(trq_grad) * sin4
    for h in range(HEADS):
        grd_g[d, :, h * HD : (h + 1) * HD] = trq_grad[h * SEQ : (h + 1) * SEQ].astype(BF16)

    def gs_copy(ry, rz):
        b = dev(ry, 4 - rz, 0)
        return remote(
            grd_g.at[b], grd_g.at[b], gs_s.at[ry, rz], gs_r.at[ry, rz], dp=dev(0, 0, 1)
        )

    def gz_copy(ry, k, sender=True):
        step = (1, 3, 1, 3)[k]
        back = (0, 0, 1, 1)[k] if sender else (1, 1, 2, 2)[k]
        b = dev(ry, 4 - back if step == 1 else back, 0)
        h = SEQ // 2
        rows = (pl.ds(0, SEQ), pl.ds(0, SEQ), pl.ds(0, h), pl.ds(h, h))[k]
        ref = grd_g.at[b, rows]
        return remote(ref, ref, gz_s.at[ry, k], gz_r.at[ry, k], dp=dev(0, step, 0))

    def gy_copy(b):
        return remote(grd_g.at[b], grd_g.at[b], gy_s, gy_r, dp=dev(1, 0, 0))

    other = lax.rem(y_hi + 1, 2)

    def z_sum(yd, sub):
        for k in (2, 3, 4, 5):
            own = (q0, q2)[sub]
            own.z_copy(yd * 4, k).wait_recv()
        rows = slice(sub * W, (sub + 1) * W)
        total = wq[core * N_T + yd * 4 + z, rows].astype(F32)
        return total + zr[yd, 0, rows].astype(F32) + zr[yd, 1, rows].astype(F32)

    def y_copy(sub):
        rows = pl.ds(sub * W, W)
        return remote(
            wq.at[core * N_T + other * 4 + z, rows], yr.at[rows], y_s.at[sub], y_r.at[sub],
            dp=dev(1, 0, 0),
        )

    def out_cross(sub):
        wq[core * N_T + other * 4 + z, sub * W : (sub + 1) * W] = z_sum(other, sub).astype(BF16)
        y_copy(sub).start()

    gy_copy(d).start()
    gz_copy(0, 0).start()
    gz_copy(0, 1).start()
    gs_copy(0, 0).start()
    q1.relay_far()
    q2.last()
    out_cross(0)
    q3.relay_near()
    q3.last()
    q2.relay_far()
    gy_copy(dev(1, 0, 0)).wait_recv()
    gz_copy(1, 0).start()
    gz_copy(1, 1).start()
    gs_copy(1, 0).start()
    for ry in range(2):
        for k, rz in ((0, 1), (1, 3)):
            gz_copy(ry, k, False).wait_recv()
            gz_copy(ry, k + 2).start()
            gs_copy(ry, rz).start()
        if ry == 0:
            q3.relay_far()

    out_cross(1)

    def product(first):
        rows = pl.ds(first * N_T, N_T)
        lhs = nrm_g[rows].reshape(N_T * SEQ, C)
        rhs = grd_g[rows].reshape(N_T * SEQ, QW + 2 * HD)
        return mm_tn(lhs, rhs)

    def arrived(ry):
        for rz in range(4):
            for rc in range(2):
                if (ry, rz, rc) != (0, 0, 0):
                    src = dev(ry, 4 - rz, rc)
                    r = (ry * 4 + rz) * 2 + rc
                    remote(
                        nrm_g.at[src], nrm_g.at[src], nrm_s.at[r], nrm_r.at[r], dp=src
                    ).wait_recv()
            b = dev(ry, 4 - rz, 1)
            remote(
                grd_g.at[b], grd_g.at[b], gs_s.at[ry, rz], gs_r.at[ry, rz], dp=dev(0, 0, 1)
            ).wait_recv()

    gz_copy(0, 2, False).wait_recv()
    gz_copy(0, 3, False).wait_recv()
    gs_copy(0, 2).start()
    for sub in range(2):
        ho[sub * W : (sub + 1) * W, :] = z_sum(y_hi, sub)
    arrived(0)
    out = product(y_hi)
    hq[...] = out[:, :QW]
    hk[...] = out[:, QW : QW + HD]
    hv[...] = out[:, QW + HD :]
    gz_copy(1, 2, False).wait_recv()
    gz_copy(1, 3, False).wait_recv()
    gs_copy(1, 2).start()
    for sub in range(2):
        y_copy(sub).wait_recv()
    ho[...] += yr[...].astype(F32)
    arrived(1)
    out = product(other)
    hq[...] += out[:, :QW]
    hk[...] += out[:, QW : QW + HD]
    hv[...] += out[:, QW + HD :]

    for rel in everyone:
        nrm_copy(*rel).wait_send()

    for quarter in (q0, q1, q2, q3):
        quarter.wait_sends()
    for yd in range(2):
        for k in range(4):
            gz_copy(yd, k).wait_send()
        for rz in range(4):
            gs_copy(yd, rz).wait_send()
        y_copy(yd).wait_send()
    gy_copy(d).wait_send()


def hand_over(a, b, c, e, a_out, b_out, c_out, e_out, a_buf, b_buf, c_buf, e_buf, sem):
    arrays = ((a, a_buf, a_out), (e, e_buf, e_out), (b, b_buf, b_out), (c, c_buf, c_out))
    loads, stores = [], []
    for i, (src, buf, dst) in enumerate(arrays):
        for part in range(2):
            rows = pl.ds(part * (C // 2), C // 2)
            loads.append(
                pltpu.make_async_copy(src.at[rows], buf.at[rows], sem.at[0, 2 * i + part])
            )
            stores.append(
                pltpu.make_async_copy(buf.at[rows], dst.at[rows], sem.at[1, 2 * i + part])
            )
    for load in loads:
        load.start()
    for load, store in zip(loads, stores):
        load.wait()
        store.start()
    for store in stores:
        store.wait()


def tables():
    frequency = np.exp(
        np.float32(-math.log(10000.0)) * np.arange(HD // 2, dtype=np.float32) * np.float32(2.0)
        / np.float32(HD)
    ).astype(np.float32)
    angles = np.arange(SEQ, dtype=np.float32)[:, None] * frequency[None, :]
    cosine = np.cos(angles).astype(np.float32)
    sine = np.sin(angles).astype(np.float32)
    return np.concatenate([cosine, cosine], 1), np.concatenate([-sine, sine], 1)


def local(
    tokens, target, norm_gain, w_query, w_key, w_value, w_out, t_query, t_key, t_value, t_out
):
    cos_t, sin_t = tables()
    any_spec = pl.BlockSpec(memory_space=pl.ANY)
    vmem = pl.BlockSpec(memory_space=pltpu.VMEM)
    dma = pltpu.SemaphoreType.DMA
    block = (2 * SEQ, C // 2)
    scratch = [
        pltpu.VMEM((SEQ, D), BF16),
        pltpu.VMEM((SEQ, 2 * C), BF16),
        pltpu.VMEM((N_DP, C, QW), BF16),
        pltpu.VMEM((N_DP, C, HD), BF16),
        pltpu.VMEM((N_DP, C, HD), BF16),
        pltpu.VMEM((N_DP, QW, C), BF16),
        pltpu.VMEM((N_DP, SEQ, C), BF16),
        pltpu.VMEM((N_DP, SEQ, C), BF16),
        pltpu.VMEM((2 * SEQ, QW), BF16),
        pltpu.VMEM((N_T, C, QW), BF16),
        pltpu.VMEM((2, 2, 2, SEQ, QW), BF16),
        pltpu.VMEM((2, 2, C, QW), BF16),
        pltpu.VMEM((C, QW), BF16),
        pltpu.VMEM((N_DP, SEQ, QW + 2 * HD), BF16),
        pltpu.VMEM((4, 2, 4) + block, BF16),
        pltpu.VMEM((4, 2, 2, SEQ, C // 2), BF16),
        pltpu.VMEM((4, 2, 2) + block, BF16),
        pltpu.VMEM((7,) + block, BF16),
        pltpu.VMEM((4, N_T) + block, BF16),
        pltpu.VMEM((2 * SEQ, QW), F32),
        pltpu.VMEM((SEQ, QW + 2 * HD), F32),
        pltpu.VMEM((HEADS * SEQ, SEQ), F32),
        pltpu.VMEM((HEADS * SEQ, SEQ), F32),
        pltpu.VMEM((2 * HEADS * SEQ, HD), BF16),
        pltpu.VMEM((4, SEQ, HD), BF16),
        dma((2,)), dma((3, N_DP)), dma((N_DP,)),
        dma((N_DP,)), dma((N_DP,)), dma((N_T, 2)), dma((N_T, 2)), dma((2, 2, 6)), dma((2, 2, 6)),
        dma((2,)), dma((2,)), dma((2, 4)), dma((2, 4)), dma, dma, dma((2, 4)), dma((2, 4)),
        dma((4, 2, 6)), dma((4, 2, 6)), dma((7,)), dma((7,)), dma((4, 9)), dma((4, 9)),
    ]
    shapes = tuple(jax.ShapeDtypeStruct((C, n), F32) for n in (QW, HD, HD, QW))
    results = pl.pallas_call(
        kernel,
        out_shape=shapes,
        in_specs=[
            any_spec, any_spec, vmem, any_spec, any_spec, any_spec, any_spec,
            vmem, vmem, vmem, vmem, vmem, vmem,
        ],
        out_specs=(vmem, vmem, vmem, vmem),
        scratch_shapes=scratch,
        compiler_params=pltpu.CompilerParams(
            collective_id=0, has_side_effects=True, vmem_limit_bytes=62 * 1024 * 1024
        ),
        cost_estimate=pl.CostEstimate(
            flops=10_000_000_000, bytes_accessed=26_000_000, transcendentals=65536
        ),
        name="hvp",
    )(
        tokens, target, norm_gain.reshape(1, D), w_query, w_key, w_value, w_out,
        t_query.reshape(1, QW), t_key.reshape(1, HD), t_value.reshape(1, HD),
        t_out.reshape(1, D), jnp.asarray(cos_t), jnp.asarray(sin_t),
    )
    return pl.pallas_call(
        hand_over,
        out_shape=shapes,
        in_specs=[any_spec] * 4,
        out_specs=(any_spec,) * 4,
        scratch_shapes=[pltpu.VMEM((C, n), F32) for n in (QW, HD, HD, QW)] + [dma((2, 8))],
        compiler_params=pltpu.CompilerParams(vmem_limit_bytes=62 * 1024 * 1024),
        name="results",
    )(*results)


def solution(mesh):
    return jax.shard_map(
        local,
        mesh=mesh,
        in_specs=(
            P("dp", None),
            P("dp", None),
            P(),
            P(None, "tensor"),
            P(None, "tensor"),
            P(None, "tensor"),
            P("tensor", None),
            P("tensor"),
            P("tensor"),
            P("tensor"),
            P(),
        ),
        out_specs=(P("dp", "tensor"), P("dp", "tensor"), P("dp", "tensor"), P("dp", "tensor")),
        check_vma=False,
    )
```

```python
import functools
import math

import jax
import jax.numpy as jnp
import numpy as np
from jax import lax
from jax.experimental import pallas as pl
from jax.experimental.pallas import tpu as pltpu
from jax.sharding import PartitionSpec as P

HD = 128
HEADS = 4
SEQ = 128
D = 8192
QW = HEADS * HD
N_DP = 16
N_T = 8
C = 512
EPS = 1e-05
F32 = jnp.float32
BF16 = jnp.bfloat16
MESH = pl.DeviceIdType.MESH


def mm(a, b):
    return lax.dot_general(
        a.astype(BF16), b.astype(BF16), (((1,), (0,)), ((), ())), preferred_element_type=F32
    )


def mm_nt(a, b):
    return lax.dot_general(
        a.astype(BF16), b.astype(BF16), (((1,), (1,)), ((), ())), preferred_element_type=F32
    )


def mm_tn(a, b):
    return lax.dot_general(
        a.astype(BF16), b.astype(BF16), (((0,), (0,)), ((), ())), preferred_element_type=F32
    )


def mm_nt_wide(a, b):
    a_hi = a.astype(BF16)
    b_hi = b.astype(BF16)
    a_lo = (a - a_hi.astype(F32)).astype(BF16)
    b_lo = (b - b_hi.astype(F32)).astype(BF16)
    return mm_nt(a_hi, b_hi) + (mm_nt(a_hi, b_lo) + mm_nt(a_lo, b_hi))


def swap_halves(x):
    return jnp.concatenate([x[:, HD // 2 :], x[:, : HD // 2]], axis=1)


def stack_heads(x):
    return jnp.concatenate([x[:, h * HD : (h + 1) * HD] for h in range(HEADS)], axis=0)


def kernel(
    tok_hbm, tgt_hbm, gain, wq_hbm, wk_hbm, wv_hbm, wo_hbm, tq, tk, tv, t_out, cos_t, sin_t,
    hq_hbm, hk_hbm, hv_hbm, ho_hbm,
    hq, hk, hv, ho, tok, tgt, wq, wk, wv, wo, nrm, nrm_g, att, sib, zf, zr, yr, grd_g, gkv_g,
    pq, pf, pv, pc, r_all, g_acc, proj,
    prob, tprob, rot_q, kv,
    in_sem, out_sem, wqkv_sem, wo_sem,
    nrm_s, nrm_r, sib_s, sib_r, z_s, z_r, y_s, y_r,
    gz_s, gz_r, gy_r, gs_s, gs_r, hz_s, hz_r, hy_r, hs_s, hs_r,
    rs_s, rs_r, cr_r, ga_s, ga_r,
):
    d = lax.axis_index("dp")
    t = lax.axis_index("tensor")
    x = lax.rem(t, 4)
    y = t // 4
    core = lax.rem(d, 2)
    z = lax.rem(d // 2, 4)
    y_hi = d // 8

    def dev(ry, rz, rc):
        return (lax.rem(y_hi + ry, 2) * 4 + lax.rem(z + rz, 4)) * 2 + lax.rem(core + rc, 2)

    def at(dy, dx):
        return lax.rem(y + dy, 2) * 4 + lax.rem(x + dx, 4)

    def remote(src, dst, s_sem, r_sem, **where):
        return pltpu.make_async_remote_copy(
            src_ref=src, dst_ref=dst, send_sem=s_sem, recv_sem=r_sem,
            device_id=where, device_id_type=MESH,
        )

    bar = pltpu.get_barrier_semaphore()

    @pl.loop(1, N_DP)
    def _(r):
        pl.semaphore_signal(
            bar, inc=1, device_id={"dp": lax.rem(d + r, N_DP)}, device_id_type=MESH
        )

    for dy, dx in ((1, 0), (0, 1), (0, 2), (0, 3)):
        pl.semaphore_signal(bar, inc=1, device_id={"tensor": at(dy, dx)}, device_id_type=MESH)

    tok_copy = pltpu.make_async_copy(tok_hbm, tok, in_sem.at[0])
    tok_copy.start()
    tgt_copy = pltpu.make_async_copy(
        tgt_hbm.at[:, pl.ds(pl.multiple_of(t * 2 * C, 2 * C), 2 * C)], tgt, in_sem.at[1]
    )

    GROUP = 4

    def w_copies(g):
        part = pl.ds(g * GROUP, GROUP)
        return [
            pltpu.make_async_copy(src.at[part], dst.at[part], wqkv_sem.at[i, g])
            for i, (src, dst) in enumerate(((wq_hbm, wq), (wk_hbm, wk), (wv_hbm, wv)))
        ]

    def wo_copy(c):
        return pltpu.make_async_copy(
            wo_hbm.at[:, pl.ds(pl.multiple_of(c * C, C), C)], wo.at[c], wo_sem
        )

    @pl.loop(0, N_DP // GROUP)
    def _(g):
        for cp in w_copies(g):
            cp.start()

    tgt_copy.start()

    @pl.loop(0, N_DP)
    def _(c):
        wo_copy(c).start()

    tok_copy.wait()

    def square_step(c, acc):
        v = tok[:, pl.ds(pl.multiple_of(c * C, C), C)].astype(F32)
        return acc + v * v

    squares = lax.fori_loop(0, N_DP, square_step, jnp.zeros((SEQ, C), F32))
    inv = lax.rsqrt(jnp.sum(squares, axis=1, keepdims=True) * (1.0 / D) + EPS)

    @pl.loop(0, N_DP)
    def _(c):
        cols = pl.ds(pl.multiple_of(c * C, C), C)
        nrm[c] = (tok[:, cols].astype(F32) * inv * gain[:, cols]).astype(BF16)

    nrm_g[d] = nrm[d]

    pl.semaphore_wait(bar, N_DP - 1 + 4)

    def nrm_copy(ry, rz, rc):
        dest = dev(ry, rz, rc)
        r = (ry * 4 + rz) * 2 + rc
        return remote(nrm.at[dest], nrm_g.at[d], nrm_s, nrm_r.at[r], dp=dest)

    early = [(0, rz, rc) for rz in (1, 3, 2) for rc in (0, 1)] + [(0, 0, 1)]
    crossing = [[(1, rz, rc) for rc in (0, 1)] for rz in (2, 1, 3, 0)]
    everyone = early + sum(crossing, [])

    def nrm_cross(i):
        for rel in crossing[i]:
            nrm_copy(*rel).start()

    for rel in early:
        nrm_copy(*rel).start()
    nrm_cross(0)

    @pl.loop(0, N_DP // GROUP)
    def _(g):
        total = [jnp.zeros((SEQ, n), F32) for n in (QW, HD, HD)]
        for cp in w_copies(g):
            cp.wait()
        for i in range(GROUP):
            c = g * GROUP + i
            lhs = nrm[c]
            total = [a + mm(lhs, w[c]) for a, w in zip(total, (wq, wk, wv))]

        @pl.when(g == 0)
        def _():
            proj[...] = jnp.concatenate(total, axis=1)

        @pl.when(g > 0)
        def _():
            proj[...] += jnp.concatenate(total, axis=1)

    cos1 = cos_t[...]
    sin1 = sin_t[...]
    cos4 = jnp.concatenate([cos1] * HEADS, axis=0)
    sin4 = jnp.concatenate([sin1] * HEADS, axis=0)
    scale = 1.0 / math.sqrt(HD)

    q2 = proj[:, :QW]
    key = proj[:, QW : QW + HD]
    val = proj[:, QW + HD :]
    tval = val * tv[...]
    qs = stack_heads(q2)
    tqs = stack_heads(q2 * tq[...])
    rq = qs * cos4 + swap_halves(qs) * sin4
    trq = tqs * cos4 + swap_halves(tqs) * sin4
    tkey = key * tk[...]
    rk = key * cos1 + swap_halves(key) * sin1
    trk = tkey * cos1 + swap_halves(tkey) * sin1
    rot_q[...] = jnp.concatenate([rq.astype(BF16), trq.astype(BF16)], axis=0)
    kv[0] = rk.astype(BF16)
    kv[1] = trk.astype(BF16)
    kv[2] = val.astype(BF16)
    kv[3] = tval.astype(BF16)
    scores = mm_nt_wide(rq, rk) * scale
    tscores = (mm_nt_wide(trq, rk) + mm_nt_wide(rq, trk)) * scale
    row = lax.rem(lax.broadcasted_iota(jnp.int32, (HEADS * SEQ, SEQ), 0), SEQ)
    col = lax.broadcasted_iota(jnp.int32, (HEADS * SEQ, SEQ), 1)
    scores = jnp.where(row >= col, scores, -1e30)
    e = jnp.exp(scores - jnp.max(scores, axis=1, keepdims=True))
    p = e / jnp.sum(e, axis=1, keepdims=True)
    tp = p * (tscores - jnp.sum(p * tscores, axis=1, keepdims=True))
    prob[...] = p
    tprob[...] = tp
    o = mm(p, val)
    to = mm(tp, val) + mm(p, tval)
    for h in range(HEADS):
        att[:SEQ, h * HD : (h + 1) * HD] = to[h * SEQ : (h + 1) * SEQ].astype(BF16)
        att[SEQ:, h * HD : (h + 1) * HD] = o[h * SEQ : (h + 1) * SEQ].astype(BF16)

    pltpu.make_async_copy(wo, wo, wo_sem).wait()

    W = C // 2

    def t_cols(c, sub):
        return t_out[:, pl.ds(pl.multiple_of(c * C + sub * W, W), W)]

    class Quarter:
        def __init__(self, q, y_first, base):
            self.q, self.half, self.sub, self.y_first, self.base = q, q // 2, q % 2, y_first, base
            self.cols = slice(self.sub * W, (self.sub + 1) * W)

        def part(self, dy, dx):
            c = at(dy, dx) * 2 + self.half
            rows = mm(att[...], wo[c, :, self.cols])
            pq[self.q, dy, dx, :SEQ, :] = rows[SEQ:].astype(BF16)
            pq[self.q, dy, dx, SEQ:, :] = (rows[:SEQ] + rows[SEQ:] * t_cols(c, self.sub)).astype(BF16)

        def ring(self, dy, k):
            dx, upper, step = ((2, 0, 1), (2, 1, 3), (1, 1, 1), (3, 0, 3), (1, 0, 1), (3, 1, 3))[k]
            rows = pl.ds(upper * SEQ, SEQ)
            side = 0 if step == 1 else 1
            dst = pf.at[self.q, dy, side] if k < 2 else pv.at[self.q, dy, side, rows]
            return remote(
                pq.at[self.q, dy, dx, rows], dst, rs_s.at[self.q], rs_r.at[self.q, dy, k],
                tensor=at(0, step),
            )

        def cross(self, dx):
            slot = self.base + dx
            return remote(
                pq.at[self.q, 1, dx], pc.at[slot], rs_s.at[self.q], cr_r.at[slot], tensor=at(1, 0)
            )

        def add(self, dx, rows, dy, value):
            old = pq[self.q, dy, dx, rows].astype(F32)
            pq[self.q, dy, dx, rows] = (old + value.astype(F32)).astype(BF16)

        def relay(self, dy):
            self.ring(dy, 0).wait_recv()
            self.add(1, slice(0, SEQ), dy, pf[self.q, dy, 0])
            self.ring(dy, 4).start()
            self.ring(dy, 1).wait_recv()
            self.add(3, slice(SEQ, 2 * SEQ), dy, pf[self.q, dy, 1])
            self.ring(dy, 5).start()

        def row_sum(self, dy):
            for k in (2, 3, 4, 5):
                self.ring(dy, k).wait_recv()
            own = pq[self.q, dy, 0].astype(F32)
            return own + pv[self.q, dy, 0].astype(F32) + pv[self.q, dy, 1].astype(F32)

        def gather(self, k, sender=True):
            if self.y_first:
                sent = (t, t, t, at(0, 3), at(0, 1), at(0, 3), at(0, 1), at(0, 2))
                came = (at(1, 0), at(0, 3), at(0, 1), at(0, 2), at(0, 2), at(1, 3), at(1, 1), at(1, 2))
                to = (at(1, 0), at(0, 1), at(0, 3), at(0, 1), at(0, 3)) + (at(1, 0),) * 3
                lower, upper = (3,), (4,)
            else:
                sent = (t, t, t, at(0, 3), at(0, 1), at(1, 0), at(1, 0), at(1, 3), at(1, 1))
                came = (at(1, 0), at(0, 3), at(0, 1), at(0, 2), at(0, 2)) + (
                    at(1, 3), at(1, 1), at(1, 2), at(1, 2),
                )
                to = (at(1, 0),) + (at(0, 1), at(0, 3)) * 4
                lower, upper = (3, 7), (4, 8)
            j = (sent if sender else came)[k]
            ref = r_all.at[self.q, j]
            if k in lower:
                ref = r_all.at[self.q, j, pl.ds(0, SEQ)]
            if k in upper:
                ref = r_all.at[self.q, j, pl.ds(SEQ, SEQ)]
            return remote(ref, ref, ga_s.at[self.q], ga_r.at[self.q, k], tensor=to[k])

        def came(self, *ks):
            for k in ks:
                self.gather(k, False).wait_recv()

        def pass_on(self, *ks):
            for k in ks:
                self.gather(k).start()

        def first(self):
            if self.y_first:
                for dx in (2, 1, 3, 0):
                    self.part(1, dx)
                    self.cross(dx).start()
                for dx in (2, 1, 3, 0):
                    self.part(0, dx)
                return
            for dy in (1, 0):
                for dx, ks in ((2, (0, 1)), (1, (2,)), (3, (3,))):
                    self.part(dy, dx)
                    for k in ks:
                        self.ring(dy, k).start()
            self.part(1, 0)
            self.part(0, 0)

        def second(self):
            if self.y_first:
                for dx, ks in ((2, (0, 1)), (1, (2,)), (3, (3,))):
                    self.cross(dx).wait_recv()
                    self.add(dx, slice(None), 0, pc[self.base + dx])
                    for k in ks:
                        self.ring(0, k).start()
                return
            self.relay(1)
            self.relay(0)

        def third(self):
            if self.y_first:
                self.relay(0)
                return
            pq[self.q, 1, 0] = self.row_sum(1).astype(BF16)
            self.cross(0).start()

        def finish(self):
            total = self.row_sum(0)
            self.cross(0).wait_recv()
            total = total + pc[self.base].astype(F32)
            c = t * 2 + self.half
            base = tok[:, pl.ds(pl.multiple_of(c * C + self.sub * W, W), W)].astype(F32)
            aim = tgt[:, self.q * W : (self.q + 1) * W].astype(F32)
            r_all[self.q, t, :SEQ, :] = (base + total[:SEQ] - aim).astype(BF16)
            r_all[self.q, t, SEQ:, :] = total[SEQ:].astype(BF16)
            self.pass_on(*((1, 2, 0) if self.y_first else (0, 1, 2)))

        def sib_copy(self, j):
            rows = pl.ds(self.sub * W, W)
            return remote(
                wq.at[self.half * N_T + j, rows], sib.at[j, rows], sib_s.at[self.sub],
                sib_r.at[j, self.sub], dp=dev(0, 0, 1),
            )

        def use(self, *blocks):
            for j in blocks:
                rows = r_all[self.q, j]
                wq[self.half * N_T + j, self.cols] = mm_tn(rows, att[...]).astype(BF16)

                @pl.when(core != self.half)
                def _():
                    self.sib_copy(j).start()

                c = 2 * j + self.half
                res = rows[:SEQ]
                back = (rows[SEQ:].astype(F32) + res.astype(F32) * t_cols(c, self.sub)).astype(BF16)
                g_acc[...] += mm_nt(jnp.concatenate([res, back], axis=0), wo[c, :, self.cols])

        def z_copy(self, j, k):
            dx, upper, step = ((2, 0, 1), (2, 1, 3), (1, 1, 1), (3, 0, 3), (1, 0, 1), (3, 1, 3))[k]
            yd = j // 4
            rows = pl.ds(self.sub * W + upper * SEQ, SEQ)
            side = 0 if step == 1 else 1
            dst = zf.at[self.sub, yd, side] if k < 2 else zr.at[yd, side, rows]
            return remote(
                wq.at[self.half * N_T + j, rows], dst, z_s.at[self.sub],
                z_r.at[self.sub, yd, k], dp=dev(0, step, 0),
            )

        def combine(self, *blocks):
            @pl.when(core == self.half)
            def _():
                for j in blocks:
                    slot = self.half * N_T + j
                    self.sib_copy(j).wait_recv()
                    both = wq[slot, self.cols].astype(F32) + sib[j, self.cols].astype(F32)
                    wq[slot, self.cols] = both.astype(BF16)
                    rel = lax.rem(lax.rem(j, 4) + 4 - z, 4)
                    for want, ks in ((2, (0, 1)), (1, (2,)), (3, (3,))):

                        @pl.when(rel == want)
                        def _():
                            for k in ks:
                                self.z_copy(j, k).start()

        def z_relay(self, *blocks):
            @pl.when(core == self.half)
            def _():
                for j in blocks:
                    slot = self.half * N_T + j
                    rel = lax.rem(lax.rem(j, 4) + 4 - z, 4)
                    for want, side in ((1, 0), (3, 1)):

                        @pl.when(rel == want)
                        def _():
                            self.z_copy(j, side).wait_recv()
                            lo = self.sub * W + side * SEQ
                            old = wq[slot, lo : lo + SEQ].astype(F32)
                            new = old + zf[self.sub, j // 4, side].astype(F32)
                            wq[slot, lo : lo + SEQ] = new.astype(BF16)
                            self.z_copy(j, 4 + side).start()

        def near(self):
            self.came(1)
            self.pass_on(*((3, 5) if self.y_first else (3,)))
            self.came(2)
            self.pass_on(*((4, 6) if self.y_first else (4,)))
            if not self.y_first:
                self.came(0)
                self.pass_on(5, 6)

        def far(self):
            if self.y_first:
                self.came(3, 4)
                self.pass_on(7)
            else:
                self.came(5)
                self.pass_on(7)
                self.came(6)
                self.pass_on(8)

        def own(self):
            self.use(t)

        def own_sum(self):
            self.combine(t)

        def near_use(self):
            self.use(at(0, 3), at(0, 1))
            if self.y_first:
                self.came(0)
            self.use(at(1, 0))

        def next_use(self):
            self.combine(at(0, 3), at(0, 1), at(1, 0))
            if not self.y_first:
                self.came(3, 4)
            self.use(at(0, 2))

        def far_use(self):
            if self.y_first:
                self.came(5, 6)
            self.combine(at(0, 2))
            self.use(at(1, 3), at(1, 1))

        def last_use(self):
            self.came(*((7,) if self.y_first else (7, 8)))
            self.use(at(1, 2))
            self.combine(at(1, 3), at(1, 1))

        def relay_near(self):
            self.z_relay(t, at(0, 3), at(0, 1))

        def last(self):
            self.combine(at(1, 2))
            self.z_relay(at(1, 0), at(0, 2))

        def relay_far(self):
            self.z_relay(at(1, 3), at(1, 1))

        def relay_last(self):
            self.z_relay(at(1, 2))

        def wait_sends(self):
            sent = r_all.at[self.q, pl.ds(0, 7)]
            pltpu.make_async_copy(sent, sent, rs_s.at[self.q]).wait()
            pltpu.make_async_copy(sent, sent, ga_s.at[self.q]).wait()

            @pl.when(core != self.half)
            def _():
                to_core = wq.at[pl.ds(0, 4)]
                pltpu.make_async_copy(to_core, to_core, sib_s.at[self.sub]).wait()

            @pl.when(core == self.half)
            def _():
                along_z = wq.at[pl.ds(0, 3)]
                pltpu.make_async_copy(along_z, along_z, z_s.at[self.sub]).wait()

    q0 = Quarter(0, False, 0)
    q1 = Quarter(2, False, 1)
    q2 = Quarter(1, True, 2)
    q3 = Quarter(3, False, 6)
    other = lax.rem(y_hi + 1, 2)

    def z_sum(yd, sub):
        for k in (2, 3, 4, 5):
            own = (q0, q2)[sub]
            own.z_copy(yd * 4, k).wait_recv()
        rows = slice(sub * W, (sub + 1) * W)
        total = wq[core * N_T + yd * 4 + z, rows].astype(F32)
        return total + zr[yd, 0, rows].astype(F32) + zr[yd, 1, rows].astype(F32)

    def y_copy(sub):
        rows = pl.ds(sub * W, W)
        return remote(
            wq.at[core * N_T + other * 4 + z, rows], yr.at[rows], y_s.at[sub], y_r.at[sub],
            dp=dev(1, 0, 0),
        )

    def out_cross(sub):
        wq[core * N_T + other * 4 + z, sub * W : (sub + 1) * W] = z_sum(other, sub).astype(BF16)
        y_copy(sub).start()

    g_acc[...] = jnp.zeros_like(g_acc)
    tgt_copy.wait()
    q0.first()
    q2.first()
    q0.second()
    q1.first()
    q0.third()
    q1.second()
    q0.finish()
    q2.second()
    q3.first()
    q1.third()
    nrm_cross(1)
    q0.own()
    q0.near()
    q1.finish()
    q1.own()
    q2.third()
    q0.own_sum()
    q0.near_use()
    q3.second()
    nrm_cross(2)
    q1.own_sum()
    q0.next_use()
    q0.far()
    q0.far_use()
    q1.near()
    q1.near_use()
    q2.finish()
    q2.own()
    q0.relay_near()
    q3.third()
    q0.last_use()
    q2.own_sum()
    q0.last()
    q1.far()
    q1.next_use()
    q2.near()
    q1.far_use()
    q3.finish()
    q3.own()
    q2.near_use()
    q0.relay_far()
    q2.far()
    q3.own_sum()
    q1.relay_near()
    q1.last_use()
    q0.relay_last()
    q3.near()
    q2.next_use()
    q1.last()
    q2.far_use()
    q3.near_use()
    q1.relay_far()
    q3.far()
    nrm_cross(3)
    q2.relay_near()
    q2.last_use()
    q3.next_use()
    q2.last()
    q1.relay_last()
    out_cross(0)
    q3.far_use()
    q3.last_use()

    key = kv[0]
    tkey = kv[1]
    val = kv[2]
    tval = kv[3]
    g1 = stack_heads(g_acc[:SEQ]).astype(BF16)
    g2 = stack_heads(g_acc[SEQ:]).astype(BF16)
    p = prob[...]
    tp = tprob[...]
    dpr = mm_nt(g1, val)
    tdpr = mm_nt(g2, val) + mm_nt(g1, tval)
    tval_grad = mm_tn(jnp.concatenate([tp, p], axis=0), jnp.concatenate([g1, g2], axis=0))
    gkv_g[d, :, HD:] = tval_grad.astype(BF16)
    dpr = dpr - jnp.sum(p * dpr, axis=1, keepdims=True)
    tdpr = tdpr - jnp.sum(tp * dpr + p * tdpr, axis=1, keepdims=True)
    ds = (p * dpr).astype(BF16)
    tds = (tp * dpr + p * tdpr).astype(BF16)
    both = jnp.concatenate([tds, ds], axis=0)
    trk_grad = mm_tn(both, rot_q[...]) * scale
    trk_grad = trk_grad * cos1 - swap_halves(trk_grad) * sin1
    gkv_g[d, :, :HD] = trk_grad.astype(BF16)
    trq_grad = (mm(tds, key) + mm(ds, tkey)) * scale
    trq_grad = trq_grad * cos4 - swap_halves(trq_grad) * sin4
    for h in range(HEADS):
        grd_g[d, :, h * HD : (h + 1) * HD] = trq_grad[h * SEQ : (h + 1) * SEQ].astype(BF16)

    def gs_copy(ry, rz):
        b = dev(ry, 4 - rz, 0)
        return remote(
            grd_g.at[b], grd_g.at[b], gs_s, gs_r.at[ry, rz], dp=dev(0, 0, 1)
        )

    def gz_copy(ry, k, sender=True):
        step = (1, 3, 1, 3)[k]
        back = (0, 0, 1, 1)[k] if sender else (1, 1, 2, 2)[k]
        b = dev(ry, 4 - back if step == 1 else back, 0)
        h = SEQ // 2
        rows = (pl.ds(0, SEQ), pl.ds(0, SEQ), pl.ds(0, h), pl.ds(h, h))[k]
        ref = grd_g.at[b, rows]
        return remote(ref, ref, gz_s, gz_r.at[ry, k], dp=dev(0, step, 0))

    def gy_copy(b):
        return remote(grd_g.at[b], grd_g.at[b], gz_s, gy_r, dp=dev(1, 0, 0))

    def hs_copy(ry, rz):
        b = dev(ry, 4 - rz, 0)
        return remote(
            gkv_g.at[b], gkv_g.at[b], hs_s, hs_r.at[ry, rz], dp=dev(0, 0, 1)
        )

    def hz_copy(k, sender=True):
        step = (1, 3, 1, 3)[k]
        back = (0, 0, 1, 1)[k] if sender else (1, 1, 2, 2)[k]
        b = dev(0, 4 - back if step == 1 else back, 0)
        h = SEQ // 2
        rows = (pl.ds(0, SEQ), pl.ds(0, SEQ), pl.ds(0, h), pl.ds(h, h))[k]
        ref = gkv_g.at[b, rows]
        return remote(ref, ref, hz_s, hz_r.at[k], dp=dev(0, step, 0))

    def hy_copy(rz, sender=True):
        b = dev(0 if sender else 1, 4 - rz, 0)
        return remote(gkv_g.at[b], gkv_g.at[b], hz_s, hy_r.at[rz], dp=dev(1, 0, 0))

    def pass_on(ry):
        for k, rz in ((0, 1), (1, 3)):
            gz_copy(ry, k, False).wait_recv()
            gz_copy(ry, k + 2).start()
            gs_copy(ry, rz).start()

    gy_copy(d).start()
    hy_copy(0).start()
    hz_copy(0).start()
    hz_copy(1).start()
    gz_copy(0, 0).start()
    gz_copy(0, 1).start()
    hs_copy(0, 0).start()
    gs_copy(0, 0).start()
    q3.relay_near()
    q3.last()
    q2.relay_far()
    q2.relay_last()
    for k, rz in ((0, 1), (1, 3)):
        hz_copy(k, False).wait_recv()
        hz_copy(k + 2).start()
        hy_copy(rz).start()
        hs_copy(0, rz).start()
    gy_copy(dev(1, 0, 0)).wait_recv()
    gz_copy(1, 0).start()
    gz_copy(1, 1).start()
    gs_copy(1, 0).start()
    q3.relay_far()
    pass_on(0)
    q3.relay_last()
    hz_copy(2, False).wait_recv()
    hz_copy(3, False).wait_recv()
    hy_copy(2).start()
    hs_copy(0, 2).start()
    hy_copy(0, False).wait_recv()
    hs_copy(1, 0).start()
    out_cross(1)
    pass_on(1)
    for rz in (1, 3):
        hy_copy(rz, False).wait_recv()
        hs_copy(1, rz).start()

    def product(first):
        rows = pl.ds(first * N_T, N_T)
        lhs = nrm_g[rows].reshape(N_T * SEQ, C)
        of_query = mm_tn(lhs, grd_g[rows].reshape(N_T * SEQ, QW))
        return of_query, mm_tn(lhs, gkv_g[rows].reshape(N_T * SEQ, 2 * HD))

    def arrived(ry):
        for rz in range(4):
            for rc in range(2):
                if (ry, rz, rc) != (0, 0, 0):
                    src = dev(ry, 4 - rz, rc)
                    r = (ry * 4 + rz) * 2 + rc
                    remote(
                        nrm_g.at[src], nrm_g.at[src], nrm_s, nrm_r.at[r], dp=src
                    ).wait_recv()
            b = dev(ry, 4 - rz, 1)
            remote(
                grd_g.at[b], grd_g.at[b], gs_s, gs_r.at[ry, rz], dp=dev(0, 0, 1)
            ).wait_recv()
            remote(
                gkv_g.at[b], gkv_g.at[b], hs_s, hs_r.at[ry, rz], dp=dev(0, 0, 1)
            ).wait_recv()

    gz_copy(0, 2, False).wait_recv()
    gz_copy(0, 3, False).wait_recv()
    gs_copy(0, 2).start()
    for sub in range(2):
        ho[sub * W : (sub + 1) * W, :] = z_sum(y_hi, sub)
    arrived(0)
    of_query, of_kv = product(y_hi)
    hq[...] = of_query
    hk[...] = of_kv[:, :HD]
    hv[...] = of_kv[:, HD:]
    gz_copy(1, 2, False).wait_recv()
    gz_copy(1, 3, False).wait_recv()
    gs_copy(1, 2).start()
    hy_copy(2, False).wait_recv()
    hs_copy(1, 2).start()
    for sub in range(2):
        y_copy(sub).wait_recv()

    def stores(i):
        src, dst = ((hq, hq_hbm), (hk, hk_hbm), (hv, hv_hbm), (ho, ho_hbm))[i]
        return [pltpu.make_async_copy(src, dst, out_sem.at[i])]

    ho[...] += yr[...].astype(F32)
    for cp in stores(3):
        cp.start()
    arrived(1)
    of_query, of_kv = product(other)
    hq[...] += of_query
    hk[...] += of_kv[:, :HD]
    hv[...] += of_kv[:, HD:]
    for i in (0, 1, 2):
        for cp in stores(i):
            cp.start()

    for quarter in (q0, q1, q2, q3):
        quarter.wait_sends()
    for sub in range(2):
        y_copy(sub).wait_send()
    for ref, blocks, sem in (
        (nrm_g, N_DP - 1, nrm_s), (grd_g, 7, gz_s), (grd_g, 8, gs_s), (gkv_g, 7, hz_s), (gkv_g, 8, hs_s),
    ):
        sent = ref.at[pl.ds(0, blocks)]
        pltpu.make_async_copy(sent, sent, sem).wait()
    for i in range(4):
        for cp in stores(i):
            cp.wait()


def hand_over(a, b, c, e, a_out, b_out, c_out, e_out, a_buf, b_buf, c_buf, e_buf, sem):
    arrays = ((a, a_buf, a_out), (e, e_buf, e_out), (b, b_buf, b_out), (c, c_buf, c_out))
    loads, stores = [], []
    for i, (src, buf, dst) in enumerate(arrays):
        for part in range(2):
            rows = pl.ds(part * (C // 2), C // 2)
            loads.append(
                pltpu.make_async_copy(src.at[rows], buf.at[rows], sem.at[0, 2 * i + part])
            )
            stores.append(
                pltpu.make_async_copy(buf.at[rows], dst.at[rows], sem.at[1, 2 * i + part])
            )
    for load in loads:
        load.start()
    for load, store in zip(loads, stores):
        load.wait()
        store.start()
    for store in stores:
        store.wait()


def tables():
    frequency = np.exp(
        np.float32(-math.log(10000.0)) * np.arange(HD // 2, dtype=np.float32) * np.float32(2.0)
        / np.float32(HD)
    ).astype(np.float32)
    angles = np.arange(SEQ, dtype=np.float32)[:, None] * frequency[None, :]
    cosine = np.cos(angles).astype(np.float32)
    sine = np.sin(angles).astype(np.float32)
    return np.concatenate([cosine, cosine], 1), np.concatenate([-sine, sine], 1)


def local(
    tokens, target, norm_gain, w_query, w_key, w_value, w_out, t_query, t_key, t_value, t_out
):
    cos_t, sin_t = tables()
    any_spec = pl.BlockSpec(memory_space=pl.ANY)
    vmem = pl.BlockSpec(memory_space=pltpu.VMEM)
    dma = pltpu.SemaphoreType.DMA
    block = (2 * SEQ, C // 2)
    scratch = [
        pltpu.VMEM((C, QW), F32),
        pltpu.VMEM((C, HD), F32),
        pltpu.VMEM((C, HD), F32),
        pltpu.VMEM((C, QW), F32),
        pltpu.VMEM((SEQ, D), BF16),
        pltpu.VMEM((SEQ, 2 * C), BF16),
        pltpu.VMEM((N_DP, C, QW), BF16),
        pltpu.VMEM((N_DP, C, HD), BF16),
        pltpu.VMEM((N_DP, C, HD), BF16),
        pltpu.VMEM((N_DP, QW, C), BF16),
        pltpu.VMEM((N_DP, SEQ, C), BF16),
        pltpu.VMEM((N_DP, SEQ, C), BF16),
        pltpu.VMEM((2 * SEQ, QW), BF16),
        pltpu.VMEM((N_T, C, QW), BF16),
        pltpu.VMEM((2, 2, 2, SEQ, QW), BF16),
        pltpu.VMEM((2, 2, C, QW), BF16),
        pltpu.VMEM((C, QW), BF16),
        pltpu.VMEM((N_DP, SEQ, QW), BF16),
        pltpu.VMEM((N_DP, SEQ, 2 * HD), BF16),
        pltpu.VMEM((4, 2, 4) + block, BF16),
        pltpu.VMEM((4, 2, 2, SEQ, C // 2), BF16),
        pltpu.VMEM((4, 2, 2) + block, BF16),
        pltpu.VMEM((7,) + block, BF16),
        pltpu.VMEM((4, N_T) + block, BF16),
        pltpu.VMEM((2 * SEQ, QW), F32),
        pltpu.VMEM((SEQ, QW + 2 * HD), F32),
        pltpu.VMEM((HEADS * SEQ, SEQ), F32),
        pltpu.VMEM((HEADS * SEQ, SEQ), F32),
        pltpu.VMEM((2 * HEADS * SEQ, HD), BF16),
        pltpu.VMEM((4, SEQ, HD), BF16),
        dma((2,)), dma((4,)), dma((3, 4)), dma,
        dma, dma((N_DP,)), dma((2,)), dma((N_T, 2)), dma((2,)), dma((2, 2, 6)), dma((2,)), dma((2,)),
        dma, dma((2, 4)), dma, dma, dma((2, 4)), dma, dma((4,)), dma((4,)), dma, dma((2, 4)),
        dma((4,)), dma((4, 2, 6)), dma((7,)), dma((4,)), dma((4, 9)),
    ]
    shapes = tuple(jax.ShapeDtypeStruct((C, n), F32) for n in (QW, HD, HD, QW))
    results = pl.pallas_call(
        kernel,
        out_shape=shapes,
        in_specs=[
            any_spec, any_spec, vmem, any_spec, any_spec, any_spec, any_spec,
            vmem, vmem, vmem, vmem, vmem, vmem,
        ],
        out_specs=(any_spec,) * 4,
        scratch_shapes=scratch,
        compiler_params=pltpu.CompilerParams(
            collective_id=0, has_side_effects=True, vmem_limit_bytes=62 * 1024 * 1024
        ),
        cost_estimate=pl.CostEstimate(
            flops=10_000_000_000, bytes_accessed=26_000_000, transcendentals=65536
        ),
        name="hvp",
    )(
        tokens, target, norm_gain.reshape(1, D), w_query.reshape(N_DP, C, QW),
        w_key.reshape(N_DP, C, HD), w_value.reshape(N_DP, C, HD), w_out,
        t_query.reshape(1, QW), t_key.reshape(1, HD), t_value.reshape(1, HD),
        t_out.reshape(1, D), jnp.asarray(cos_t), jnp.asarray(sin_t),
    )
    return pl.pallas_call(
        hand_over,
        out_shape=shapes,
        in_specs=[any_spec] * 4,
        out_specs=(any_spec,) * 4,
        scratch_shapes=[pltpu.VMEM((C, n), F32) for n in (QW, HD, HD, QW)] + [dma((2, 8))],
        compiler_params=pltpu.CompilerParams(vmem_limit_bytes=62 * 1024 * 1024),
        name="results",
    )(*results)


def solution(mesh):
    return jax.shard_map(
        local,
        mesh=mesh,
        in_specs=(
            P("dp", None),
            P("dp", None),
            P(),
            P(None, "tensor"),
            P(None, "tensor"),
            P(None, "tensor"),
            P("tensor", None),
            P("tensor"),
            P("tensor"),
            P("tensor"),
            P(),
        ),
        out_specs=(P("dp", "tensor"), P("dp", "tensor"), P("dp", "tensor"), P("dp", "tensor")),
        check_vma=False,
    )
```

```python
import functools
import math

import jax
import jax.numpy as jnp
import numpy as np
from jax import lax
from jax.experimental import pallas as pl
from jax.experimental.pallas import tpu as pltpu
from jax.sharding import PartitionSpec as P

HD = 128
HEADS = 4
SEQ = 128
D = 8192
QW = HEADS * HD
N_DP = 16
N_T = 8
C = 512
EPS = 1e-05
F32 = jnp.float32
BF16 = jnp.bfloat16
MESH = pl.DeviceIdType.MESH


def mm(a, b):
    return lax.dot_general(
        a.astype(BF16), b.astype(BF16), (((1,), (0,)), ((), ())), preferred_element_type=F32
    )


def mm_nt(a, b):
    return lax.dot_general(
        a.astype(BF16), b.astype(BF16), (((1,), (1,)), ((), ())), preferred_element_type=F32
    )


def mm_tn(a, b):
    return lax.dot_general(
        a.astype(BF16), b.astype(BF16), (((0,), (0,)), ((), ())), preferred_element_type=F32
    )


def mm_nt_wide(a, b):
    a_hi = a.astype(BF16)
    b_hi = b.astype(BF16)
    a_lo = (a - a_hi.astype(F32)).astype(BF16)
    b_lo = (b - b_hi.astype(F32)).astype(BF16)
    return mm_nt(a_hi, b_hi) + (mm_nt(a_hi, b_lo) + mm_nt(a_lo, b_hi))


def swap_halves(x):
    return jnp.concatenate([x[:, HD // 2 :], x[:, : HD // 2]], axis=1)


def stack_heads(x):
    return jnp.concatenate([x[:, h * HD : (h + 1) * HD] for h in range(HEADS)], axis=0)


def kernel(
    tok_hbm, tgt_hbm, gain, wq_hbm, wk_hbm, wv_hbm, wo_hbm, tq, tk, tv, t_out, cos_t, sin_t,
    hq_hbm, hk_hbm, hv_hbm, ho_hbm,
    hq, hk, hv, ho, tok, tgt, wq, wk, wv, wo, nrm, nrm_g, att, sib, zf, zr, yr, grd_g, gkv_g,
    pq, pf, pv, pc, r_all, g_acc, proj,
    prob, tprob, rot_q, kv,
    in_sem, out_sem, wqkv_sem, wo_sem,
    nrm_s, nrm_r, sib_s, sib_r, z_s, z_r, y_s, y_r,
    gz_s, gz_r, gy_r, gs_s, gs_r, hz_s, hz_r, hy_r, hs_s, hs_r,
    rs_s, rs_r, cr_r, ga_s, ga_r,
):
    d = lax.axis_index("dp")
    t = lax.axis_index("tensor")
    x = lax.rem(t, 4)
    y = t // 4
    core = lax.rem(d, 2)
    z = lax.rem(d // 2, 4)
    y_hi = d // 8

    def dev(ry, rz, rc):
        return (lax.rem(y_hi + ry, 2) * 4 + lax.rem(z + rz, 4)) * 2 + lax.rem(core + rc, 2)

    def at(dy, dx):
        return lax.rem(y + dy, 2) * 4 + lax.rem(x + dx, 4)

    def remote(src, dst, s_sem, r_sem, **where):
        return pltpu.make_async_remote_copy(
            src_ref=src, dst_ref=dst, send_sem=s_sem, recv_sem=r_sem,
            device_id=where, device_id_type=MESH,
        )

    bar = pltpu.get_barrier_semaphore()

    @pl.loop(1, N_DP)
    def _(r):
        pl.semaphore_signal(
            bar, inc=1, device_id={"dp": lax.rem(d + r, N_DP)}, device_id_type=MESH
        )

    for dy, dx in ((1, 0), (0, 1), (0, 2), (0, 3)):
        pl.semaphore_signal(bar, inc=1, device_id={"tensor": at(dy, dx)}, device_id_type=MESH)

    tok_copy = pltpu.make_async_copy(tok_hbm, tok, in_sem.at[0])
    tok_copy.start()
    tgt_copy = pltpu.make_async_copy(
        tgt_hbm.at[:, pl.ds(pl.multiple_of(t * 2 * C, 2 * C), 2 * C)], tgt, in_sem.at[1]
    )

    GROUP = 4

    def w_copies(g):
        part = pl.ds(g * GROUP, GROUP)
        return [
            pltpu.make_async_copy(src.at[part], dst.at[part], wqkv_sem.at[i, g])
            for i, (src, dst) in enumerate(((wq_hbm, wq), (wk_hbm, wk), (wv_hbm, wv)))
        ]

    def wo_copy(c):
        return pltpu.make_async_copy(
            wo_hbm.at[:, pl.ds(pl.multiple_of(c * C, C), C)], wo.at[c], wo_sem
        )

    @pl.loop(0, N_DP // GROUP)
    def _(g):
        for cp in w_copies(g):
            cp.start()

    tgt_copy.start()

    @pl.loop(0, N_DP)
    def _(c):
        wo_copy(c).start()

    tok_copy.wait()

    def square_step(c, acc):
        v = tok[:, pl.ds(pl.multiple_of(c * C, C), C)].astype(F32)
        v = v * v
        return acc + ((v[:, :HD] + v[:, HD : 2 * HD]) + (v[:, 2 * HD : 3 * HD] + v[:, 3 * HD :]))

    squares = lax.fori_loop(0, N_DP, square_step, jnp.zeros((SEQ, HD), F32))
    inv = lax.rsqrt(jnp.sum(squares, axis=1, keepdims=True) * (1.0 / D) + EPS)

    @pl.loop(0, N_DP)
    def _(c):
        cols = pl.ds(pl.multiple_of(c * C, C), C)
        nrm[c] = (tok[:, cols].astype(F32) * inv * gain[:, cols]).astype(BF16)

    nrm_g[d] = nrm[d]

    pl.semaphore_wait(bar, N_DP - 1 + 4)

    def nrm_copy(ry, rz, rc):
        dest = dev(ry, rz, rc)
        return remote(nrm.at[dest], nrm_g.at[d], nrm_s, nrm_r.at[ry], dp=dest)

    early = [(0, rz, rc) for rz in (1, 3, 2) for rc in (0, 1)] + [(0, 0, 1)]
    crossing = [[(1, rz, rc) for rc in (0, 1)] for rz in (2, 1, 3, 0)]
    everyone = early + sum(crossing, [])

    def nrm_cross(i):
        for rel in crossing[i]:
            nrm_copy(*rel).start()

    for rel in early:
        nrm_copy(*rel).start()
    nrm_cross(0)

    @pl.loop(0, N_DP // GROUP)
    def _(g):
        total = [jnp.zeros((SEQ, n), F32) for n in (QW, HD, HD)]
        for cp in w_copies(g):
            cp.wait()
        for i in range(GROUP):
            c = g * GROUP + i
            lhs = nrm[c]
            total = [a + mm(lhs, w[c]) for a, w in zip(total, (wq, wk, wv))]

        @pl.when(g == 0)
        def _():
            proj[...] = jnp.concatenate(total, axis=1)

        @pl.when(g > 0)
        def _():
            proj[...] += jnp.concatenate(total, axis=1)

    cos1 = cos_t[...]
    sin1 = sin_t[...]
    cos4 = jnp.concatenate([cos1] * HEADS, axis=0)
    sin4 = jnp.concatenate([sin1] * HEADS, axis=0)
    scale = 1.0 / math.sqrt(HD)

    q2 = proj[:, :QW]
    key = proj[:, QW : QW + HD]
    val = proj[:, QW + HD :]
    tval = val * tv[...]
    qs = stack_heads(q2)
    tqs = stack_heads(q2 * tq[...])
    rq = qs * cos4 + swap_halves(qs) * sin4
    trq = tqs * cos4 + swap_halves(tqs) * sin4
    tkey = key * tk[...]
    rk = key * cos1 + swap_halves(key) * sin1
    trk = tkey * cos1 + swap_halves(tkey) * sin1
    rot_q[...] = jnp.concatenate([rq.astype(BF16), trq.astype(BF16)], axis=0)
    kv[0] = rk.astype(BF16)
    kv[1] = trk.astype(BF16)
    kv[2] = val.astype(BF16)
    kv[3] = tval.astype(BF16)
    scores = mm_nt_wide(rq, rk) * scale
    tscores = (mm_nt_wide(trq, rk) + mm_nt_wide(rq, trk)) * scale
    row = lax.rem(lax.broadcasted_iota(jnp.int32, (HEADS * SEQ, SEQ), 0), SEQ)
    col = lax.broadcasted_iota(jnp.int32, (HEADS * SEQ, SEQ), 1)
    scores = jnp.where(row >= col, scores, -1e30)
    e = jnp.exp(scores - jnp.max(scores, axis=1, keepdims=True))
    p = e / jnp.sum(e, axis=1, keepdims=True)
    tp = p * (tscores - jnp.sum(p * tscores, axis=1, keepdims=True))
    prob[...] = p
    tprob[...] = tp
    o = mm(p, val)
    to = mm(tp, val) + mm(p, tval)
    for h in range(HEADS):
        att[:SEQ, h * HD : (h + 1) * HD] = to[h * SEQ : (h + 1) * SEQ].astype(BF16)
        att[SEQ:, h * HD : (h + 1) * HD] = o[h * SEQ : (h + 1) * SEQ].astype(BF16)

    pltpu.make_async_copy(wo, wo, wo_sem).wait()

    W = C // 2

    def t_cols(c, sub):
        return t_out[:, pl.ds(pl.multiple_of(c * C + sub * W, W), W)]

    class Quarter:
        def __init__(self, q, y_first, base):
            self.q, self.half, self.sub, self.y_first, self.base = q, q // 2, q % 2, y_first, base
            self.cols = slice(self.sub * W, (self.sub + 1) * W)

        def part(self, dy, dx):
            c = at(dy, dx) * 2 + self.half
            rows = mm(att[...], wo[c, :, self.cols])
            pq[self.q, dy, dx, :SEQ, :] = rows[SEQ:].astype(BF16)
            pq[self.q, dy, dx, SEQ:, :] = (rows[:SEQ] + rows[SEQ:] * t_cols(c, self.sub)).astype(BF16)

        def ring(self, dy, k):
            dx, upper, step = ((2, 0, 1), (2, 1, 3), (1, 1, 1), (3, 0, 3), (1, 0, 1), (3, 1, 3))[k]
            rows = pl.ds(upper * SEQ, SEQ)
            side = 0 if step == 1 else 1
            dst = pf.at[self.q, dy, side] if k < 2 else pv.at[self.q, dy, side, rows]
            return remote(
                pq.at[self.q, dy, dx, rows], dst, rs_s.at[self.q], rs_r.at[self.q, dy, min(k, 2)],
                tensor=at(0, step),
            )

        def cross(self, dx):
            slot = self.base + dx
            return remote(
                pq.at[self.q, 1, dx], pc.at[slot], rs_s.at[self.q], cr_r.at[slot], tensor=at(1, 0)
            )

        def add(self, dx, rows, dy, value):
            old = pq[self.q, dy, dx, rows].astype(F32)
            pq[self.q, dy, dx, rows] = (old + value.astype(F32)).astype(BF16)

        def relay(self, dy):
            self.ring(dy, 0).wait_recv()
            self.add(1, slice(0, SEQ), dy, pf[self.q, dy, 0])
            self.ring(dy, 4).start()
            self.ring(dy, 1).wait_recv()
            self.add(3, slice(SEQ, 2 * SEQ), dy, pf[self.q, dy, 1])
            self.ring(dy, 5).start()

        def row_sum(self, dy):
            came = pv.at[self.q, dy]
            pltpu.make_async_copy(came, came, rs_r.at[self.q, dy, 2]).wait()
            own = pq[self.q, dy, 0].astype(F32)
            return own + pv[self.q, dy, 0].astype(F32) + pv[self.q, dy, 1].astype(F32)

        def gather(self, k, sender=True):
            if self.y_first:
                sent = (t, t, t, at(0, 3), at(0, 1), at(0, 3), at(0, 1), at(0, 2))
                came = (at(1, 0), at(0, 3), at(0, 1), at(0, 2), at(0, 2), at(1, 3), at(1, 1), at(1, 2))
                to = (at(1, 0), at(0, 1), at(0, 3), at(0, 1), at(0, 3)) + (at(1, 0),) * 3
                lower, upper = (3,), (4,)
            else:
                sent = (t, t, t, at(0, 3), at(0, 1), at(1, 0), at(1, 0), at(1, 3), at(1, 1))
                came = (at(1, 0), at(0, 3), at(0, 1), at(0, 2), at(0, 2)) + (
                    at(1, 3), at(1, 1), at(1, 2), at(1, 2),
                )
                to = (at(1, 0),) + (at(0, 1), at(0, 3)) * 4
                lower, upper = (3, 7), (4, 8)
            j = (sent if sender else came)[k]
            ref = r_all.at[self.q, j]
            if k in lower:
                ref = r_all.at[self.q, j, pl.ds(0, SEQ)]
            if k in upper:
                ref = r_all.at[self.q, j, pl.ds(SEQ, SEQ)]
            return remote(ref, ref, ga_s.at[self.q], ga_r.at[self.q, k], tensor=to[k])

        def came(self, *ks):
            for k in ks:
                self.gather(k, False).wait_recv()

        def pass_on(self, *ks):
            for k in ks:
                self.gather(k).start()

        def first(self):
            if self.y_first:
                for dx in (2, 1, 3, 0):
                    self.part(1, dx)
                    self.cross(dx).start()
                for dx in (2, 1, 3, 0):
                    self.part(0, dx)
                return
            for dy in (1, 0):
                for dx, ks in ((2, (0, 1)), (1, (2,)), (3, (3,))):
                    self.part(dy, dx)
                    for k in ks:
                        self.ring(dy, k).start()
            self.part(1, 0)
            self.part(0, 0)

        def second(self):
            if self.y_first:
                for dx, ks in ((2, (0, 1)), (1, (2,)), (3, (3,))):
                    self.cross(dx).wait_recv()
                    self.add(dx, slice(None), 0, pc[self.base + dx])
                    for k in ks:
                        self.ring(0, k).start()
                return
            self.relay(1)
            self.relay(0)

        def third(self):
            if self.y_first:
                self.relay(0)
                return
            pq[self.q, 1, 0] = self.row_sum(1).astype(BF16)
            self.cross(0).start()

        def finish(self):
            total = self.row_sum(0)
            self.cross(0).wait_recv()
            total = total + pc[self.base].astype(F32)
            c = t * 2 + self.half
            base = tok[:, pl.ds(pl.multiple_of(c * C + self.sub * W, W), W)].astype(F32)
            aim = tgt[:, self.q * W : (self.q + 1) * W].astype(F32)
            r_all[self.q, t, :SEQ, :] = (base + total[:SEQ] - aim).astype(BF16)
            r_all[self.q, t, SEQ:, :] = total[SEQ:].astype(BF16)
            self.pass_on(*((1, 2, 0) if self.y_first else (0, 1, 2)))

        def sib_copy(self, j):
            rows = pl.ds(self.sub * W, W)
            return remote(
                wq.at[self.half * N_T + j, rows], sib.at[j, rows], sib_s.at[self.sub],
                sib_r.at[j, self.sub], dp=dev(0, 0, 1),
            )

        def use(self, *blocks):
            for j in blocks:
                rows = r_all[self.q, j]
                wq[self.half * N_T + j, self.cols] = mm_tn(rows, att[...]).astype(BF16)

                @pl.when(core != self.half)
                def _():
                    self.sib_copy(j).start()

                c = 2 * j + self.half
                res = rows[:SEQ]
                back = (rows[SEQ:].astype(F32) + res.astype(F32) * t_cols(c, self.sub)).astype(BF16)
                g_acc[...] += mm_nt(jnp.concatenate([res, back], axis=0), wo[c, :, self.cols])

        def z_copy(self, j, k):
            dx, upper, step = ((2, 0, 1), (2, 1, 3), (1, 1, 1), (3, 0, 3), (1, 0, 1), (3, 1, 3))[k]
            yd = j // 4
            rows = pl.ds(self.sub * W + upper * SEQ, SEQ)
            side = 0 if step == 1 else 1
            dst = zf.at[self.sub, yd, side] if k < 2 else zr.at[yd, side, rows]
            return remote(
                wq.at[self.half * N_T + j, rows], dst, z_s.at[self.sub],
                z_r.at[self.sub, yd, min(k, 2)], dp=dev(0, step, 0),
            )

        def combine(self, *blocks):
            @pl.when(core == self.half)
            def _():
                for j in blocks:
                    slot = self.half * N_T + j
                    self.sib_copy(j).wait_recv()
                    both = wq[slot, self.cols].astype(F32) + sib[j, self.cols].astype(F32)
                    wq[slot, self.cols] = both.astype(BF16)
                    rel = lax.rem(lax.rem(j, 4) + 4 - z, 4)
                    for want, ks in ((2, (0, 1)), (1, (2,)), (3, (3,))):

                        @pl.when(rel == want)
                        def _():
                            for k in ks:
                                self.z_copy(j, k).start()

        def z_relay(self, *blocks):
            @pl.when(core == self.half)
            def _():
                for j in blocks:
                    slot = self.half * N_T + j
                    rel = lax.rem(lax.rem(j, 4) + 4 - z, 4)
                    for want, side in ((1, 0), (3, 1)):

                        @pl.when(rel == want)
                        def _():
                            self.z_copy(j, side).wait_recv()
                            lo = self.sub * W + side * SEQ
                            old = wq[slot, lo : lo + SEQ].astype(F32)
                            new = old + zf[self.sub, j // 4, side].astype(F32)
                            wq[slot, lo : lo + SEQ] = new.astype(BF16)
                            self.z_copy(j, 4 + side).start()

        def near(self):
            self.came(1)
            self.pass_on(*((3, 5) if self.y_first else (3,)))
            self.came(2)
            self.pass_on(*((4, 6) if self.y_first else (4,)))
            if not self.y_first:
                self.came(0)
                self.pass_on(5, 6)

        def far(self):
            if self.y_first:
                self.came(3, 4)
                self.pass_on(7)
            else:
                self.came(5)
                self.pass_on(7)
                self.came(6)
                self.pass_on(8)

        def own(self):
            self.use(t)

        def own_sum(self):
            self.combine(t)

        def near_use(self):
            self.use(at(0, 3), at(0, 1))
            if self.y_first:
                self.came(0)
            self.use(at(1, 0))

        def next_use(self):
            self.combine(at(0, 3), at(0, 1), at(1, 0))
            if not self.y_first:
                self.came(3, 4)
            self.use(at(0, 2))

        def far_use(self):
            if self.y_first:
                self.came(5, 6)
            self.combine(at(0, 2))
            self.use(at(1, 3), at(1, 1))

        def last_use(self):
            self.came(*((7,) if self.y_first else (7, 8)))
            self.use(at(1, 2))
            self.combine(at(1, 3), at(1, 1))

        def relay_near(self):
            self.z_relay(t, at(0, 3), at(0, 1))

        def last(self):
            self.combine(at(1, 2))
            self.z_relay(at(1, 0), at(0, 2))

        def relay_far(self):
            self.z_relay(at(1, 3), at(1, 1))

        def relay_last(self):
            self.z_relay(at(1, 2))

        def wait_sends(self):
            sent = r_all.at[self.q, pl.ds(0, 7)]
            pltpu.make_async_copy(sent, sent, rs_s.at[self.q]).wait()
            pltpu.make_async_copy(sent, sent, ga_s.at[self.q]).wait()

            @pl.when(core != self.half)
            def _():
                to_core = wq.at[pl.ds(0, 4)]
                pltpu.make_async_copy(to_core, to_core, sib_s.at[self.sub]).wait()

            @pl.when(core == self.half)
            def _():
                along_z = wq.at[pl.ds(0, 3)]
                pltpu.make_async_copy(along_z, along_z, z_s.at[self.sub]).wait()

    q0 = Quarter(0, False, 0)
    q1 = Quarter(2, False, 1)
    q2 = Quarter(1, True, 2)
    q3 = Quarter(3, False, 6)
    other = lax.rem(y_hi + 1, 2)

    def z_sum(yd, sub):
        pltpu.make_async_copy(zr.at[yd, 0], zr.at[yd, 0], z_r.at[sub, yd, 2]).wait()
        rows = slice(sub * W, (sub + 1) * W)
        total = wq[core * N_T + yd * 4 + z, rows].astype(F32)
        return total + zr[yd, 0, rows].astype(F32) + zr[yd, 1, rows].astype(F32)

    def y_copy(sub):
        rows = pl.ds(sub * W, W)
        return remote(
            wq.at[core * N_T + other * 4 + z, rows], yr.at[rows], y_s.at[sub], y_r.at[sub],
            dp=dev(1, 0, 0),
        )

    def out_cross(sub):
        wq[core * N_T + other * 4 + z, sub * W : (sub + 1) * W] = z_sum(other, sub).astype(BF16)
        y_copy(sub).start()

    g_acc[...] = jnp.zeros_like(g_acc)
    tgt_copy.wait()
    q0.first()
    q2.first()
    q0.second()
    q1.first()
    q0.third()
    q1.second()
    q0.finish()
    q2.second()
    q3.first()
    q1.third()
    nrm_cross(1)
    q0.own()
    q0.near()
    q1.finish()
    q1.own()
    q2.third()
    q0.own_sum()
    q0.near_use()
    q3.second()
    nrm_cross(2)
    q1.own_sum()
    q0.next_use()
    q0.far()
    q0.far_use()
    q1.near()
    q1.near_use()
    q2.finish()
    q2.own()
    q0.relay_near()
    q3.third()
    q0.last_use()
    q2.own_sum()
    q0.last()
    q1.far()
    q3.finish()
    q1.next_use()
    q2.near()
    q3.own()
    q1.far_use()
    q2.near_use()
    q2.far()
    q3.near()
    q3.own_sum()
    q0.relay_far()
    q1.relay_near()
    q1.last_use()
    q0.relay_last()
    q2.next_use()
    q1.last()
    q2.far_use()
    q3.near_use()
    q3.far()
    q1.relay_far()
    nrm_cross(3)
    q2.relay_near()
    q2.last_use()
    q3.next_use()
    q2.last()
    q1.relay_last()
    out_cross(0)
    q3.far_use()
    q3.last_use()

    key = kv[0]
    tkey = kv[1]
    val = kv[2]
    tval = kv[3]
    g1 = stack_heads(g_acc[:SEQ]).astype(BF16)
    g2 = stack_heads(g_acc[SEQ:]).astype(BF16)
    p = prob[...]
    tp = tprob[...]
    dpr = mm_nt(g1, val)
    tdpr = mm_nt(g2, val) + mm_nt(g1, tval)
    tval_grad = mm_tn(jnp.concatenate([tp, p], axis=0), jnp.concatenate([g1, g2], axis=0))
    gkv_g[d, :, HD:] = tval_grad.astype(BF16)
    dpr = dpr - jnp.sum(p * dpr, axis=1, keepdims=True)
    tdpr = tdpr - jnp.sum(tp * dpr + p * tdpr, axis=1, keepdims=True)
    ds = (p * dpr).astype(BF16)
    tds = (tp * dpr + p * tdpr).astype(BF16)
    both = jnp.concatenate([tds, ds], axis=0)
    trk_grad = mm_tn(both, rot_q[...]) * scale
    trk_grad = trk_grad * cos1 - swap_halves(trk_grad) * sin1
    gkv_g[d, :, :HD] = trk_grad.astype(BF16)
    trq_grad = (mm(tds, key) + mm(ds, tkey)) * scale
    trq_grad = trq_grad * cos4 - swap_halves(trq_grad) * sin4
    for h in range(HEADS):
        grd_g[d, :, h * HD : (h + 1) * HD] = trq_grad[h * SEQ : (h + 1) * SEQ].astype(BF16)

    def gs_copy(ry, rz):
        b = dev(ry, 4 - rz, 0)
        return remote(
            grd_g.at[b], grd_g.at[b], gs_s, gs_r.at[ry], dp=dev(0, 0, 1)
        )

    def gz_copy(ry, k, sender=True):
        step = (1, 3, 1, 3)[k]
        back = (0, 0, 1, 1)[k] if sender else (1, 1, 2, 2)[k]
        b = dev(ry, 4 - back if step == 1 else back, 0)
        h = SEQ // 2
        rows = (pl.ds(0, SEQ), pl.ds(0, SEQ), pl.ds(0, h), pl.ds(h, h))[k]
        ref = grd_g.at[b, rows]
        return remote(ref, ref, gz_s, gz_r.at[ry, k], dp=dev(0, step, 0))

    def gy_copy(b):
        return remote(grd_g.at[b], grd_g.at[b], gz_s, gy_r, dp=dev(1, 0, 0))

    def hs_copy(ry, rz):
        b = dev(ry, 4 - rz, 0)
        return remote(
            gkv_g.at[b], gkv_g.at[b], hs_s, hs_r.at[ry], dp=dev(0, 0, 1)
        )

    def hz_copy(k, sender=True):
        step = (1, 3, 1, 3)[k]
        back = (0, 0, 1, 1)[k] if sender else (1, 1, 2, 2)[k]
        b = dev(0, 4 - back if step == 1 else back, 0)
        h = SEQ // 2
        rows = (pl.ds(0, SEQ), pl.ds(0, SEQ), pl.ds(0, h), pl.ds(h, h))[k]
        ref = gkv_g.at[b, rows]
        return remote(ref, ref, hz_s, hz_r.at[k], dp=dev(0, step, 0))

    def hy_copy(rz, sender=True):
        b = dev(0 if sender else 1, 4 - rz, 0)
        return remote(gkv_g.at[b], gkv_g.at[b], hz_s, hy_r.at[rz], dp=dev(1, 0, 0))

    def pass_on(ry):
        for k, rz in ((0, 1), (1, 3)):
            gz_copy(ry, k, False).wait_recv()
            gz_copy(ry, k + 2).start()
            gs_copy(ry, rz).start()

    gy_copy(d).start()
    hy_copy(0).start()
    hz_copy(0).start()
    hz_copy(1).start()
    gz_copy(0, 0).start()
    gz_copy(0, 1).start()
    hs_copy(0, 0).start()
    gs_copy(0, 0).start()
    q3.relay_near()
    q3.last()
    q2.relay_far()
    q2.relay_last()
    for k, rz in ((0, 1), (1, 3)):
        hz_copy(k, False).wait_recv()
        hz_copy(k + 2).start()
        hy_copy(rz).start()
        hs_copy(0, rz).start()
    gy_copy(dev(1, 0, 0)).wait_recv()
    gz_copy(1, 0).start()
    gz_copy(1, 1).start()
    gs_copy(1, 0).start()
    q3.relay_far()
    pass_on(0)
    q3.relay_last()
    hz_copy(2, False).wait_recv()
    hz_copy(3, False).wait_recv()
    hy_copy(2).start()
    hs_copy(0, 2).start()
    hy_copy(0, False).wait_recv()
    hs_copy(1, 0).start()
    out_cross(1)
    pass_on(1)
    for rz in (1, 3):
        hy_copy(rz, False).wait_recv()
        hs_copy(1, rz).start()

    def product(first):
        rows = pl.ds(first * N_T, N_T)
        lhs = nrm_g[rows].reshape(N_T * SEQ, C)
        of_query = mm_tn(lhs, grd_g[rows].reshape(N_T * SEQ, QW))
        return of_query, mm_tn(lhs, gkv_g[rows].reshape(N_T * SEQ, 2 * HD))

    def arrived(ry):
        for ref, blocks, sem in ((nrm_g, N_T - 1 + ry, nrm_r), (grd_g, 4, gs_r), (gkv_g, 4, hs_r)):
            came = ref.at[pl.ds(0, blocks)]
            pltpu.make_async_copy(came, came, sem.at[ry]).wait()

    gz_copy(0, 2, False).wait_recv()
    gz_copy(0, 3, False).wait_recv()
    gs_copy(0, 2).start()
    for sub in range(2):
        ho[sub * W : (sub + 1) * W, :] = z_sum(y_hi, sub)
    arrived(0)
    of_query, of_kv = product(y_hi)
    hq[...] = of_query
    hk[...] = of_kv[:, :HD]
    hv[...] = of_kv[:, HD:]
    gz_copy(1, 2, False).wait_recv()
    gz_copy(1, 3, False).wait_recv()
    gs_copy(1, 2).start()
    hy_copy(2, False).wait_recv()
    hs_copy(1, 2).start()
    for sub in range(2):
        y_copy(sub).wait_recv()

    def stores(i):
        src, dst = ((hq, hq_hbm), (hk, hk_hbm), (hv, hv_hbm), (ho, ho_hbm))[i]
        return [pltpu.make_async_copy(src, dst, out_sem.at[i])]

    ho[...] += yr[...].astype(F32)
    for cp in stores(3):
        cp.start()
    arrived(1)
    of_query, of_kv = product(other)
    hq[...] += of_query
    hk[...] += of_kv[:, :HD]
    hv[...] += of_kv[:, HD:]
    for i in (0, 1, 2):
        for cp in stores(i):
            cp.start()

    for quarter in (q0, q1, q2, q3):
        quarter.wait_sends()
    for sub in range(2):
        y_copy(sub).wait_send()
    for ref, blocks, sem in (
        (nrm_g, N_DP - 1, nrm_s), (grd_g, 7, gz_s), (grd_g, 8, gs_s), (gkv_g, 7, hz_s), (gkv_g, 8, hs_s),
    ):
        sent = ref.at[pl.ds(0, blocks)]
        pltpu.make_async_copy(sent, sent, sem).wait()
    for i in range(4):
        for cp in stores(i):
            cp.wait()


def hand_over(a, b, c, e, a_out, b_out, c_out, e_out, a_buf, b_buf, c_buf, e_buf, sem):
    arrays = ((a, a_buf, a_out), (e, e_buf, e_out), (b, b_buf, b_out), (c, c_buf, c_out))
    loads, stores = [], []
    for i, (src, buf, dst) in enumerate(arrays):
        for part in range(2):
            rows = pl.ds(part * (C // 2), C // 2)
            loads.append(
                pltpu.make_async_copy(src.at[rows], buf.at[rows], sem.at[0, 2 * i + part])
            )
            stores.append(
                pltpu.make_async_copy(buf.at[rows], dst.at[rows], sem.at[1, 2 * i + part])
            )
    for load in loads:
        load.start()
    for load, store in zip(loads, stores):
        load.wait()
        store.start()
    for store in stores:
        store.wait()


def tables():
    frequency = np.exp(
        np.float32(-math.log(10000.0)) * np.arange(HD // 2, dtype=np.float32) * np.float32(2.0)
        / np.float32(HD)
    ).astype(np.float32)
    angles = np.arange(SEQ, dtype=np.float32)[:, None] * frequency[None, :]
    cosine = np.cos(angles).astype(np.float32)
    sine = np.sin(angles).astype(np.float32)
    return np.concatenate([cosine, cosine], 1), np.concatenate([-sine, sine], 1)


def local(
    tokens, target, norm_gain, w_query, w_key, w_value, w_out, t_query, t_key, t_value, t_out
):
    cos_t, sin_t = tables()
    any_spec = pl.BlockSpec(memory_space=pl.ANY)
    vmem = pl.BlockSpec(memory_space=pltpu.VMEM)
    dma = pltpu.SemaphoreType.DMA
    block = (2 * SEQ, C // 2)
    scratch = [
        pltpu.VMEM((C, QW), F32),
        pltpu.VMEM((C, HD), F32),
        pltpu.VMEM((C, HD), F32),
        pltpu.VMEM((C, QW), F32),
        pltpu.VMEM((SEQ, D), BF16),
        pltpu.VMEM((SEQ, 2 * C), BF16),
        pltpu.VMEM((N_DP, C, QW), BF16),
        pltpu.VMEM((N_DP, C, HD), BF16),
        pltpu.VMEM((N_DP, C, HD), BF16),
        pltpu.VMEM((N_DP, QW, C), BF16),
        pltpu.VMEM((N_DP, SEQ, C), BF16),
        pltpu.VMEM((N_DP, SEQ, C), BF16),
        pltpu.VMEM((2 * SEQ, QW), BF16),
        pltpu.VMEM((N_T, C, QW), BF16),
        pltpu.VMEM((2, 2, 2, SEQ, QW), BF16),
        pltpu.VMEM((2, 2, C, QW), BF16),
        pltpu.VMEM((C, QW), BF16),
        pltpu.VMEM((N_DP, SEQ, QW), BF16),
        pltpu.VMEM((N_DP, SEQ, 2 * HD), BF16),
        pltpu.VMEM((4, 2, 4) + block, BF16),
        pltpu.VMEM((4, 2, 2, SEQ, C // 2), BF16),
        pltpu.VMEM((4, 2, 2) + block, BF16),
        pltpu.VMEM((7,) + block, BF16),
        pltpu.VMEM((4, N_T) + block, BF16),
        pltpu.VMEM((2 * SEQ, QW), F32),
        pltpu.VMEM((SEQ, QW + 2 * HD), F32),
        pltpu.VMEM((HEADS * SEQ, SEQ), F32),
        pltpu.VMEM((HEADS * SEQ, SEQ), F32),
        pltpu.VMEM((2 * HEADS * SEQ, HD), BF16),
        pltpu.VMEM((4, SEQ, HD), BF16),
        dma((2,)), dma((4,)), dma((3, 4)), dma,
        dma, dma((2,)), dma((2,)), dma((N_T, 2)), dma((2,)), dma((2, 2, 3)), dma((2,)), dma((2,)),
        dma, dma((2, 4)), dma, dma, dma((2,)), dma, dma((4,)), dma((4,)), dma, dma((2,)),
        dma((4,)), dma((4, 2, 3)), dma((7,)), dma((4,)), dma((4, 9)),
    ]
    shapes = tuple(jax.ShapeDtypeStruct((C, n), F32) for n in (QW, HD, HD, QW))
    results = pl.pallas_call(
        kernel,
        out_shape=shapes,
        in_specs=[
            any_spec, any_spec, vmem, any_spec, any_spec, any_spec, any_spec,
            vmem, vmem, vmem, vmem, vmem, vmem,
        ],
        out_specs=(any_spec,) * 4,
        scratch_shapes=scratch,
        compiler_params=pltpu.CompilerParams(
            collective_id=0, has_side_effects=True, vmem_limit_bytes=62 * 1024 * 1024
        ),
        cost_estimate=pl.CostEstimate(
            flops=10_000_000_000, bytes_accessed=26_000_000, transcendentals=65536
        ),
        name="hvp",
    )(
        tokens, target, norm_gain.reshape(1, D), w_query.reshape(N_DP, C, QW),
        w_key.reshape(N_DP, C, HD), w_value.reshape(N_DP, C, HD), w_out,
        t_query.reshape(1, QW), t_key.reshape(1, HD), t_value.reshape(1, HD),
        t_out.reshape(1, D), jnp.asarray(cos_t), jnp.asarray(sin_t),
    )
    return pl.pallas_call(
        hand_over,
        out_shape=shapes,
        in_specs=[any_spec] * 4,
        out_specs=(any_spec,) * 4,
        scratch_shapes=[pltpu.VMEM((C, n), F32) for n in (QW, HD, HD, QW)] + [dma((2, 8))],
        compiler_params=pltpu.CompilerParams(vmem_limit_bytes=62 * 1024 * 1024),
        name="results",
    )(*results)


def solution(mesh):
    return jax.shard_map(
        local,
        mesh=mesh,
        in_specs=(
            P("dp", None),
            P("dp", None),
            P(),
            P(None, "tensor"),
            P(None, "tensor"),
            P(None, "tensor"),
            P("tensor", None),
            P("tensor"),
            P("tensor"),
            P("tensor"),
            P(),
        ),
        out_specs=(P("dp", "tensor"), P("dp", "tensor"), P("dp", "tensor"), P("dp", "tensor")),
        check_vma=False,
    )
```

```python
import functools
import math

import jax
import jax.numpy as jnp
import numpy as np
from jax import lax
from jax.experimental import pallas as pl
from jax.experimental.pallas import tpu as pltpu
from jax.sharding import PartitionSpec as P

HD = 128
HEADS = 4
SEQ = 128
D = 8192
QW = HEADS * HD
N_DP = 16
N_T = 8
C = 512
EPS = 1e-05
F32 = jnp.float32
BF16 = jnp.bfloat16
MESH = pl.DeviceIdType.MESH


def mm(a, b):
    return lax.dot_general(
        a.astype(BF16), b.astype(BF16), (((1,), (0,)), ((), ())), preferred_element_type=F32
    )


def mm_nt(a, b):
    return lax.dot_general(
        a.astype(BF16), b.astype(BF16), (((1,), (1,)), ((), ())), preferred_element_type=F32
    )


def mm_tn(a, b):
    return lax.dot_general(
        a.astype(BF16), b.astype(BF16), (((0,), (0,)), ((), ())), preferred_element_type=F32
    )


def mm_nt_wide(a, b):
    a_hi = a.astype(BF16)
    b_hi = b.astype(BF16)
    a_lo = (a - a_hi.astype(F32)).astype(BF16)
    b_lo = (b - b_hi.astype(F32)).astype(BF16)
    return mm_nt(a_hi, b_hi) + (mm_nt(a_hi, b_lo) + mm_nt(a_lo, b_hi))


def swap_halves(x):
    return jnp.concatenate([x[:, HD // 2 :], x[:, : HD // 2]], axis=1)


def stack_heads(x):
    return jnp.concatenate([x[:, h * HD : (h + 1) * HD] for h in range(HEADS)], axis=0)


def kernel(
    tok_hbm, tgt_hbm, gain, wq_hbm, wk_hbm, wv_hbm, wo_hbm, tq, tk, tv, t_out, cos_t, sin_t,
    hq_hbm, hk_hbm, hv_hbm, ho_hbm,
    hq, hk, hv, ho, tok, tgt, wq, wk, wv, wo, nrm, nrm_g, att, sib, zf, zr, yr, grd_g, gkv_g,
    pq, pf, pv, pc, r_all, g_acc, proj,
    prob, tprob, rot_q, kv,
    in_sem, out_sem, wqkv_sem, wo_sem,
    nrm_s, nrm_r, sib_s, sib_r, z_s, z_r, y_s, y_r,
    gz_s, gz_r, gy_r, gs_s, gs_r, hz_s, hz_r, hy_r, hs_s, hs_r,
    rs_s, rs_r, cr_r, ga_s, ga_r,
):
    d = lax.axis_index("dp")
    t = lax.axis_index("tensor")
    x = lax.rem(t, 4)
    y = t // 4
    core = lax.rem(d, 2)
    z = lax.rem(d // 2, 4)
    y_hi = d // 8

    def dev(ry, rz, rc):
        return (lax.rem(y_hi + ry, 2) * 4 + lax.rem(z + rz, 4)) * 2 + lax.rem(core + rc, 2)

    def at(dy, dx):
        return lax.rem(y + dy, 2) * 4 + lax.rem(x + dx, 4)

    def remote(src, dst, s_sem, r_sem, **where):
        return pltpu.make_async_remote_copy(
            src_ref=src, dst_ref=dst, send_sem=s_sem, recv_sem=r_sem,
            device_id=where, device_id_type=MESH,
        )

    bar = pltpu.get_barrier_semaphore()

    @pl.loop(1, N_DP)
    def _(r):
        pl.semaphore_signal(
            bar, inc=1, device_id={"dp": lax.rem(d + r, N_DP)}, device_id_type=MESH
        )

    for dy, dx in ((1, 0), (0, 1), (0, 2), (0, 3)):
        pl.semaphore_signal(bar, inc=1, device_id={"tensor": at(dy, dx)}, device_id_type=MESH)

    tok_copy = pltpu.make_async_copy(tok_hbm, tok, in_sem.at[0])
    tok_copy.start()
    tgt_copy = pltpu.make_async_copy(
        tgt_hbm.at[:, pl.ds(pl.multiple_of(t * 2 * C, 2 * C), 2 * C)], tgt, in_sem.at[1]
    )

    GROUP = 4

    def w_copies(g):
        part = pl.ds(g * GROUP, GROUP)
        return [
            pltpu.make_async_copy(src.at[part], dst.at[part], wqkv_sem.at[i, g])
            for i, (src, dst) in enumerate(((wq_hbm, wq), (wk_hbm, wk), (wv_hbm, wv)))
        ]

    def wo_copy(c):
        return pltpu.make_async_copy(
            wo_hbm.at[:, pl.ds(pl.multiple_of(c * C, C), C)], wo.at[c], wo_sem
        )

    @pl.loop(0, N_DP // GROUP)
    def _(g):
        for cp in w_copies(g):
            cp.start()

    tgt_copy.start()

    @pl.loop(0, N_DP)
    def _(c):
        wo_copy(c).start()

    tok_copy.wait()

    def square_step(c, acc):
        v = tok[:, pl.ds(pl.multiple_of(c * C, C), C)].astype(F32)
        v = v * v
        return acc + ((v[:, :HD] + v[:, HD : 2 * HD]) + (v[:, 2 * HD : 3 * HD] + v[:, 3 * HD :]))

    squares = lax.fori_loop(0, N_DP, square_step, jnp.zeros((SEQ, HD), F32))
    inv = lax.rsqrt(jnp.sum(squares, axis=1, keepdims=True) * (1.0 / D) + EPS)

    @pl.loop(0, N_DP)
    def _(c):
        cols = pl.ds(pl.multiple_of(c * C, C), C)
        nrm[c] = (tok[:, cols].astype(F32) * inv * gain[:, cols]).astype(BF16)

    nrm_g[d] = nrm[d]

    pl.semaphore_wait(bar, N_DP - 1 + 4)

    def nrm_copy(ry, rz, rc):
        dest = dev(ry, rz, rc)
        return remote(nrm.at[dest], nrm_g.at[d], nrm_s, nrm_r.at[ry], dp=dest)

    early = [(0, rz, rc) for rz in (1, 3, 2) for rc in (0, 1)] + [(0, 0, 1)]
    crossing = [[(1, rz, rc) for rc in (0, 1)] for rz in (2, 1, 3, 0)]
    everyone = early + sum(crossing, [])

    def nrm_cross(i):
        for rel in crossing[i]:
            nrm_copy(*rel).start()

    for rel in early:
        nrm_copy(*rel).start()
    nrm_cross(0)

    @pl.loop(0, N_DP // GROUP)
    def _(g):
        total = [jnp.zeros((SEQ, n), F32) for n in (QW, HD, HD)]
        for cp in w_copies(g):
            cp.wait()
        for i in range(GROUP):
            c = g * GROUP + i
            lhs = nrm[c]
            total = [a + mm(lhs, w[c]) for a, w in zip(total, (wq, wk, wv))]

        @pl.when(g == 0)
        def _():
            proj[...] = jnp.concatenate(total, axis=1)

        @pl.when(g > 0)
        def _():
            proj[...] += jnp.concatenate(total, axis=1)

    cos1 = cos_t[...]
    sin1 = sin_t[...]
    cos4 = jnp.concatenate([cos1] * HEADS, axis=0)
    sin4 = jnp.concatenate([sin1] * HEADS, axis=0)
    scale = 1.0 / math.sqrt(HD)

    q2 = proj[:, :QW]
    key = proj[:, QW : QW + HD]
    val = proj[:, QW + HD :]
    tval = val * tv[...]
    qs = stack_heads(q2)
    tqs = stack_heads(q2 * tq[...])
    rq = qs * cos4 + swap_halves(qs) * sin4
    trq = tqs * cos4 + swap_halves(tqs) * sin4
    tkey = key * tk[...]
    rk = key * cos1 + swap_halves(key) * sin1
    trk = tkey * cos1 + swap_halves(tkey) * sin1
    rot_q[...] = jnp.concatenate([rq.astype(BF16), trq.astype(BF16)], axis=0)
    kv[0] = rk.astype(BF16)
    kv[1] = trk.astype(BF16)
    kv[2] = val.astype(BF16)
    kv[3] = tval.astype(BF16)
    scores = mm_nt_wide(rq, rk) * scale
    tscores = (mm_nt_wide(trq, rk) + mm_nt_wide(rq, trk)) * scale
    row = lax.rem(lax.broadcasted_iota(jnp.int32, (HEADS * SEQ, SEQ), 0), SEQ)
    col = lax.broadcasted_iota(jnp.int32, (HEADS * SEQ, SEQ), 1)
    scores = jnp.where(row >= col, scores, -1e30)
    e = jnp.exp(scores - jnp.max(scores, axis=1, keepdims=True))
    p = e / jnp.sum(e, axis=1, keepdims=True)
    tp = p * (tscores - jnp.sum(p * tscores, axis=1, keepdims=True))
    prob[...] = p
    tprob[...] = tp
    o = mm(p, val)
    to = mm(tp, val) + mm(p, tval)
    for h in range(HEADS):
        att[:SEQ, h * HD : (h + 1) * HD] = to[h * SEQ : (h + 1) * SEQ].astype(BF16)
        att[SEQ:, h * HD : (h + 1) * HD] = o[h * SEQ : (h + 1) * SEQ].astype(BF16)

    pltpu.make_async_copy(wo, wo, wo_sem).wait()

    W = C // 2

    def t_cols(c, sub):
        return t_out[:, pl.ds(pl.multiple_of(c * C + sub * W, W), W)]

    class Quarter:
        def __init__(self, q, y_first, base):
            self.q, self.half, self.sub, self.y_first, self.base = q, q // 2, q % 2, y_first, base
            self.cols = slice(self.sub * W, (self.sub + 1) * W)

        def part(self, dy, dx):
            c = at(dy, dx) * 2 + self.half
            rows = mm(att[...], wo[c, :, self.cols])
            pq[self.q, dy, dx, :SEQ, :] = rows[SEQ:].astype(BF16)
            pq[self.q, dy, dx, SEQ:, :] = (rows[:SEQ] + rows[SEQ:] * t_cols(c, self.sub)).astype(BF16)

        def ring(self, dy, k):
            dx, upper, step = ((2, 0, 1), (2, 1, 3), (1, 1, 1), (3, 0, 3), (1, 0, 1), (3, 1, 3))[k]
            rows = pl.ds(upper * SEQ, SEQ)
            side = 0 if step == 1 else 1
            dst = pf.at[self.q, dy, side] if k < 2 else pv.at[self.q, dy, side, rows]
            return remote(
                pq.at[self.q, dy, dx, rows], dst, rs_s.at[self.q], rs_r.at[self.q, dy, min(k, 2)],
                tensor=at(0, step),
            )

        def cross(self, dx):
            slot = self.base + dx
            return remote(
                pq.at[self.q, 1, dx], pc.at[slot], rs_s.at[self.q], cr_r.at[slot], tensor=at(1, 0)
            )

        def add(self, dx, rows, dy, value):
            old = pq[self.q, dy, dx, rows].astype(F32)
            pq[self.q, dy, dx, rows] = (old + value.astype(F32)).astype(BF16)

        def relay(self, dy):
            self.ring(dy, 0).wait_recv()
            self.add(1, slice(0, SEQ), dy, pf[self.q, dy, 0])
            self.ring(dy, 4).start()
            self.ring(dy, 1).wait_recv()
            self.add(3, slice(SEQ, 2 * SEQ), dy, pf[self.q, dy, 1])
            self.ring(dy, 5).start()

        def row_sum(self, dy):
            came = pv.at[self.q, dy]
            pltpu.make_async_copy(came, came, rs_r.at[self.q, dy, 2]).wait()
            own = pq[self.q, dy, 0].astype(F32)
            return own + pv[self.q, dy, 0].astype(F32) + pv[self.q, dy, 1].astype(F32)

        def gather(self, k, sender=True):
            if self.y_first:
                sent = (t, t, t, at(0, 3), at(0, 1), at(0, 3), at(0, 1), at(0, 2))
                came = (at(1, 0), at(0, 3), at(0, 1), at(0, 2), at(0, 2), at(1, 3), at(1, 1), at(1, 2))
                to = (at(1, 0), at(0, 1), at(0, 3), at(0, 1), at(0, 3)) + (at(1, 0),) * 3
                lower, upper = (3,), (4,)
            else:
                sent = (t, t, t, at(0, 3), at(0, 1), at(1, 0), at(1, 0), at(1, 3), at(1, 1))
                came = (at(1, 0), at(0, 3), at(0, 1), at(0, 2), at(0, 2)) + (
                    at(1, 3), at(1, 1), at(1, 2), at(1, 2),
                )
                to = (at(1, 0),) + (at(0, 1), at(0, 3)) * 4
                lower, upper = (3, 7), (4, 8)
            j = (sent if sender else came)[k]
            ref = r_all.at[self.q, j]
            if k in lower:
                ref = r_all.at[self.q, j, pl.ds(0, SEQ)]
            if k in upper:
                ref = r_all.at[self.q, j, pl.ds(SEQ, SEQ)]
            return remote(ref, ref, ga_s.at[self.q], ga_r.at[self.q, k], tensor=to[k])

        def came(self, *ks):
            for k in ks:
                self.gather(k, False).wait_recv()

        def pass_on(self, *ks):
            for k in ks:
                self.gather(k).start()

        def first(self):
            if self.y_first:
                for dx in (2, 1, 3, 0):
                    self.part(1, dx)
                    self.cross(dx).start()
                for dx in (2, 1, 3, 0):
                    self.part(0, dx)
                return
            for dy in (1, 0):
                for dx, ks in ((2, (0, 1)), (1, (2,)), (3, (3,))):
                    self.part(dy, dx)
                    for k in ks:
                        self.ring(dy, k).start()
            self.part(1, 0)
            self.part(0, 0)

        def second(self):
            if self.y_first:
                for dx, ks in ((2, (0, 1)), (1, (2,)), (3, (3,))):
                    self.cross(dx).wait_recv()
                    self.add(dx, slice(None), 0, pc[self.base + dx])
                    for k in ks:
                        self.ring(0, k).start()
                return
            self.relay(1)
            self.relay(0)

        def third(self):
            if self.y_first:
                self.relay(0)
                return
            pq[self.q, 1, 0] = self.row_sum(1).astype(BF16)
            self.cross(0).start()

        def finish(self):
            total = self.row_sum(0)
            self.cross(0).wait_recv()
            total = total + pc[self.base].astype(F32)
            c = t * 2 + self.half
            base = tok[:, pl.ds(pl.multiple_of(c * C + self.sub * W, W), W)].astype(F32)
            aim = tgt[:, self.q * W : (self.q + 1) * W].astype(F32)
            r_all[self.q, t, :SEQ, :] = (base + total[:SEQ] - aim).astype(BF16)
            r_all[self.q, t, SEQ:, :] = total[SEQ:].astype(BF16)
            self.pass_on(*((1, 2, 0) if self.y_first else (0, 1, 2)))

        def sib_copy(self, j):
            rows = pl.ds(self.sub * W, W)
            return remote(
                wq.at[self.half * N_T + j, rows], sib.at[j, rows], sib_s.at[self.sub],
                sib_r.at[j, self.sub], dp=dev(0, 0, 1),
            )

        def use(self, *blocks):
            for j in blocks:
                rows = r_all[self.q, j]
                wq[self.half * N_T + j, self.cols] = mm_tn(rows, att[...]).astype(BF16)

                @pl.when(core != self.half)
                def _():
                    self.sib_copy(j).start()

                c = 2 * j + self.half
                res = rows[:SEQ]
                back = (rows[SEQ:].astype(F32) + res.astype(F32) * t_cols(c, self.sub)).astype(BF16)
                g_acc[...] += mm_nt(jnp.concatenate([res, back], axis=0), wo[c, :, self.cols])

        def z_copy(self, j, k):
            dx, upper, step = ((2, 0, 1), (2, 1, 3), (1, 1, 1), (3, 0, 3), (1, 0, 1), (3, 1, 3))[k]
            yd = j // 4
            rows = pl.ds(self.sub * W + upper * SEQ, SEQ)
            side = 0 if step == 1 else 1
            dst = zf.at[self.sub, yd, side] if k < 2 else zr.at[yd, side, rows]
            return remote(
                wq.at[self.half * N_T + j, rows], dst, z_s.at[self.sub],
                z_r.at[self.sub, yd, min(k, 2)], dp=dev(0, step, 0),
            )

        def combine(self, *blocks):
            @pl.when(core == self.half)
            def _():
                for j in blocks:
                    slot = self.half * N_T + j
                    self.sib_copy(j).wait_recv()
                    both = wq[slot, self.cols].astype(F32) + sib[j, self.cols].astype(F32)
                    wq[slot, self.cols] = both.astype(BF16)
                    rel = lax.rem(lax.rem(j, 4) + 4 - z, 4)
                    for want, ks in ((2, (0, 1)), (1, (2,)), (3, (3,))):

                        @pl.when(rel == want)
                        def _():
                            for k in ks:
                                self.z_copy(j, k).start()

        def z_relay(self, *blocks):
            @pl.when(core == self.half)
            def _():
                for j in blocks:
                    slot = self.half * N_T + j
                    rel = lax.rem(lax.rem(j, 4) + 4 - z, 4)
                    for want, side in ((1, 0), (3, 1)):

                        @pl.when(rel == want)
                        def _():
                            self.z_copy(j, side).wait_recv()
                            lo = self.sub * W + side * SEQ
                            old = wq[slot, lo : lo + SEQ].astype(F32)
                            new = old + zf[self.sub, j // 4, side].astype(F32)
                            wq[slot, lo : lo + SEQ] = new.astype(BF16)
                            self.z_copy(j, 4 + side).start()

        def near(self):
            self.came(1)
            self.pass_on(*((3, 5) if self.y_first else (3,)))
            self.came(2)
            self.pass_on(*((4, 6) if self.y_first else (4,)))
            if not self.y_first:
                self.came(0)
                self.pass_on(5, 6)

        def far(self):
            if self.y_first:
                self.came(3, 4)
                self.pass_on(7)
            else:
                self.came(5)
                self.pass_on(7)
                self.came(6)
                self.pass_on(8)

        def own(self):
            self.use(t)

        def own_sum(self):
            self.combine(t)

        def near_use(self):
            self.use(at(0, 3), at(0, 1))
            if self.y_first:
                self.came(0)
            self.use(at(1, 0))

        def next_use(self):
            self.combine(at(0, 3), at(0, 1), at(1, 0))
            if not self.y_first:
                self.came(3, 4)
            self.use(at(0, 2))

        def far_use(self):
            if self.y_first:
                self.came(5, 6)
            self.combine(at(0, 2))
            self.use(at(1, 3), at(1, 1))

        def last_use(self):
            self.came(*((7,) if self.y_first else (7, 8)))
            self.use(at(1, 2))
            self.combine(at(1, 3), at(1, 1))

        def relay_near(self):
            self.z_relay(t, at(0, 3), at(0, 1))

        def last(self):
            self.combine(at(1, 2))
            self.z_relay(at(1, 0), at(0, 2))

        def relay_far(self):
            self.z_relay(at(1, 3), at(1, 1))

        def relay_last(self):
            self.z_relay(at(1, 2))

        def wait_sends(self):
            sent = r_all.at[self.q, pl.ds(0, 7)]
            pltpu.make_async_copy(sent, sent, rs_s.at[self.q]).wait()
            pltpu.make_async_copy(sent, sent, ga_s.at[self.q]).wait()

            @pl.when(core != self.half)
            def _():
                to_core = wq.at[pl.ds(0, 4)]
                pltpu.make_async_copy(to_core, to_core, sib_s.at[self.sub]).wait()

            @pl.when(core == self.half)
            def _():
                along_z = wq.at[pl.ds(0, 3)]
                pltpu.make_async_copy(along_z, along_z, z_s.at[self.sub]).wait()

    q0 = Quarter(0, False, 0)
    q1 = Quarter(2, False, 1)
    q2 = Quarter(1, True, 2)
    q3 = Quarter(3, False, 6)
    other = lax.rem(y_hi + 1, 2)

    def z_sum(yd, sub):
        pltpu.make_async_copy(zr.at[yd, 0], zr.at[yd, 0], z_r.at[sub, yd, 2]).wait()
        rows = slice(sub * W, (sub + 1) * W)
        total = wq[core * N_T + yd * 4 + z, rows].astype(F32)
        return total + zr[yd, 0, rows].astype(F32) + zr[yd, 1, rows].astype(F32)

    def y_copy(sub):
        rows = pl.ds(sub * W, W)
        return remote(
            wq.at[core * N_T + other * 4 + z, rows], yr.at[rows], y_s.at[sub], y_r.at[sub],
            dp=dev(1, 0, 0),
        )

    def out_cross(sub):
        wq[core * N_T + other * 4 + z, sub * W : (sub + 1) * W] = z_sum(other, sub).astype(BF16)
        y_copy(sub).start()

    g_acc[...] = jnp.zeros_like(g_acc)
    tgt_copy.wait()
    q0.first()
    q2.first()
    q0.second()
    q1.first()
    q0.third()
    q1.second()
    q0.finish()
    q2.second()
    q3.first()
    q1.third()
    nrm_cross(1)
    q0.own()
    q0.near()
    q1.finish()
    q1.own()
    q2.third()
    q0.own_sum()
    q0.near_use()
    q3.second()
    nrm_cross(2)
    q1.own_sum()
    q0.next_use()
    q0.far()
    q0.far_use()
    q1.near()
    q1.near_use()
    q2.finish()
    q2.own()
    q0.relay_near()
    q3.third()
    q0.last_use()
    q2.own_sum()
    q0.last()
    q1.far()
    q3.finish()
    q1.next_use()
    q2.near()
    q3.own()
    q1.far_use()
    q2.near_use()
    q2.far()
    q3.near()
    q3.own_sum()
    q0.relay_far()
    q1.relay_near()
    q1.last_use()
    q0.relay_last()
    q2.next_use()
    q1.last()
    q2.far_use()
    q3.near_use()
    q3.far()
    q1.relay_far()
    nrm_cross(3)
    q2.relay_near()
    q2.last_use()
    q3.next_use()
    q2.last()
    q1.relay_last()
    q3.far_use()
    q3.last_use()

    key = kv[0]
    tkey = kv[1]
    val = kv[2]
    tval = kv[3]
    g1 = stack_heads(g_acc[:SEQ]).astype(BF16)
    g2 = stack_heads(g_acc[SEQ:]).astype(BF16)
    p = prob[...]
    tp = tprob[...]
    dpr = mm_nt(g1, val)
    tdpr = mm_nt(g2, val) + mm_nt(g1, tval)
    tval_grad = mm_tn(jnp.concatenate([tp, p], axis=0), jnp.concatenate([g1, g2], axis=0))
    gkv_g[d, :, HD:] = tval_grad.astype(BF16)
    dpr = dpr - jnp.sum(p * dpr, axis=1, keepdims=True)
    tdpr = tdpr - jnp.sum(tp * dpr + p * tdpr, axis=1, keepdims=True)
    ds = (p * dpr).astype(BF16)
    tds = (tp * dpr + p * tdpr).astype(BF16)
    both = jnp.concatenate([tds, ds], axis=0)
    trk_grad = mm_tn(both, rot_q[...]) * scale
    trk_grad = trk_grad * cos1 - swap_halves(trk_grad) * sin1
    gkv_g[d, :, :HD] = trk_grad.astype(BF16)
    trq_grad = (mm(tds, key) + mm(ds, tkey)) * scale
    trq_grad = trq_grad * cos4 - swap_halves(trq_grad) * sin4
    for h in range(HEADS):
        grd_g[d, :, h * HD : (h + 1) * HD] = trq_grad[h * SEQ : (h + 1) * SEQ].astype(BF16)

    def gs_copy(ry, rz):
        b = dev(ry, 4 - rz, 0)
        return remote(
            grd_g.at[b], grd_g.at[b], gs_s, gs_r.at[ry], dp=dev(0, 0, 1)
        )

    def gz_copy(ry, k, sender=True):
        step = (1, 3, 1, 3)[k]
        back = (0, 0, 1, 1)[k] if sender else (1, 1, 2, 2)[k]
        b = dev(ry, 4 - back if step == 1 else back, 0)
        h = SEQ // 2
        rows = (pl.ds(0, SEQ), pl.ds(0, SEQ), pl.ds(0, h), pl.ds(h, h))[k]
        ref = grd_g.at[b, rows]
        return remote(ref, ref, gz_s, gz_r.at[ry, k], dp=dev(0, step, 0))

    def gy_copy(b):
        return remote(grd_g.at[b], grd_g.at[b], gz_s, gy_r, dp=dev(1, 0, 0))

    def hs_copy(ry, rz):
        b = dev(ry, 4 - rz, 0)
        return remote(
            gkv_g.at[b], gkv_g.at[b], hs_s, hs_r.at[ry], dp=dev(0, 0, 1)
        )

    def hz_copy(k, sender=True):
        step = (1, 3, 1, 3)[k]
        back = (0, 0, 1, 1)[k] if sender else (1, 1, 2, 2)[k]
        b = dev(0, 4 - back if step == 1 else back, 0)
        h = SEQ // 2
        rows = (pl.ds(0, SEQ), pl.ds(0, SEQ), pl.ds(0, h), pl.ds(h, h))[k]
        ref = gkv_g.at[b, rows]
        return remote(ref, ref, hz_s, hz_r.at[k], dp=dev(0, step, 0))

    def hy_copy(rz, sender=True):
        b = dev(0 if sender else 1, 4 - rz, 0)
        return remote(gkv_g.at[b], gkv_g.at[b], hz_s, hy_r.at[rz], dp=dev(1, 0, 0))

    def pass_on(ry):
        for k, rz in ((0, 1), (1, 3)):
            gz_copy(ry, k, False).wait_recv()
            gz_copy(ry, k + 2).start()
            gs_copy(ry, rz).start()

    gy_copy(d).start()
    hy_copy(0).start()
    hz_copy(0).start()
    hz_copy(1).start()
    gz_copy(0, 0).start()
    gz_copy(0, 1).start()
    hs_copy(0, 0).start()
    gs_copy(0, 0).start()
    q3.relay_near()
    out_cross(0)
    q3.last()
    q2.relay_far()
    q2.relay_last()
    for k, rz in ((0, 1), (1, 3)):
        hz_copy(k, False).wait_recv()
        hz_copy(k + 2).start()
        hy_copy(rz).start()
        hs_copy(0, rz).start()
    gy_copy(dev(1, 0, 0)).wait_recv()
    gz_copy(1, 0).start()
    gz_copy(1, 1).start()
    gs_copy(1, 0).start()
    q3.relay_far()
    pass_on(0)
    q3.relay_last()
    hz_copy(2, False).wait_recv()
    hz_copy(3, False).wait_recv()
    hy_copy(2).start()
    hs_copy(0, 2).start()
    hy_copy(0, False).wait_recv()
    hs_copy(1, 0).start()
    out_cross(1)
    pass_on(1)
    for rz in (1, 3):
        hy_copy(rz, False).wait_recv()
        hs_copy(1, rz).start()

    def product(first):
        rows = pl.ds(first * N_T, N_T)
        lhs = nrm_g[rows].reshape(N_T * SEQ, C)
        of_query = mm_tn(lhs, grd_g[rows].reshape(N_T * SEQ, QW))
        return of_query, mm_tn(lhs, gkv_g[rows].reshape(N_T * SEQ, 2 * HD))

    def arrived(ry):
        for ref, blocks, sem in ((nrm_g, N_T - 1 + ry, nrm_r), (grd_g, 4, gs_r), (gkv_g, 4, hs_r)):
            came = ref.at[pl.ds(0, blocks)]
            pltpu.make_async_copy(came, came, sem.at[ry]).wait()

    gz_copy(0, 2, False).wait_recv()
    gz_copy(0, 3, False).wait_recv()
    gs_copy(0, 2).start()
    for sub in range(2):
        ho[sub * W : (sub + 1) * W, :] = z_sum(y_hi, sub)
    arrived(0)
    of_query, of_kv = product(y_hi)
    hq[...] = of_query
    hk[...] = of_kv[:, :HD]
    hv[...] = of_kv[:, HD:]
    gz_copy(1, 2, False).wait_recv()
    gz_copy(1, 3, False).wait_recv()
    gs_copy(1, 2).start()
    hy_copy(2, False).wait_recv()
    hs_copy(1, 2).start()
    for sub in range(2):
        y_copy(sub).wait_recv()

    def stores(i):
        src, dst = ((hq, hq_hbm), (hk, hk_hbm), (hv, hv_hbm), (ho, ho_hbm))[i]
        return [pltpu.make_async_copy(src, dst, out_sem.at[i])]

    ho[...] += yr[...].astype(F32)
    for cp in stores(3):
        cp.start()
    arrived(1)
    of_query, of_kv = product(other)
    hq[...] += of_query
    hk[...] += of_kv[:, :HD]
    hv[...] += of_kv[:, HD:]
    for i in (0, 1, 2):
        for cp in stores(i):
            cp.start()

    for quarter in (q0, q1, q2, q3):
        quarter.wait_sends()
    for sub in range(2):
        y_copy(sub).wait_send()
    for ref, blocks, sem in (
        (nrm_g, N_DP - 1, nrm_s), (grd_g, 7, gz_s), (grd_g, 8, gs_s), (gkv_g, 7, hz_s), (gkv_g, 8, hs_s),
    ):
        sent = ref.at[pl.ds(0, blocks)]
        pltpu.make_async_copy(sent, sent, sem).wait()
    for i in range(4):
        for cp in stores(i):
            cp.wait()


def hand_over(a, b, c, e, a_out, b_out, c_out, e_out, a_buf, b_buf, c_buf, e_buf, sem):
    arrays = ((a, a_buf, a_out), (e, e_buf, e_out), (b, b_buf, b_out), (c, c_buf, c_out))
    loads, stores = [], []
    for i, (src, buf, dst) in enumerate(arrays):
        for part in range(2):
            rows = pl.ds(part * (C // 2), C // 2)
            loads.append(
                pltpu.make_async_copy(src.at[rows], buf.at[rows], sem.at[0, 2 * i + part])
            )
            stores.append(
                pltpu.make_async_copy(buf.at[rows], dst.at[rows], sem.at[1, 2 * i + part])
            )
    for load in loads:
        load.start()
    for load, store in zip(loads, stores):
        load.wait()
        store.start()
    for store in stores:
        store.wait()


def tables():
    frequency = np.exp(
        np.float32(-math.log(10000.0)) * np.arange(HD // 2, dtype=np.float32) * np.float32(2.0)
        / np.float32(HD)
    ).astype(np.float32)
    angles = np.arange(SEQ, dtype=np.float32)[:, None] * frequency[None, :]
    cosine = np.cos(angles).astype(np.float32)
    sine = np.sin(angles).astype(np.float32)
    return np.concatenate([cosine, cosine], 1), np.concatenate([-sine, sine], 1)


def local(
    tokens, target, norm_gain, w_query, w_key, w_value, w_out, t_query, t_key, t_value, t_out
):
    cos_t, sin_t = tables()
    any_spec = pl.BlockSpec(memory_space=pl.ANY)
    vmem = pl.BlockSpec(memory_space=pltpu.VMEM)
    dma = pltpu.SemaphoreType.DMA
    block = (2 * SEQ, C // 2)
    scratch = [
        pltpu.VMEM((C, QW), F32),
        pltpu.VMEM((C, HD), F32),
        pltpu.VMEM((C, HD), F32),
        pltpu.VMEM((C, QW), F32),
        pltpu.VMEM((SEQ, D), BF16),
        pltpu.VMEM((SEQ, 2 * C), BF16),
        pltpu.VMEM((N_DP, C, QW), BF16),
        pltpu.VMEM((N_DP, C, HD), BF16),
        pltpu.VMEM((N_DP, C, HD), BF16),
        pltpu.VMEM((N_DP, QW, C), BF16),
        pltpu.VMEM((N_DP, SEQ, C), BF16),
        pltpu.VMEM((N_DP, SEQ, C), BF16),
        pltpu.VMEM((2 * SEQ, QW), BF16),
        pltpu.VMEM((N_T, C, QW), BF16),
        pltpu.VMEM((2, 2, 2, SEQ, QW), BF16),
        pltpu.VMEM((2, 2, C, QW), BF16),
        pltpu.VMEM((C, QW), BF16),
        pltpu.VMEM((N_DP, SEQ, QW), BF16),
        pltpu.VMEM((N_DP, SEQ, 2 * HD), BF16),
        pltpu.VMEM((4, 2, 4) + block, BF16),
        pltpu.VMEM((4, 2, 2, SEQ, C // 2), BF16),
        pltpu.VMEM((4, 2, 2) + block, BF16),
        pltpu.VMEM((7,) + block, BF16),
        pltpu.VMEM((4, N_T) + block, BF16),
        pltpu.VMEM((2 * SEQ, QW), F32),
        pltpu.VMEM((SEQ, QW + 2 * HD), F32),
        pltpu.VMEM((HEADS * SEQ, SEQ), F32),
        pltpu.VMEM((HEADS * SEQ, SEQ), F32),
        pltpu.VMEM((2 * HEADS * SEQ, HD), BF16),
        pltpu.VMEM((4, SEQ, HD), BF16),
        dma((2,)), dma((4,)), dma((3, 4)), dma,
        dma, dma((2,)), dma((2,)), dma((N_T, 2)), dma((2,)), dma((2, 2, 3)), dma((2,)), dma((2,)),
        dma, dma((2, 4)), dma, dma, dma((2,)), dma, dma((4,)), dma((4,)), dma, dma((2,)),
        dma((4,)), dma((4, 2, 3)), dma((7,)), dma((4,)), dma((4, 9)),
    ]
    shapes = tuple(jax.ShapeDtypeStruct((C, n), F32) for n in (QW, HD, HD, QW))
    results = pl.pallas_call(
        kernel,
        out_shape=shapes,
        in_specs=[
            any_spec, any_spec, vmem, any_spec, any_spec, any_spec, any_spec,
            vmem, vmem, vmem, vmem, vmem, vmem,
        ],
        out_specs=(any_spec,) * 4,
        scratch_shapes=scratch,
        compiler_params=pltpu.CompilerParams(
            collective_id=0, has_side_effects=True, vmem_limit_bytes=62 * 1024 * 1024
        ),
        cost_estimate=pl.CostEstimate(
            flops=10_000_000_000, bytes_accessed=26_000_000, transcendentals=65536
        ),
        name="hvp",
    )(
        tokens, target, norm_gain.reshape(1, D), w_query.reshape(N_DP, C, QW),
        w_key.reshape(N_DP, C, HD), w_value.reshape(N_DP, C, HD), w_out,
        t_query.reshape(1, QW), t_key.reshape(1, HD), t_value.reshape(1, HD),
        t_out.reshape(1, D), jnp.asarray(cos_t), jnp.asarray(sin_t),
    )
    return pl.pallas_call(
        hand_over,
        out_shape=shapes,
        in_specs=[any_spec] * 4,
        out_specs=(any_spec,) * 4,
        scratch_shapes=[pltpu.VMEM((C, n), F32) for n in (QW, HD, HD, QW)] + [dma((2, 8))],
        compiler_params=pltpu.CompilerParams(vmem_limit_bytes=62 * 1024 * 1024),
        name="results",
    )(*results)


def solution(mesh):
    return jax.shard_map(
        local,
        mesh=mesh,
        in_specs=(
            P("dp", None),
            P("dp", None),
            P(),
            P(None, "tensor"),
            P(None, "tensor"),
            P(None, "tensor"),
            P("tensor", None),
            P("tensor"),
            P("tensor"),
            P("tensor"),
            P(),
        ),
        out_specs=(P("dp", "tensor"), P("dp", "tensor"), P("dp", "tensor"), P("dp", "tensor")),
        check_vma=False,
    )
```
